32 devices in a mesh: ctx: 2 (over y), tp: 16 (over z, x, core).
Axes of the slice: x: 2, y: 2, z: 4, core: 2. Of those that a mesh axis runs over, the one named last changes fastest.
Arguments:
- hidden: bfloat16 [512, 2048], P(('ctx', 'tp')), may hold values from -6 to 6
- w_in: bfloat16 [2048, 2048], P(None, 'tp'), may hold values from -0.125 to 0.125
- w_bc: bfloat16 [2048, 32], replicated, may hold values from -0.125 to 0.125
- w_dt: bfloat16 [16, 2048], P('tp'), may hold values from -0.125 to 0.125
- dt_bias: float32 [16], P('tp'), may hold values from -5 to -3
- a_log: float32 [16], P('tp'), may hold values from -4.6 to 0
- d_skip: float32 [16], P('tp'), may hold values from 0.5 to 1.5
- conv_w: float32 [4, 1024], P(None, 'tp'), may hold values from -3 to 3
- w_out: bfloat16 [1024, 2048], P('tp'), may hold values from -0.1875 to 0.1875
- d_out: bfloat16 [512, 2048], P(('ctx', 'tp')), may hold values from -6 to 6
Outputs:
- d_hidden: bfloat16 [512, 2048], P(('ctx', 'tp'))
- d_w_in: float32 [2048, 2048], P(None, 'tp')
- d_w_out: float32 [1024, 2048], P('tp')
- d_w_bc: float32 [2048, 32], replicated
The draws below stay inside these ranges and needn't reach their ends.
All inputs are finite; a program needn't handle non-finite values.
Results may differ from the reference program's by a relative error of at most 0.017.
Values may be sent and summed in bfloat16 or wider, within the bound.
No kernel may reach another device: no remote copies, remote signals or barrier semaphores. Data moves between devices by JAX's collectives and lax.ppermute only.
A program may use at most 64 MiB of HBM per device.

```python
import math
import jax
import jax.numpy as jnp
from jax import lax

D = 2048
HEAD_DIM = 64
STATE = 16
CONV = 4
SEQ_DEV = 256
HEADS = 16
INNER = 1024
LENGTH = 512


def shard_levels(stream_key, dims, shards, low, high):
    level, own = 1.0, jax.random.fold_in(stream_key, 6)
    for axis_at, shards_of in shards:
        heights = jnp.exp(jax.random.uniform(jax.random.fold_in(own, axis_at), (shards_of,), jnp.float32, low / len(shards), high / len(shards)))
        level = level * jnp.repeat(heights, dims[axis_at] // shards_of).reshape([-1 if axis == axis_at else 1 for axis in range(len(dims))])
    return level


def bell_draw(stream_key, dims, scale, reach, split=(), held_as=jnp.bfloat16):
    result = scale * jax.random.normal(stream_key, dims, jnp.float32)
    if split:
        result = result * shard_levels(stream_key, dims, split, -0.22, 0.18)
    return jnp.clip(result, -reach, reach).astype(held_as)


def setup_inputs(seed: int = 0) -> dict:
    seeds = jax.random.split(jax.random.key(seed), 11)
    hidden = bell_draw(seeds[0], (LENGTH, D), 1.0, 6.0, ((0, 32),))
    w_in = bell_draw(seeds[1], (D, 2 * INNER), D ** -0.5, 0.125, ((1, 16),))
    w_bc = bell_draw(seeds[2], (D, 2 * STATE), D ** -0.5, 0.125)
    w_dt = bell_draw(seeds[3], (HEADS, D), D ** -0.5, 0.125, ((0, 16),))
    dt_bias = jnp.clip(-5.0 + 2.0 * jax.random.uniform(seeds[4], (HEADS,), jnp.float32) ** shard_levels(seeds[4], (HEADS,), ((0, 16),), -0.2, 0.2), -5.0, -3.0)
    a_log = jnp.clip(-4.6 + 4.6 * jax.random.uniform(seeds[5], (HEADS,), jnp.float32) ** shard_levels(seeds[5], (HEADS,), ((0, 16),), -0.2, 0.2), -4.6, 0.0)
    d_skip = jnp.clip(0.5 + 1.0 * jax.random.uniform(seeds[6], (HEADS,), jnp.float32) ** shard_levels(seeds[6], (HEADS,), ((0, 16),), -0.2, 0.2), 0.5, 1.5)
    conv_w = bell_draw(seeds[7], (CONV, INNER), CONV ** -0.5, 3.0, ((1, 16),), jnp.float32)
    w_out = bell_draw(seeds[8], (INNER, D), INNER ** -0.5, 0.1875, ((0, 16),))
    d_out = bell_draw(seeds[9], (LENGTH, D), 1.0, 6.0, ((0, 32),))
    return dict(hidden=hidden, w_in=w_in, w_bc=w_bc, w_dt=w_dt, dt_bias=dt_bias, a_log=a_log, d_skip=d_skip, conv_w=conv_w, w_out=w_out, d_out=d_out)


precise = lax.Precision.HIGHEST

def block_ssd(conv_out, steps_dt, b_rows, c_rows, decay_rate, state_in):
    positions = conv_out.shape[0]
    log_keep = jnp.cumsum(steps_dt * decay_rate)
    causal = lax.broadcasted_iota(jnp.int32, (positions, positions), 0) >= lax.broadcasted_iota(jnp.int32, (positions, positions), 1)
    decays = jnp.exp(jnp.where(causal, log_keep[:, None] - log_keep[None, :], -jnp.inf))
    scores = jnp.einsum('in,jn->ij', c_rows, b_rows, precision=precise) * decays
    weighted = steps_dt[:, None] * conv_out
    outputs = jnp.einsum('ij,jp->ip', scores, weighted, precision=precise)
    outputs = outputs + jnp.exp(log_keep)[:, None] * jnp.einsum('in,pn->ip', c_rows, state_in, precision=precise)
    remains = jnp.exp(log_keep[-1] - log_keep)
    state_out = jnp.exp(log_keep[-1]) * state_in + jnp.einsum('j,jp,jn->pn', remains, weighted, b_rows, precision=precise)
    return (outputs, state_out)

def conv_silu(x_raw, conv_w):
    padded = jnp.pad(x_raw, ((CONV - 1, 0), (0, 0)))
    summed = conv_w[0] * padded[0:LENGTH]
    for shift_k in range(1, CONV):
        summed = summed + conv_w[shift_k] * padded[shift_k:shift_k + LENGTH]
    return jax.nn.silu(summed)

def head_scan(conv_out, steps_dt, b_rows, c_rows, decay_rate):
    blocks = LENGTH // SEQ_DEV

    def advance(state_in, elements):
        outputs, state_out = block_ssd(elements[0], elements[1], elements[2], elements[3], decay_rate, state_in)
        return (state_out, outputs)
    starting = jnp.zeros((HEAD_DIM, STATE), jnp.float32)
    elements = (conv_out.reshape(blocks, SEQ_DEV, HEAD_DIM), steps_dt.reshape(blocks, SEQ_DEV), b_rows.reshape(blocks, SEQ_DEV, STATE), c_rows.reshape(blocks, SEQ_DEV, STATE))
    _, outputs = lax.scan(jax.checkpoint(advance), starting, elements)
    return outputs.reshape(LENGTH, HEAD_DIM)

def strand_gate(x_raw, gate_in, b_c, dt_raw, dt_bias, a_log, d_skip, conv_w):
    conv_out = conv_silu(x_raw, conv_w)
    steps_dt = jax.nn.softplus(dt_raw + dt_bias)
    per_head = conv_out.reshape(LENGTH, HEADS, HEAD_DIM)
    outputs = jax.vmap(head_scan, in_axes=(1, 1, None, None, 0), out_axes=1)(per_head, steps_dt, b_c[:, :STATE], b_c[:, STATE:], -jnp.exp(a_log))
    outputs = outputs.reshape(LENGTH, INNER) + jnp.repeat(d_skip, HEAD_DIM) * conv_out
    return outputs * jax.nn.silu(gate_in)

def reference(hidden, w_in, w_bc, w_dt, dt_bias, a_log, d_skip, conv_w, w_out, d_out):
    d_hidden = jnp.zeros((LENGTH, D), jnp.float32)
    d_w_in = jnp.zeros((D, 2 * INNER), jnp.float32)
    d_w_bc = jnp.zeros((D, 2 * STATE), jnp.float32)
    d_w_out = jnp.zeros((INNER, D), jnp.float32)
    strands = ((hidden, d_out, False), (hidden[::-1, ::-1], d_out[::-1, ::-1], True))
    for strand_in, cotangent, mirrored in strands:
        projected = jnp.dot(strand_in, w_in, preferred_element_type=jnp.float32).astype(jnp.bfloat16)
        per_head = projected.reshape(LENGTH, HEADS, 2, HEAD_DIM).astype(jnp.float32)
        x_raw = per_head[:, :, 0].reshape(LENGTH, INNER)
        gate_in = per_head[:, :, 1].reshape(LENGTH, INNER)
        b_c = jnp.dot(strand_in, w_bc, preferred_element_type=jnp.float32)
        dt_raw = jnp.dot(strand_in, w_dt.T, preferred_element_type=jnp.float32)

        def gate_only(x_part, z_part, bc_part, dt_part):
            return strand_gate(x_part, z_part, bc_part, dt_part, dt_bias, a_log, d_skip, conv_w)
        gated, pullback = jax.vjp(gate_only, x_raw, gate_in, b_c, dt_raw)
        gated_low = gated.astype(jnp.bfloat16)
        grad_gate = jnp.dot(cotangent, w_out.T, preferred_element_type=jnp.float32)
        grad_x, grad_z, grad_b, grad_t = pullback(grad_gate)
        grad_proj = jnp.stack([grad_x.reshape(LENGTH, HEADS, HEAD_DIM), grad_z.reshape(LENGTH, HEADS, HEAD_DIM)], axis=2).reshape(LENGTH, 2 * INNER).astype(jnp.bfloat16)
        grad_b_low = grad_b.astype(jnp.bfloat16)
        grad_t_low = grad_t.astype(jnp.bfloat16)
        grad_in = jnp.dot(grad_proj, w_in.T, preferred_element_type=jnp.float32)
        grad_in = grad_in + jnp.dot(grad_b_low, w_bc.T, preferred_element_type=jnp.float32)
        grad_in = grad_in + jnp.dot(grad_t_low, w_dt, preferred_element_type=jnp.float32)
        if mirrored:
            grad_in = grad_in[::-1, ::-1]
        d_hidden = d_hidden + grad_in
        d_w_in = d_w_in + jnp.dot(strand_in.T, grad_proj, preferred_element_type=jnp.float32)
        d_w_bc = d_w_bc + jnp.dot(strand_in.T, grad_b_low, preferred_element_type=jnp.float32)
        d_w_out = d_w_out + jnp.dot(gated_low.T, cotangent, preferred_element_type=jnp.float32)
    scaling = 1.0 / math.sqrt(LENGTH)
    return (d_hidden.astype(jnp.bfloat16), d_w_in * scaling, d_w_out * scaling, d_w_bc * scaling)
```

```python
import functools
import math

import jax
import jax.numpy as jnp
from jax import lax
from jax.experimental import pallas as pl
from jax.experimental.pallas import tpu as pltpu
from jax.sharding import PartitionSpec as P

STATE = 16
CONV = 4
LANES = 128
BLOCK = 256
TILE_ROWS = 16
VMEM_LIMIT = 60 * 1024 * 1024
f32 = jnp.float32
bf16 = jnp.bfloat16


def dot(a, b):
    return jnp.dot(a, b, preferred_element_type=f32)


def dot_nt(a, b):
    return lax.dot_general(a, b, (((1,), (1,)), ((), ())), preferred_element_type=f32)


def dot_tn(a, b):
    return lax.dot_general(a, b, (((0,), (0,)), ((), ())), preferred_element_type=f32)


def iota(shape, dim):
    return lax.broadcasted_iota(jnp.int32, shape, dim)


def mirror(size):
    return jnp.where(iota((size, size), 0) + iota((size, size), 1) == size - 1, 1.0, 0.0).astype(
        bf16
    )


def split(value, terms):
    parts = []
    for _ in range(terms):
        part = value.astype(bf16)
        parts.append(part)
        value = value - part.astype(f32)
    return parts


def flip_rows(value, flip):
    count = value.shape[0] // BLOCK
    return jnp.concatenate(
        [dot(flip, value[(count - 1 - i) * BLOCK : (count - i) * BLOCK]) for i in range(count)],
        axis=0,
    )


def assemble(ids_ref, pieces, h_ref, d_ref, layout):
    tp_size, own_rows, coords = layout
    nz = tp_size // 4
    z, x, core, ctx = (ids_ref[i] for i in range(4))
    ctx_size = max(c[0] for c in coords) + 1
    for piece, (dc, dx, dcore) in zip(pieces, coords):
        from_ctx = lax.rem(ctx + dc, ctx_size)
        for j in range(nz):
            owner = ((z ^ j) * 2 + (x ^ dx)) * 2 + (core ^ dcore)
            at = pl.multiple_of((from_ctx * tp_size + owner) * own_rows, own_rows)
            base = 2 * j * own_rows
            if h_ref is not None:
                h_ref[pl.ds(at, own_rows), :] = piece[base : base + own_rows, :]
            if d_ref is not None:
                d_ref[pl.ds(at, own_rows), :] = piece[base + own_rows : base + 2 * own_rows, :]


def prep_kernel(wcat_ref, wrev_ref):
    flip = mirror(BLOCK)
    count = wcat_ref.shape[0] // BLOCK
    for i in range(count):
        wrev_ref[i * BLOCK : (i + 1) * BLOCK, :] = dot(
            flip, wcat_ref[(count - 1 - i) * BLOCK : (count - i) * BLOCK, :]
        ).astype(bf16)


def own_source(shape, dim, ids_ref, tp_size, own_rows):
    z, x, core, ctx = (ids_ref[i] for i in range(4))
    nz = tp_size // 4
    row = iota(shape, dim)
    block = row // own_rows
    j = block % nz
    dx = 1 - (block // nz) % 2
    dcore = 1 - block // (2 * nz)
    owner = ((z ^ j) * 2 + (x ^ dx)) * 2 + (core ^ dcore)
    return (ctx * tp_size + owner) * own_rows + row % own_rows


def core_kernel(n_pieces, layout, *refs):
    ids_ref, par_ref = refs[:2]
    pieces = refs[2 : 2 + n_pieces]
    wcat_ref, wrev_ref, wout_ref, cw_ref = refs[2 + n_pieces : 6 + n_pieces]
    send_ref, keep_ref, gcat_ref, gated_ref = refs[6 + n_pieces : 10 + n_pieces]
    tp_size, own_rows, coords = layout
    if coords is None:
        h_ref, d_ref = pieces
    else:
        h_ref, d_ref = refs[10 + n_pieces :]
        assemble(ids_ref, pieces, h_ref, d_ref, layout)
    length, width = h_ref.shape
    chunks = length // BLOCK
    columns = width // BLOCK
    flip = mirror(BLOCK)
    bias, rate, skip = par_ref[0], par_ref[1], par_ref[2]
    lane = iota((1, LANES), 1)
    low = lane < LANES // 2
    tri = jnp.where(iota((BLOCK, BLOCK), 0) >= iota((BLOCK, BLOCK), 1), 1.0, 0.0).astype(bf16)
    causal = iota((BLOCK, BLOCK), 0) >= iota((BLOCK, BLOCK), 1)
    row_at = iota((length, LANES), 0)

    proj_f = dot(h_ref[...], wcat_ref[...])
    grad_f = dot_nt(d_ref[...], wout_ref[...])
    proj_r = jnp.zeros_like(proj_f)
    grad_r = jnp.zeros_like(grad_f)
    for i in range(columns):
        cols = slice(i * BLOCK, (i + 1) * BLOCK)
        back = slice((columns - 1 - i) * BLOCK, (columns - i) * BLOCK)
        proj_r += dot(h_ref[:, cols], wrev_ref[cols, :])
        turned = dot(wout_ref[:, back], flip).astype(bf16)
        grad_r += dot_nt(d_ref[:, cols], turned)
    xz_r = flip_rows(proj_r[:, :LANES].astype(bf16), flip)
    rest_r = sum(flip_rows(part, flip) for part in split(proj_r[:, LANES:], 3))
    grad_r = sum(flip_rows(part, flip) for part in split(grad_r, 2))
    strands = (
        (proj_f[:, :LANES].astype(bf16).astype(f32), proj_f[:, LANES:], grad_f),
        (xz_r, rest_r, grad_r),
    )
    small = []
    for which, (xz, rest, grad_g) in enumerate(strands):
        pre = cw_ref[CONV - 1 : CONV, :] * xz
        for shift in range(1, CONV):
            moved = jnp.where(row_at >= shift, pltpu.roll(xz, shift, 0), 0.0)
            pre += cw_ref[CONV - 1 - shift : CONV - shift, :] * moved
        sig = jax.nn.sigmoid(pre)
        u = pre * sig
        slope = sig * (1.0 + pre * (1.0 - sig))
        u_other = pltpu.roll(u, LANES // 2, 1)
        raw = jnp.broadcast_to(rest[:, 2 * STATE : 2 * STATE + 1], (length, LANES)) + bias
        dt = jnp.maximum(raw, 0.0) + jnp.log1p(jnp.exp(-jnp.abs(raw)))
        dt_slope = jax.nn.sigmoid(raw)
        b_all = jnp.where(lane < STATE, rest, 0.0)
        c_all = jnp.where(lane < STATE, pltpu.roll(rest, LANES - STATE, 1), 0.0)
        w_all = dt * u
        g_y = jnp.where(low, grad_g * u_other, 0.0)
        saved = []
        state = jnp.zeros((LANES, LANES), f32)
        outs = []
        for c in range(chunks):
            rows = slice(c * BLOCK, (c + 1) * BLOCK)
            log_keep = sum(dot(tri, part) for part in split(dt[rows] * rate, 3))
            across = jnp.transpose(log_keep)[0:1, :]
            gap = jnp.concatenate([log_keep] * (BLOCK // LANES), axis=1) - across
            decay = jnp.exp(jnp.where(causal, gap, -jnp.inf))
            b_rows, c_rows = b_all[rows], c_all[rows]
            b_low, c_low = b_rows.astype(bf16), c_rows.astype(bf16)
            mixed = (dot_nt(c_low, b_low) * decay).astype(bf16)
            w_low = w_all[rows].astype(bf16)
            last = log_keep[BLOCK - 1 : BLOCK, :]
            enter = jnp.exp(log_keep)
            leave = jnp.exp(last - log_keep)
            total = jnp.exp(last)
            b_left = (leave * b_rows).astype(bf16)
            out = dot(mixed, w_low) + enter * dot(c_low, state.astype(bf16))
            saved.append((decay, mixed, b_low, c_low, w_low, b_left, enter, leave, total, state))
            state = total * state + dot_tn(b_left, w_low)
            saved[-1] += (state,)
            outs.append(out)
        y = jnp.concatenate(outs, axis=0) + skip * u
        gated = jnp.where(low, y * u_other, 0.0).astype(bf16)
        g_gate = jnp.where(low, grad_g * y, 0.0)
        d_state = jnp.zeros((LANES, LANES), f32)
        d_w, g_b, g_c, g_a = [None] * chunks, [None] * chunks, [None] * chunks, [None] * chunks
        for c in reversed(range(chunks)):
            rows = slice(c * BLOCK, (c + 1) * BLOCK)
            decay, mixed, b_low, c_low, w_low, b_left, enter, leave, total, state, after = saved[c]
            gy = g_y[rows]
            gy_low = gy.astype(bf16)
            ds_low = d_state.astype(bf16)
            dw = dot_tn(mixed, gy_low) + dot(b_left, ds_low)
            d_scores = (dot_nt(gy_low, w_low) * decay).astype(bf16)
            g_c[c] = dot(d_scores, b_low) + enter * dot_nt(gy_low, state.astype(bf16))
            g_b[c] = dot_tn(d_scores, c_low) + leave * dot_nt(w_low, ds_low)
            d_log = jnp.sum(
                jnp.where(low, gy * outs[c] - w_all[rows] * dw, 0.0), axis=1, keepdims=True
            )
            at_end = jnp.sum(jnp.where(low, after * d_state, 0.0))
            d_log = jnp.broadcast_to(d_log, (BLOCK, LANES))
            d_sum = sum(dot_tn(tri, part) for part in split(d_log, 2)) + at_end
            d_dt = rate * d_sum + jnp.sum(
                jnp.where(low, u[rows] * dw, 0.0), axis=1, keepdims=True
            )
            g_a[c] = d_dt
            d_w[c] = dw
            carried = (enter * c_all[rows]).astype(bf16)
            d_state = total * d_state + dot_tn(carried, gy_low)
        d_w = jnp.concatenate(d_w, axis=0)
        g_b = jnp.concatenate(g_b, axis=0)
        g_c = jnp.concatenate(g_c, axis=0)
        g_raw = jnp.concatenate(g_a, axis=0) * dt_slope
        d_u = jnp.where(low, skip * g_y + dt * d_w, pltpu.roll(g_gate, LANES // 2, 1))
        d_pre = d_u * slope
        g_xz = cw_ref[CONV - 1 : CONV, :] * d_pre
        for shift in range(1, CONV):
            moved = jnp.where(
                row_at < length - shift, pltpu.roll(d_pre, length - shift, 0), 0.0
            )
            g_xz += cw_ref[CONV - 1 - shift : CONV - shift, :] * moved
        shared = jnp.where(lane < STATE, g_b, 0.0) + jnp.where(
            (lane >= STATE) & (lane < 2 * STATE), pltpu.roll(g_c, STATE, 1), 0.0
        )
        g_rest = shared + jnp.where(lane == 2 * STATE, g_raw, 0.0)
        g_cat = jnp.concatenate([g_xz, g_rest], axis=1).astype(bf16)
        small.append(shared)
        if which == 0:
            gcat_ref[:, 0 : 2 * LANES] = g_cat
            gated_ref[:, 0:LANES] = gated
        else:
            gcat_ref[:, 2 * LANES :] = flip_rows(g_cat, flip).astype(bf16)
            gated_ref[:, LANES:] = flip_rows(gated, flip).astype(bf16)

    pair = small[0] + pltpu.roll(small[1], 2 * STATE, 1)
    shared_t = jnp.transpose(pair)[: 4 * STATE].astype(bf16)
    groups = width // length
    step = 4 * STATE // groups
    for i in range(groups):
        part = shared_t[i * step : (i + 1) * step, :]
        send_ref[0:step, i * length : (i + 1) * length] = part
        keep_ref[0:step, i * length : (i + 1) * length] = part.astype(f32)
    own = tp_size * own_rows
    source = own_source((own, length), 0, ids_ref, tp_size, own_rows)
    pick = jnp.where(source == iota((own, length), 1), 1.0, 0.0).astype(bf16)
    picked = dot(pick, gcat_ref[...]).astype(bf16)
    half = own // 2
    for i in range(columns):
        cols = slice(i * BLOCK, (i + 1) * BLOCK)
        part = dot_nt(picked[:, : 2 * LANES], wcat_ref[cols, :]) + dot_nt(
            picked[:, 2 * LANES :], wrev_ref[cols, :]
        )
        send_ref[step:, cols] = part[:half].astype(bf16)
        keep_ref[step:, cols] = part[half:]


def weight_kernel(n_pieces, layout, scaling, *refs):
    ids_ref = refs[0]
    pieces = refs[1 : 1 + n_pieces]
    gcat_ref, gated_ref, dwin_ref, dwout_ref = refs[1 + n_pieces : 5 + n_pieces]
    if layout[2] is None:
        h_ref, d_ref = pieces
    else:
        h_ref, d_ref = refs[5 + n_pieces :]
        assemble(ids_ref, pieces, h_ref, d_ref, layout)
    flip = mirror(BLOCK)
    columns = h_ref.shape[1] // BLOCK
    head = dwout_ref.shape[0]
    g_f = gcat_ref[:, 0:LANES]
    g_r = gcat_ref[:, 2 * LANES : 3 * LANES]
    y_f = gated_ref[:, 0:LANES]
    y_r = gated_ref[:, LANES:]
    for i in range(columns):
        cols = slice(i * BLOCK, (i + 1) * BLOCK)
        back = slice((columns - 1 - i) * BLOCK, (columns - i) * BLOCK)
        turned = dot(h_ref[:, back], flip).astype(bf16)
        grad = dot_tn(g_f, h_ref[:, cols]) + dot_tn(g_r, turned)
        dwin_ref[cols, :] = jnp.transpose(grad * scaling)
        turned = dot(d_ref[:, back], flip).astype(bf16)
        grad = dot_tn(y_f, d_ref[:, cols]) + dot_tn(y_r, turned)
        dwout_ref[:, cols] = grad[:head] * scaling


def last_kernel(n_pieces, layout, scaling, *refs):
    ids_ref, shared_ref = refs[:2]
    pieces = refs[2 : 2 + n_pieces]
    dwbc_ref = refs[2 + n_pieces]
    if layout[2] is None:
        h_ref = pieces[0]
    else:
        h_ref = refs[3 + n_pieces]
        assemble(ids_ref, pieces, h_ref, None, layout)
    flip = mirror(BLOCK)
    length, width = h_ref.shape
    columns = width // BLOCK
    groups = width // length
    shared = jnp.concatenate(
        [shared_ref[:, i * length : (i + 1) * length] for i in range(groups)], axis=0
    ).astype(bf16)
    fwd = shared[: 2 * STATE]
    rev = shared[2 * STATE :]
    count = length // BLOCK
    rev = jnp.concatenate(
        [
            dot(rev[:, (count - 1 - i) * BLOCK : (count - i) * BLOCK], flip).astype(bf16)
            for i in range(count)
        ],
        axis=1,
    )
    pad = jnp.zeros((LANES - 2 * STATE, length), bf16)
    fwd = jnp.concatenate([fwd, pad], axis=0)
    rev = jnp.concatenate([rev, pad], axis=0)
    for i in range(columns):
        cols = slice(i * BLOCK, (i + 1) * BLOCK)
        back = slice((columns - 1 - i) * BLOCK, (columns - i) * BLOCK)
        turned = dot(h_ref[:, back], flip).astype(bf16)
        grad = (dot(fwd, h_ref[:, cols]) + dot(rev, turned)) * scaling
        dwbc_ref[cols, :] = jnp.transpose(grad)[:, : 2 * STATE]


def spec(memory=pltpu.VMEM):
    return pl.BlockSpec(memory_space=memory)


def call(kernel, inputs, n_smem, outs, scratch, flops, moved):
    return pl.pallas_call(
        kernel,
        out_shape=outs,
        in_specs=[spec(pltpu.SMEM)] * n_smem + [spec()] * (len(inputs) - n_smem),
        out_specs=jax.tree.map(lambda _: spec(), outs),
        scratch_shapes=scratch,
        compiler_params=pltpu.CompilerParams(vmem_limit_bytes=VMEM_LIMIT),
        cost_estimate=pl.CostEstimate(flops=flops, bytes_accessed=moved, transcendentals=0),
    )(*inputs)


def local(ctx_size, tp_size, hidden, w_in, w_bc, w_dt, dt_bias, a_log, d_skip, conv_w, w_out, d_out):
    own_rows, width = hidden.shape
    length = own_rows * tp_size * ctx_size
    head = w_out.shape[0]
    nz = tp_size // 4
    t = lax.axis_index("tp")
    ids = jnp.stack([t >> 2, (t >> 1) & 1, t & 1, lax.axis_index("ctx")]).astype(jnp.int32)
    params = jnp.stack([dt_bias[0], -jnp.exp(a_log[0]), d_skip[0]])
    wcat = jnp.concatenate(
        [w_in, w_bc, w_dt.T, jnp.zeros((width, 2 * LANES - 2 * head - 2 * STATE - 1), bf16)], axis=1
    )
    keep_z = jnp.zeros((CONV, LANES - head), f32).at[CONV - 1].set(1.0)
    taps = jnp.concatenate([conv_w, keep_z], axis=1)
    wout = jnp.concatenate([w_out, jnp.zeros((LANES - head, width), bf16)], axis=0)
    wrev = call(
        prep_kernel,
        [wcat],
        0,
        jax.ShapeDtypeStruct(wcat.shape, bf16),
        [],
        2 * width * BLOCK * BLOCK,
        2 * wcat.size * 2,
    )

    def across(value, flip_bits):
        return lax.ppermute(value, "tp", [(i, i ^ flip_bits) for i in range(tp_size)])

    def along(value, offset):
        return lax.ppermute(
            value, "ctx", [((i + offset) % ctx_size, i) for i in range(ctx_size)]
        )

    def along_x(value, offset):
        pairs = []
        for c in range(ctx_size):
            for i in range(tp_size):
                source = ((c + offset) % ctx_size) * tp_size + (i ^ 2)
                pairs.append((source, c * tp_size + i))
        return lax.ppermute(value, ("ctx", "tp"), pairs)

    if own_rows % TILE_ROWS == 0:
        both = jnp.concatenate([hidden, d_out], axis=0)
        column = jnp.concatenate([both] + [across(both, 4 * j) for j in range(1, nz)], axis=0)
        plane = []
        for dc in range(ctx_size):
            plane.append(((dc, 0), along(column, dc) if dc else column))
            plane.append(((dc, 1), along_x(column, dc) if dc else across(column, 2)))
        coords, pieces = [], []
        for (dc, dx), piece in plane:
            coords += [(dc, dx, 0), (dc, dx, 1)]
            pieces += [piece, across(piece, 1)]
        coords = tuple(coords)
        rows = [pltpu.VMEM((length, width), bf16)]
        h_pieces = pieces
    else:
        pieces = [lax.all_gather(a, ("ctx", "tp"), axis=0, tiled=True) for a in (hidden, d_out)]
        h_pieces = pieces[:1]
        coords, rows = None, []
    layout = (tp_size, own_rows, coords)
    extra = 4 * STATE * length // width
    half = tp_size * own_rows // 2
    send, keep, gcat, gated = call(
        functools.partial(core_kernel, len(pieces), layout),
        [ids, params, *pieces, wcat, wrev, wout, taps],
        2,
        (
            jax.ShapeDtypeStruct((extra + half, width), bf16),
            jax.ShapeDtypeStruct((extra + half, width), f32),
            jax.ShapeDtypeStruct((length, 4 * LANES), bf16),
            jax.ShapeDtypeStruct((length, 2 * LANES), bf16),
        ),
        rows * 2,
        8 * length * width * BLOCK,
        8 * length * width,
    )
    scaling = 1.0 / math.sqrt(length)
    got = across(send, 1)
    d_w_in, d_w_out = call(
        functools.partial(weight_kernel, len(pieces), layout, scaling),
        [ids, *pieces, gcat, gated],
        1,
        (
            jax.ShapeDtypeStruct((width, LANES), f32),
            jax.ShapeDtypeStruct((head, width), f32),
        ),
        rows * 2,
        8 * length * width * BLOCK,
        8 * length * width,
    )
    quarter = half // 2
    summed = keep + got.astype(f32)
    send = summed[: extra + quarter].astype(bf16)
    keep = jnp.concatenate(
        [summed[:extra].astype(bf16).astype(f32), summed[extra + quarter :]], axis=0
    )
    summed = keep + across(send, 2).astype(f32)
    shared = [summed[:extra].astype(bf16)]
    total = summed[extra : extra + own_rows]
    for j in range(1, nz):
        at = extra + j * own_rows
        piece = jnp.concatenate([summed[:extra], summed[at : at + own_rows]], axis=0)
        got = across(piece.astype(bf16), 4 * j)
        shared.append(got[:extra])
        total = total + got[extra:].astype(f32)
    while len(shared) > 1:
        shared = [
            a.astype(f32) + b.astype(f32) for a, b in zip(shared[0::2], shared[1::2])
        ]
    d_w_bc = call(
        functools.partial(last_kernel, len(h_pieces), layout, scaling),
        [ids, shared[0], *h_pieces],
        1,
        jax.ShapeDtypeStruct((width, 2 * STATE), f32),
        rows,
        4 * length * width * BLOCK,
        4 * length * width,
    )
    return (total.astype(bf16), d_w_in, d_w_out, d_w_bc)


def solution(mesh):
    in_specs = (
        P(("ctx", "tp"), None),
        P(None, "tp"),
        P(),
        P("tp", None),
        P("tp"),
        P("tp"),
        P("tp"),
        P(None, "tp"),
        P("tp", None),
        P(("ctx", "tp"), None),
    )
    out_specs = (P(("ctx", "tp"), None), P(None, "tp"), P("tp", None), P())
    body = functools.partial(local, mesh.shape["ctx"], mesh.shape["tp"])
    return jax.shard_map(body, mesh=mesh, in_specs=in_specs, out_specs=out_specs, check_vma=False)
```

```python
import functools
import math

import jax
import jax.numpy as jnp
from jax import lax
from jax.experimental import pallas as pl
from jax.experimental.pallas import tpu as pltpu
from jax.sharding import PartitionSpec as P

STATE = 16
CONV = 4
LANES = 128
BLOCK = 256
TILE_ROWS = 16
VMEM_LIMIT = 60 * 1024 * 1024
f32 = jnp.float32
bf16 = jnp.bfloat16


def dot(a, b):
    return jnp.dot(a, b, preferred_element_type=f32)


def dot_nt(a, b):
    return lax.dot_general(a, b, (((1,), (1,)), ((), ())), preferred_element_type=f32)


def dot_tn(a, b):
    return lax.dot_general(a, b, (((0,), (0,)), ((), ())), preferred_element_type=f32)


def iota(shape, dim):
    return lax.broadcasted_iota(jnp.int32, shape, dim)


def mirror(size):
    return jnp.where(iota((size, size), 0) + iota((size, size), 1) == size - 1, 1.0, 0.0).astype(
        bf16
    )


def split(value, terms):
    parts = []
    for _ in range(terms):
        part = value.astype(bf16)
        parts.append(part)
        value = value - part.astype(f32)
    return parts


def flip_rows(value, flip):
    count = value.shape[0] // BLOCK
    return jnp.concatenate(
        [dot(flip, value[(count - 1 - i) * BLOCK : (count - i) * BLOCK]) for i in range(count)],
        axis=0,
    )


def assemble(ids_ref, pieces, out_ref, layout):
    tp_size, own_rows, coords = layout
    z, x, core, ctx = (ids_ref[i] for i in range(4))
    ctx_size = max(c[0] for c in coords) + 1
    for piece, (dc, dx, dcore, blocks) in zip(pieces, coords):
        from_ctx = lax.rem(ctx + dc, ctx_size)
        for k, j in enumerate(blocks):
            owner = ((z ^ j) * 2 + (x ^ dx)) * 2 + (core ^ dcore)
            at = pl.multiple_of((from_ctx * tp_size + owner) * own_rows, own_rows)
            out_ref[pl.ds(at, own_rows), :] = piece[k * own_rows : (k + 1) * own_rows, :]


def turn_columns(value, flip):
    count = value.shape[1] // BLOCK
    return jnp.concatenate(
        [dot(value[:, (count - 1 - i) * BLOCK : (count - i) * BLOCK], flip) for i in range(count)],
        axis=1,
    )


def prep_kernel(win_ref, wbct_ref, wdt_ref, wout_ref, conv_ref, late_ref, *outs):
    wcat_ref, wrev_ref, wpad_ref, wturn_ref, taps_ref, copy_ref = outs
    copy_ref[...] = late_ref[...]
    flip = mirror(BLOCK)
    width = win_ref.shape[0]
    head = wout_ref.shape[0]
    count = width // BLOCK
    for i in range(count):
        cols = slice(i * BLOCK, (i + 1) * BLOCK)
        rows = jnp.concatenate(
            [
                wbct_ref[:, cols].astype(f32),
                wdt_ref[:, cols].astype(f32),
                jnp.zeros((LANES - 2 * STATE - 1, BLOCK), f32),
            ],
            axis=0,
        )
        wcat_ref[cols, :LANES] = win_ref[cols, :]
        wcat_ref[cols, LANES:] = jnp.transpose(rows).astype(bf16)
    for i in range(count):
        wrev_ref[i * BLOCK : (i + 1) * BLOCK, :] = dot(
            flip, wcat_ref[(count - 1 - i) * BLOCK : (count - i) * BLOCK, :]
        ).astype(bf16)
    zeros = jnp.zeros((LANES - head, width), bf16)
    wpad_ref[:head, :] = wout_ref[...]
    wpad_ref[head:, :] = zeros
    wturn_ref[...] = turn_columns(wpad_ref[...], flip).astype(bf16)
    tap = iota((CONV, LANES - head), 0)
    taps_ref[:, :head] = conv_ref[...]
    taps_ref[:, head:] = jnp.where(tap == CONV - 1, 1.0, 0.0)


def own_source(shape, dim, ids_ref, tp_size, own_rows):
    z, x, core, ctx = (ids_ref[i] for i in range(4))
    nz = tp_size // 4
    row = iota(shape, dim)
    block = row // own_rows
    j = block % nz
    dx = 1 - (block // nz) % 2
    dcore = 1 - block // (2 * nz)
    owner = ((z ^ j) * 2 + (x ^ dx)) * 2 + (core ^ dcore)
    return (ctx * tp_size + owner) * own_rows + row % own_rows


def exact(parts, apply):
    return sum(apply(part) for part in parts)


def decay_rate(par_refs):
    return -jnp.exp(jnp.full((1, LANES), par_refs[1][0], f32))


def forward_kernel(n_pieces, layout, *refs):
    ids_ref, par_refs = refs[0], refs[1:4]
    pieces = refs[4 : 4 + n_pieces]
    wcat_ref, wrev_ref, taps_ref = refs[4 + n_pieces : 7 + n_pieces]
    full_ref, low_ref, state_ref, gated_ref = refs[7 + n_pieces : 11 + n_pieces]
    if layout[2] is None:
        h_ref = pieces[0]
    else:
        h_ref = refs[11 + n_pieces]
        assemble(ids_ref, pieces, h_ref, layout)
    length, width = h_ref.shape
    chunks = length // BLOCK
    columns = width // BLOCK
    flip = mirror(BLOCK)
    bias, rate, skip = par_refs[0][0], decay_rate(par_refs), par_refs[2][0]
    lane = iota((1, LANES), 1)
    low = lane < LANES // 2
    causal = iota((BLOCK, BLOCK), 0) >= iota((BLOCK, BLOCK), 1)
    tri = jnp.where(causal, 1.0, 0.0).astype(bf16)
    row_at = iota((length, LANES), 0)

    proj_f = dot(h_ref[...], wcat_ref[...])
    proj_r = dot(h_ref[...], wrev_ref[...])
    xz_r = flip_rows(proj_r[:, :LANES].astype(bf16), flip)
    rest_r = exact(split(proj_r[:, LANES:], 3), lambda part: flip_rows(part, flip))
    strands = (
        (proj_f[:, :LANES].astype(bf16).astype(f32), proj_f[:, LANES:]),
        (xz_r, rest_r),
    )
    for s, (xz, rest) in enumerate(strands):
        pre = taps_ref[CONV - 1 : CONV, :] * xz
        for shift in range(1, CONV):
            moved = jnp.where(row_at >= shift, pltpu.roll(xz, shift, 0), 0.0)
            pre += taps_ref[CONV - 1 - shift : CONV - shift, :] * moved
        sig = jax.nn.sigmoid(pre)
        u = pre * sig
        raw = jnp.broadcast_to(rest[:, 2 * STATE : 2 * STATE + 1], (length, LANES)) + bias
        dt = jnp.maximum(raw, 0.0) + jnp.log1p(jnp.exp(-jnp.abs(raw)))
        b_all = jnp.where(lane < STATE, rest, 0.0)
        c_all = jnp.where(lane < STATE, pltpu.roll(rest, LANES - STATE, 1), 0.0)
        w_all = dt * u
        full_ref[s, :, 0:LANES] = u
        full_ref[s, :, LANES : 2 * LANES] = sig * (1.0 + pre * (1.0 - sig))
        full_ref[s, :, 2 * LANES : 3 * LANES] = dt
        full_ref[s, :, 3 * LANES : 4 * LANES] = jax.nn.sigmoid(raw)
        low_ref[s, :, 0:LANES] = b_all.astype(bf16)
        low_ref[s, :, LANES : 2 * LANES] = c_all.astype(bf16)
        low_ref[s, :, 2 * LANES : 3 * LANES] = w_all.astype(bf16)
        state = jnp.zeros((LANES, LANES), f32)
        state_ref[s, 0] = state
        for c in range(chunks):
            rows = slice(c * BLOCK, (c + 1) * BLOCK)
            log_keep = exact(split(dt[rows] * rate, 3), lambda part: dot(tri, part))
            across = jnp.transpose(log_keep)[0:1, :]
            gap = jnp.concatenate([log_keep] * (BLOCK // LANES), axis=1) - across
            decay = jnp.exp(jnp.where(causal, gap, -jnp.inf))
            b_low, c_low = b_all[rows].astype(bf16), c_all[rows].astype(bf16)
            w_low = w_all[rows].astype(bf16)
            mixed = (dot_nt(c_low, b_low) * decay).astype(bf16)
            last = log_keep[BLOCK - 1 : BLOCK, :]
            b_left = (jnp.exp(last - log_keep) * b_all[rows]).astype(bf16)
            out = dot(mixed, w_low) + jnp.exp(log_keep) * dot(c_low, state.astype(bf16))
            state = jnp.exp(last) * state + dot_tn(b_left, w_low)
            full_ref[s, rows, 4 * LANES : 5 * LANES] = out
            full_ref[s, rows, 5 * LANES : 6 * LANES] = log_keep
            full_ref[s, rows, 6 * LANES :] = decay
            low_ref[s, rows, 3 * LANES : 4 * LANES] = b_left
            low_ref[s, rows, 4 * LANES :] = mixed
            state_ref[s, c + 1] = state
        y = full_ref[s, :, 4 * LANES : 5 * LANES] + skip * u
        gated = jnp.where(low, y * pltpu.roll(u, LANES // 2, 1), 0.0).astype(bf16)
        if s == 1:
            gated = flip_rows(gated, flip).astype(bf16)
        gated_ref[:, s * LANES : (s + 1) * LANES] = gated


def backward_kernel(n_pieces, layout, *refs):
    ids_ref, par_refs = refs[0], refs[1:4]
    pieces = refs[4 : 4 + n_pieces]
    full_ref, low_ref, state_ref = refs[4 + n_pieces : 7 + n_pieces]
    wcat_ref, wrev_ref, wpad_ref, wturn_ref, taps_ref = refs[7 + n_pieces : 12 + n_pieces]
    send_ref, keep_ref, gcat_ref = refs[12 + n_pieces : 15 + n_pieces]
    tp_size, own_rows, coords = layout
    if coords is None:
        d_ref = pieces[0]
    else:
        d_ref = refs[15 + n_pieces]
        assemble(ids_ref, pieces, d_ref, layout)
    length, width = d_ref.shape
    chunks = length // BLOCK
    columns = width // BLOCK
    flip = mirror(BLOCK)
    rate, skip = decay_rate(par_refs), par_refs[2][0]
    lane = iota((1, LANES), 1)
    low = lane < LANES // 2
    tri = jnp.where(iota((BLOCK, BLOCK), 0) >= iota((BLOCK, BLOCK), 1), 1.0, 0.0).astype(bf16)
    row_at = iota((length, LANES), 0)
    grad_f = dot_nt(d_ref[...], wpad_ref[...])
    grad_r = exact(
        split(dot_nt(d_ref[...], wturn_ref[...]), 2), lambda part: flip_rows(part, flip)
    )
    small = []
    for s, grad_g in enumerate((grad_f, grad_r)):
        u = full_ref[s, :, 0:LANES]
        slope = full_ref[s, :, LANES : 2 * LANES]
        dt = full_ref[s, :, 2 * LANES : 3 * LANES]
        dt_slope = full_ref[s, :, 3 * LANES : 4 * LANES]
        out = full_ref[s, :, 4 * LANES : 5 * LANES]
        u_other = pltpu.roll(u, LANES // 2, 1)
        g_y = jnp.where(low, grad_g * u_other, 0.0)
        g_gate = jnp.where(low, grad_g * (out + skip * u), 0.0)
        d_state = jnp.zeros((LANES, LANES), f32)
        d_w, g_b, g_c, g_a = [None] * chunks, [None] * chunks, [None] * chunks, [None] * chunks
        for c in reversed(range(chunks)):
            rows = slice(c * BLOCK, (c + 1) * BLOCK)
            log_keep = full_ref[s, rows, 5 * LANES : 6 * LANES]
            decay = full_ref[s, rows, 6 * LANES :]
            b_low = low_ref[s, rows, 0:LANES]
            c_low = low_ref[s, rows, LANES : 2 * LANES]
            w_low = low_ref[s, rows, 2 * LANES : 3 * LANES]
            b_left = low_ref[s, rows, 3 * LANES : 4 * LANES]
            mixed = low_ref[s, rows, 4 * LANES :]
            last = log_keep[BLOCK - 1 : BLOCK, :]
            enter = jnp.exp(log_keep)
            leave = jnp.exp(last - log_keep)
            gy = g_y[rows]
            gy_low = gy.astype(bf16)
            ds_low = d_state.astype(bf16)
            dw = dot_tn(mixed, gy_low) + dot(b_left, ds_low)
            d_scores = (dot_nt(gy_low, w_low) * decay).astype(bf16)
            g_c[c] = dot(d_scores, b_low) + enter * dot_nt(
                gy_low, state_ref[s, c].astype(bf16)
            )
            g_b[c] = dot_tn(d_scores, c_low) + leave * dot_nt(w_low, ds_low)
            d_log = jnp.sum(
                jnp.where(low, gy * out[rows] - dt[rows] * u[rows] * dw, 0.0),
                axis=1,
                keepdims=True,
            )
            at_end = jnp.sum(jnp.where(low, state_ref[s, c + 1] * d_state, 0.0))
            d_log = jnp.broadcast_to(d_log, (BLOCK, LANES))
            d_sum = exact(split(d_log, 2), lambda part: dot_tn(tri, part)) + at_end
            g_a[c] = rate * d_sum + jnp.sum(
                jnp.where(low, u[rows] * dw, 0.0), axis=1, keepdims=True
            )
            d_w[c] = dw
            carried = (enter * c_low).astype(bf16)
            d_state = jnp.exp(last) * d_state + dot_tn(carried, gy_low)
        d_w = jnp.concatenate(d_w, axis=0)
        g_b = jnp.concatenate(g_b, axis=0)
        g_c = jnp.concatenate(g_c, axis=0)
        g_raw = jnp.concatenate(g_a, axis=0) * dt_slope
        d_u = jnp.where(low, skip * g_y + dt * d_w, pltpu.roll(g_gate, LANES // 2, 1))
        d_pre = d_u * slope
        g_xz = taps_ref[CONV - 1 : CONV, :] * d_pre
        for shift in range(1, CONV):
            moved = jnp.where(
                row_at < length - shift, pltpu.roll(d_pre, length - shift, 0), 0.0
            )
            g_xz += taps_ref[CONV - 1 - shift : CONV - shift, :] * moved
        shared = jnp.where(lane < STATE, g_b, 0.0) + jnp.where(
            (lane >= STATE) & (lane < 2 * STATE), pltpu.roll(g_c, STATE, 1), 0.0
        )
        g_rest = shared + jnp.where(lane == 2 * STATE, g_raw, 0.0)
        g_cat = jnp.concatenate([g_xz, g_rest], axis=1).astype(bf16)
        small.append(shared)
        if s == 0:
            gcat_ref[:, : 2 * LANES] = g_cat
        else:
            gcat_ref[:, 2 * LANES :] = flip_rows(g_cat, flip).astype(bf16)

    pair = small[0] + pltpu.roll(small[1], 2 * STATE, 1)
    shared_t = jnp.transpose(pair)[: 4 * STATE].astype(bf16)
    groups = width // length
    step = 4 * STATE // groups
    for i in range(groups):
        part = shared_t[i * step : (i + 1) * step, :]
        send_ref[0:step, i * length : (i + 1) * length] = part
        keep_ref[0:step, i * length : (i + 1) * length] = part.astype(f32)
    own = tp_size * own_rows
    source = own_source((own, length), 0, ids_ref, tp_size, own_rows)
    pick = jnp.where(source == iota((own, length), 1), 1.0, 0.0).astype(bf16)
    picked = dot(pick, gcat_ref[...]).astype(bf16)
    half = own // 2
    for i in range(columns):
        cols = slice(i * BLOCK, (i + 1) * BLOCK)
        part = dot_nt(picked[:, : 2 * LANES], wcat_ref[cols, :]) + dot_nt(
            picked[:, 2 * LANES :], wrev_ref[cols, :]
        )
        send_ref[step:, cols] = part[:half].astype(bf16)
        keep_ref[step:, cols] = part[half:]


def weight_kernel(n_h, n_d, h_layout, d_layout, scaling, *refs):
    ids_ref = refs[0]
    h_pieces = refs[1 : 1 + n_h]
    d_pieces = refs[1 + n_h : 1 + n_h + n_d]
    refs = refs[1 + n_h + n_d :]
    gcat_ref, gated_ref, dwin_ref, dwout_ref = refs[:4]
    if h_layout[2] is None:
        h_ref, d_ref = h_pieces[0], d_pieces[0]
    else:
        h_ref, d_ref = refs[4:]
        assemble(ids_ref, h_pieces, h_ref, h_layout)
        assemble(ids_ref, d_pieces, d_ref, d_layout)
    flip = mirror(BLOCK)
    columns = h_ref.shape[1] // BLOCK
    head = dwout_ref.shape[0]
    g_f = gcat_ref[:, 0:LANES]
    g_r = gcat_ref[:, 2 * LANES : 3 * LANES]
    y_f = gated_ref[:, 0:LANES]
    y_r = gated_ref[:, LANES:]
    for i in range(columns):
        cols = slice(i * BLOCK, (i + 1) * BLOCK)
        back = slice((columns - 1 - i) * BLOCK, (columns - i) * BLOCK)
        turned = dot(h_ref[:, back], flip).astype(bf16)
        grad = dot_tn(g_f, h_ref[:, cols]) + dot_tn(g_r, turned)
        dwin_ref[cols, :] = jnp.transpose(grad * scaling)
        turned = dot(d_ref[:, back], flip).astype(bf16)
        grad = dot_tn(y_f, d_ref[:, cols]) + dot_tn(y_r, turned)
        dwout_ref[:, cols] = grad[:head] * scaling


def last_kernel(n_got, n_pieces, layout, scaling, *refs):
    ids_ref, own_ref = refs[:2]
    got_refs = refs[2 : 2 + n_got]
    pieces = refs[2 + n_got : 2 + n_got + n_pieces]
    refs = refs[2 + n_got + n_pieces :]
    dhid_ref, dwbct_ref = refs[:2]
    if layout[2] is None:
        h_ref = pieces[0]
    else:
        h_ref = refs[2]
        assemble(ids_ref, pieces, h_ref, layout)
    flip = mirror(BLOCK)
    length, width = h_ref.shape
    own_rows = layout[1]
    groups = width // length
    extra = 4 * STATE // groups
    total = own_ref[extra : extra + own_rows, :]
    for got in got_refs:
        total += got[extra : extra + own_rows, :].astype(f32)
    dhid_ref[...] = total.astype(bf16)
    sums = [own_ref[:extra, :].astype(bf16).astype(f32)]
    sums += [got[:extra, :].astype(f32) for got in got_refs]
    while len(sums) > 1:
        sums = [a + b for a, b in zip(sums[0::2], sums[1::2])]
    shared = sums[0].astype(bf16)
    shared = jnp.concatenate(
        [shared[:, i * length : (i + 1) * length] for i in range(groups)], axis=0
    )
    fwd = shared[: 2 * STATE]
    rev = turn_columns(shared[2 * STATE :], flip).astype(bf16)
    pairs = dot(jnp.concatenate([fwd, rev], axis=0), h_ref[...])
    turned = exact(split(pairs[2 * STATE :], 3), lambda part: turn_columns(part, flip))
    dwbct_ref[...] = (pairs[: 2 * STATE] + turned) * scaling


def spec(memory=pltpu.VMEM):
    return pl.BlockSpec(memory_space=memory)


def call(kernel, inputs, n_smem, outs, scratch, flops, moved):
    return pl.pallas_call(
        kernel,
        out_shape=outs,
        in_specs=[spec(pltpu.SMEM)] * n_smem + [spec()] * (len(inputs) - n_smem),
        out_specs=jax.tree.map(lambda _: spec(), outs),
        scratch_shapes=scratch,
        compiler_params=pltpu.CompilerParams(vmem_limit_bytes=VMEM_LIMIT),
        cost_estimate=pl.CostEstimate(flops=flops, bytes_accessed=moved, transcendentals=0),
    )(*inputs)


def shape(dims, dtype):
    return jax.ShapeDtypeStruct(dims, dtype)


def local(ctx_size, tp_size, hidden, w_in, w_bc, w_dt, dt_bias, a_log, d_skip, conv_w, w_out, d_out):
    own_rows, width = hidden.shape
    length = own_rows * tp_size * ctx_size
    head = w_out.shape[0]
    nz = tp_size // 4
    chunks = length // BLOCK
    t = lax.axis_index("tp")
    ids = jnp.stack([t >> 2, (t >> 1) & 1, t & 1, lax.axis_index("ctx")]).astype(jnp.int32)
    params = [dt_bias, a_log, d_skip]
    wcat, wrev, wpad, wturn, taps, late = call(
        prep_kernel,
        [w_in, w_bc.T, w_dt, w_out, conv_w, d_out],
        0,
        (
            shape((width, 2 * LANES), bf16),
            shape((width, 2 * LANES), bf16),
            shape((LANES, width), bf16),
            shape((LANES, width), bf16),
            shape((CONV, LANES), f32),
            shape(d_out.shape, bf16),
        ),
        [],
        2 * width * BLOCK * BLOCK,
        8 * width * LANES,
    )

    def across(value, flip_bits):
        return lax.ppermute(value, "tp", [(i, i ^ flip_bits) for i in range(tp_size)])

    def along(value, offset):
        return lax.ppermute(
            value, "ctx", [((i + offset) % ctx_size, i) for i in range(ctx_size)]
        )

    def gather(own):
        zs = [own] + [across(own, 4 * j) for j in range(1, nz)]
        groups = [range(0, nz // 2), range(nz // 2, nz)]
        coords, pieces = [], []
        for g, blocks in enumerate(groups):
            chunk = jnp.concatenate([zs[j] for j in blocks], axis=0)
            beside = across(chunk, 2)
            plane = [((0, 0), chunk), ((0, 1), beside)]
            for dc in range(1, ctx_size):
                ahead = along(chunk, dc)
                diagonal = across(ahead, 2) if g == 0 else along(beside, dc)
                plane += [((dc, 0), ahead), ((dc, 1), diagonal)]
            for (dc, dx), piece in plane:
                coords += [(dc, dx, 0, tuple(blocks)), (dc, dx, 1, tuple(blocks))]
                pieces += [piece, across(piece, 1)]
        return pieces, (tp_size, own_rows, tuple(coords))

    if own_rows % TILE_ROWS == 0:
        h_pieces, layout = gather(hidden)
        d_pieces, _ = gather(late)
        rows = [pltpu.VMEM((length, width), bf16)]
    else:
        h_pieces, d_pieces = (
            [lax.all_gather(a, ("ctx", "tp"), axis=0, tiled=True)] for a in (hidden, late)
        )
        layout, rows = (tp_size, own_rows, None), []
    n_pieces = len(h_pieces)
    extra = 4 * STATE * length // width
    half = tp_size * own_rows // 2
    full, low, states, gated = call(
        functools.partial(forward_kernel, n_pieces, layout),
        [ids, *params, *h_pieces, wcat, wrev, taps],
        4,
        (
            shape((2, length, 6 * LANES + BLOCK), f32),
            shape((2, length, 4 * LANES + BLOCK), bf16),
            shape((2, chunks + 1, LANES, LANES), f32),
            shape((length, 2 * LANES), bf16),
        ),
        rows,
        4 * length * width * BLOCK,
        16 * length * width,
    )
    send, keep, gcat = call(
        functools.partial(backward_kernel, n_pieces, layout),
        [ids, *params, *d_pieces, full, low, states, wcat, wrev, wpad, wturn, taps],
        4,
        (
            shape((extra + half, width), bf16),
            shape((extra + half, width), f32),
            shape((length, 4 * LANES), bf16),
        ),
        rows,
        4 * length * width * BLOCK,
        16 * length * width,
    )
    scaling = 1.0 / math.sqrt(length)
    got = across(send, 1)
    d_w_in, d_w_out = call(
        functools.partial(weight_kernel, n_pieces, n_pieces, layout, layout, scaling),
        [ids, *h_pieces, *d_pieces, gcat, gated],
        1,
        (
            shape((width, LANES), f32),
            shape((head, width), f32),
        ),
        rows * 2,
        8 * length * width * BLOCK,
        8 * length * width,
    )
    quarter = half // 2
    summed = keep + got.astype(f32)
    send = summed[: extra + quarter].astype(bf16)
    keep = jnp.concatenate(
        [summed[:extra].astype(bf16).astype(f32), summed[extra + quarter :]], axis=0
    )
    summed = keep + across(send, 2).astype(f32)
    got = []
    for j in range(1, nz):
        at = extra + j * own_rows
        piece = jnp.concatenate([summed[:extra], summed[at : at + own_rows]], axis=0)
        got.append(across(piece.astype(bf16), 4 * j))
    d_hidden, d_w_bc = call(
        functools.partial(last_kernel, len(got), n_pieces, layout, scaling),
        [ids, summed[: extra + own_rows], *got, *h_pieces],
        1,
        (shape((own_rows, width), bf16), shape((2 * STATE, width), f32)),
        rows,
        2 * length * width * LANES,
        4 * length * width,
    )
    return (d_hidden, d_w_in, d_w_out, d_w_bc.T)


def solution(mesh):
    in_specs = (
        P(("ctx", "tp"), None),
        P(None, "tp"),
        P(),
        P("tp", None),
        P("tp"),
        P("tp"),
        P("tp"),
        P(None, "tp"),
        P("tp", None),
        P(("ctx", "tp"), None),
    )
    out_specs = (P(("ctx", "tp"), None), P(None, "tp"), P("tp", None), P())
    body = functools.partial(local, mesh.shape["ctx"], mesh.shape["tp"])
    return jax.shard_map(body, mesh=mesh, in_specs=in_specs, out_specs=out_specs, check_vma=False)
```

```python
import functools
import math

import jax
import jax.numpy as jnp
from jax import lax
from jax.experimental import pallas as pl
from jax.experimental.pallas import tpu as pltpu
from jax.sharding import PartitionSpec as P

STATE = 16
CONV = 4
LANES = 128
BLOCK = 256
TILE_ROWS = 16
VMEM_LIMIT = 60 * 1024 * 1024
f32 = jnp.float32
bf16 = jnp.bfloat16


def dot(a, b):
    return jnp.dot(a, b, preferred_element_type=f32)


def dot_nt(a, b):
    return lax.dot_general(a, b, (((1,), (1,)), ((), ())), preferred_element_type=f32)


def dot_tn(a, b):
    return lax.dot_general(a, b, (((0,), (0,)), ((), ())), preferred_element_type=f32)


def iota(shape, dim):
    return lax.broadcasted_iota(jnp.int32, shape, dim)


def mirror(size):
    return jnp.where(iota((size, size), 0) + iota((size, size), 1) == size - 1, 1.0, 0.0).astype(
        bf16
    )


def split(value, terms):
    parts = []
    for _ in range(terms):
        part = value.astype(bf16)
        parts.append(part)
        value = value - part.astype(f32)
    return parts


def flip_rows(value, flip):
    count = value.shape[0] // BLOCK
    return jnp.concatenate(
        [dot(flip, value[(count - 1 - i) * BLOCK : (count - i) * BLOCK]) for i in range(count)],
        axis=0,
    )


def assemble(ids_ref, pieces, h_ref, d_ref, layout):
    tp_size, own_rows, coords = layout
    z, x, core, ctx = (ids_ref[i] for i in range(4))
    ctx_size = max(c[0] for c in coords) + 1
    for piece, (dc, dx, dcore, blocks) in zip(pieces, coords):
        from_ctx = lax.rem(ctx + dc, ctx_size)
        for k, j in enumerate(blocks):
            owner = ((z ^ j) * 2 + (x ^ dx)) * 2 + (core ^ dcore)
            at = pl.multiple_of((from_ctx * tp_size + owner) * own_rows, own_rows)
            base = 2 * k * own_rows
            h_ref[pl.ds(at, own_rows), :] = piece[base : base + own_rows, :]
            if d_ref is not None:
                d_ref[pl.ds(at, own_rows), :] = piece[base + own_rows : base + 2 * own_rows, :]


def turn_columns(value, flip):
    count = value.shape[1] // BLOCK
    return jnp.concatenate(
        [dot(value[:, (count - 1 - i) * BLOCK : (count - i) * BLOCK], flip) for i in range(count)],
        axis=1,
    )


def prep_kernel(win_ref, wbct_ref, wdt_ref, wout_ref, conv_ref, *outs):
    wall_ref, wallt_ref, gall_ref, taps_ref = outs
    flip = mirror(BLOCK)
    width = win_ref.shape[0]
    head = wout_ref.shape[0]
    count = width // BLOCK
    shared = 2 * STATE + 1
    for i in range(count):
        cols = slice(i * BLOCK, (i + 1) * BLOCK)
        rows = jnp.concatenate(
            [
                wbct_ref[:, cols].astype(f32),
                wdt_ref[:, cols].astype(f32),
                jnp.zeros((LANES - shared, BLOCK), f32),
            ],
            axis=0,
        )
        block = win_ref[cols, :]
        wall_ref[cols, :LANES] = block
        wall_ref[cols, LANES : 2 * LANES] = jnp.transpose(rows).astype(bf16)
        wallt_ref[:LANES, cols] = jnp.transpose(block.astype(f32)).astype(bf16)
        wallt_ref[LANES : 2 * LANES, cols] = rows.astype(bf16)
        out = jnp.concatenate(
            [wout_ref[:, cols].astype(f32), jnp.zeros((LANES - head, BLOCK), f32)], axis=0
        )
        gall_ref[cols, :LANES] = jnp.transpose(out).astype(bf16)
    for i in range(count):
        cols = slice(i * BLOCK, (i + 1) * BLOCK)
        back = slice((count - 1 - i) * BLOCK, (count - i) * BLOCK)
        wall_ref[cols, 2 * LANES :] = dot(flip, wall_ref[back, : 2 * LANES]).astype(bf16)
        gall_ref[cols, LANES:] = dot(flip, gall_ref[back, :LANES]).astype(bf16)
        wallt_ref[2 * LANES :, cols] = dot(wallt_ref[: 2 * LANES, back], flip).astype(bf16)
    tap = iota((CONV, LANES - head), 0)
    taps_ref[:, :head] = conv_ref[...]
    taps_ref[:, head:] = jnp.where(tap == CONV - 1, 1.0, 0.0)


def pack_kernel(*refs):
    out_ref = refs[-1]
    at = 0
    for ref in refs[:-2]:
        out_ref[at : at + ref.shape[0], :] = ref[...]
        at += ref.shape[0]


def own_source(shape, dim, ids_ref, tp_size, own_rows):
    z, x, core, ctx = (ids_ref[i] for i in range(4))
    nz = tp_size // 4
    row = iota(shape, dim)
    block = row // own_rows
    j = block % nz
    dx = 1 - (block // nz) % 2
    dcore = 1 - block // (2 * nz)
    owner = ((z ^ j) * 2 + (x ^ dx)) * 2 + (core ^ dcore)
    return (ctx * tp_size + owner) * own_rows + row % own_rows


def exact(parts, apply):
    return sum(apply(part) for part in parts)


def decay_rate(par_refs):
    return -jnp.exp(jnp.full((1, LANES), par_refs[1][0], f32))


def core_kernel(n_pieces, layout, *refs):
    ids_ref, par_refs = refs[0], refs[1:4]
    pieces = refs[4 : 4 + n_pieces]
    wall_ref, wallt_ref, gall_ref, taps_ref = refs[4 + n_pieces : 8 + n_pieces]
    send_ref, keep_ref, gcat_ref, gated_ref = refs[8 + n_pieces : 12 + n_pieces]
    tp_size, own_rows, coords = layout
    if coords is None:
        h_ref, d_ref = pieces
    else:
        h_ref, d_ref = refs[12 + n_pieces :]
        assemble(ids_ref, pieces, h_ref, d_ref, layout)
    length, width = h_ref.shape
    chunks = length // BLOCK
    flip = mirror(BLOCK)
    bias, rate, skip = par_refs[0][0], decay_rate(par_refs), par_refs[2][0]
    lane = iota((1, LANES), 1)
    low = lane < LANES // 2
    causal = iota((BLOCK, BLOCK), 0) >= iota((BLOCK, BLOCK), 1)
    tri = jnp.where(causal, 1.0, 0.0).astype(bf16)
    row_at = iota((length, LANES), 0)

    proj = dot(h_ref[...], wall_ref[...])
    grads = dot(d_ref[...], gall_ref[...])
    turned = [proj[:, 2 * LANES : 3 * LANES].astype(bf16)]
    turned += split(proj[:, 3 * LANES :], 3) + split(grads[:, LANES:], 2)
    turned = flip_rows(jnp.concatenate(turned, axis=1), flip)
    turned = [turned[:, i * LANES : (i + 1) * LANES] for i in range(6)]
    strands = (
        (
            proj[:, :LANES].astype(bf16).astype(f32),
            proj[:, LANES : 2 * LANES],
            grads[:, :LANES],
        ),
        (turned[0], turned[1] + turned[2] + turned[3], turned[4] + turned[5]),
    )
    small = []
    for s, (xz, rest, grad_g) in enumerate(strands):
        pre = taps_ref[CONV - 1 : CONV, :] * xz
        for shift in range(1, CONV):
            moved = jnp.where(row_at >= shift, pltpu.roll(xz, shift, 0), 0.0)
            pre += taps_ref[CONV - 1 - shift : CONV - shift, :] * moved
        sig = jax.nn.sigmoid(pre)
        u = pre * sig
        slope = sig * (1.0 + pre * (1.0 - sig))
        u_other = pltpu.roll(u, LANES // 2, 1)
        raw = jnp.broadcast_to(rest[:, 2 * STATE : 2 * STATE + 1], (length, LANES)) + bias
        dt = jnp.maximum(raw, 0.0) + jnp.log1p(jnp.exp(-jnp.abs(raw)))
        b_all = jnp.where(lane < STATE, rest, 0.0)
        c_all = jnp.where(lane < STATE, pltpu.roll(rest, LANES - STATE, 1), 0.0)
        w_all = dt * u
        g_y = jnp.where(low, grad_g * u_other, 0.0)
        state = jnp.zeros((LANES, LANES), f32)
        saved, outs = [], []
        for c in range(chunks):
            rows = slice(c * BLOCK, (c + 1) * BLOCK)
            log_keep = dot(tri, jnp.concatenate(split(dt[rows] * rate, 3), axis=1))
            log_keep = (
                log_keep[:, :LANES] + log_keep[:, LANES : 2 * LANES] + log_keep[:, 2 * LANES :]
            )
            across = jnp.transpose(log_keep)[0:1, :]
            gap = jnp.concatenate([log_keep] * (BLOCK // LANES), axis=1) - across
            decay = jnp.exp(jnp.where(causal, gap, -jnp.inf))
            b_low, c_low = b_all[rows].astype(bf16), c_all[rows].astype(bf16)
            w_low = w_all[rows].astype(bf16)
            mixed = (dot_nt(c_low, b_low) * decay).astype(bf16)
            last = log_keep[BLOCK - 1 : BLOCK, :]
            enter = jnp.exp(log_keep)
            leave = jnp.exp(last - log_keep)
            b_left = (leave * b_all[rows]).astype(bf16)
            out = dot(mixed, w_low) + enter * dot(c_low, state.astype(bf16))
            before = state
            state = jnp.exp(last) * state + dot_tn(b_left, w_low)
            saved.append(
                (decay, mixed, b_low, c_low, w_low, b_left, enter, leave, last, before, state)
            )
            outs.append(out)
        out = jnp.concatenate(outs, axis=0)
        y = out + skip * u
        gated = jnp.where(low, y * u_other, 0.0).astype(bf16)
        g_gate = jnp.where(low, grad_g * y, 0.0)
        d_state = jnp.zeros((LANES, LANES), f32)
        d_w, g_b, g_c, g_a = [None] * chunks, [None] * chunks, [None] * chunks, [None] * chunks
        for c in reversed(range(chunks)):
            rows = slice(c * BLOCK, (c + 1) * BLOCK)
            decay, mixed, b_low, c_low, w_low, b_left, enter, leave, last, before, after = saved[c]
            gy = g_y[rows]
            gy_low = gy.astype(bf16)
            ds_low = d_state.astype(bf16)
            dw = dot_tn(mixed, gy_low) + dot(b_left, ds_low)
            d_scores = (dot_nt(gy_low, w_low) * decay).astype(bf16)
            g_c[c] = dot(d_scores, b_low) + enter * dot_nt(gy_low, before.astype(bf16))
            g_b[c] = dot_tn(d_scores, c_low) + leave * dot_nt(w_low, ds_low)
            d_log = jnp.sum(
                jnp.where(low, gy * outs[c] - w_all[rows] * dw, 0.0), axis=1, keepdims=True
            )
            at_end = jnp.sum(jnp.where(low, after * d_state, 0.0))
            d_log = jnp.broadcast_to(d_log, (BLOCK, LANES))
            d_sum = dot_tn(tri, jnp.concatenate(split(d_log, 2), axis=1))
            d_sum = d_sum[:, :LANES] + d_sum[:, LANES:] + at_end
            g_a[c] = rate * d_sum + jnp.sum(
                jnp.where(low, u[rows] * dw, 0.0), axis=1, keepdims=True
            )
            d_w[c] = dw
            carried = (enter * c_all[rows]).astype(bf16)
            d_state = jnp.exp(last) * d_state + dot_tn(carried, gy_low)
        d_w = jnp.concatenate(d_w, axis=0)
        g_b = jnp.concatenate(g_b, axis=0)
        g_c = jnp.concatenate(g_c, axis=0)
        g_raw = jnp.concatenate(g_a, axis=0) * jax.nn.sigmoid(raw)
        d_u = jnp.where(low, skip * g_y + dt * d_w, pltpu.roll(g_gate, LANES // 2, 1))
        d_pre = d_u * slope
        g_xz = taps_ref[CONV - 1 : CONV, :] * d_pre
        for shift in range(1, CONV):
            moved = jnp.where(
                row_at < length - shift, pltpu.roll(d_pre, length - shift, 0), 0.0
            )
            g_xz += taps_ref[CONV - 1 - shift : CONV - shift, :] * moved
        shared = jnp.where(lane < STATE, g_b, 0.0) + jnp.where(
            (lane >= STATE) & (lane < 2 * STATE), pltpu.roll(g_c, STATE, 1), 0.0
        )
        g_rest = shared + jnp.where(lane == 2 * STATE, g_raw, 0.0)
        result = jnp.concatenate([g_xz.astype(bf16), g_rest.astype(bf16), gated], axis=1)
        small.append(shared)
        if s == 1:
            result = flip_rows(result, flip).astype(bf16)
        gcat_ref[:, 2 * s * LANES : 2 * (s + 1) * LANES] = result[:, : 2 * LANES]
        gated_ref[:, s * LANES : (s + 1) * LANES] = result[:, 2 * LANES :]

    pair = small[0] + pltpu.roll(small[1], 2 * STATE, 1)
    shared_t = jnp.transpose(pair)[: 4 * STATE].astype(bf16)
    groups = width // length
    step = 4 * STATE // groups
    for i in range(groups):
        part = shared_t[i * step : (i + 1) * step, :]
        send_ref[0:step, i * length : (i + 1) * length] = part
        keep_ref[0:step, i * length : (i + 1) * length] = part.astype(f32)
    own = tp_size * own_rows
    source = own_source((own, length), 0, ids_ref, tp_size, own_rows)
    pick = jnp.where(source == iota((own, length), 1), 1.0, 0.0).astype(bf16)
    picked = dot(pick, gcat_ref[...]).astype(bf16)
    half = own // 2
    part = dot(picked, wallt_ref[...])
    send_ref[step:, :] = part[:half].astype(bf16)
    keep_ref[step:, :] = part[half:]


def weight_kernel(n_pieces, layout, scaling, *refs):
    ids_ref = refs[0]
    pieces = refs[1 : 1 + n_pieces]
    gcat_ref, gated_ref, dwin_ref, dwout_ref = refs[1 + n_pieces : 5 + n_pieces]
    if layout[2] is None:
        h_ref, d_ref = pieces
    else:
        h_ref, d_ref = refs[5 + n_pieces :]
        assemble(ids_ref, pieces, h_ref, d_ref, layout)
    flip = mirror(BLOCK)
    columns = h_ref.shape[1] // BLOCK
    head = dwout_ref.shape[0]
    g_f = gcat_ref[:, 0:LANES]
    g_r = gcat_ref[:, 2 * LANES : 3 * LANES]
    y_f = gated_ref[:, 0:LANES]
    y_r = gated_ref[:, LANES:]
    for i in range(columns):
        cols = slice(i * BLOCK, (i + 1) * BLOCK)
        back = slice((columns - 1 - i) * BLOCK, (columns - i) * BLOCK)
        turned = dot(h_ref[:, back], flip).astype(bf16)
        grad = dot_tn(g_f, h_ref[:, cols]) + dot_tn(g_r, turned)
        dwin_ref[cols, :] = jnp.transpose(grad * scaling)
        turned = dot(d_ref[:, back], flip).astype(bf16)
        grad = dot_tn(y_f, d_ref[:, cols]) + dot_tn(y_r, turned)
        dwout_ref[:, cols] = grad[:head] * scaling


def last_kernel(n_got, n_pieces, layout, scaling, *refs):
    ids_ref, own_ref = refs[:2]
    got_refs = refs[2 : 2 + n_got]
    pieces = refs[2 + n_got : 2 + n_got + n_pieces]
    refs = refs[2 + n_got + n_pieces :]
    dhid_ref, dwbct_ref = refs[:2]
    if layout[2] is None:
        h_ref = pieces[0]
    else:
        h_ref = refs[2]
        assemble(ids_ref, pieces, h_ref, None, layout)
    flip = mirror(BLOCK)
    length, width = h_ref.shape
    own_rows = layout[1]
    groups = width // length
    extra = 4 * STATE // groups
    total = own_ref[extra : extra + own_rows, :]
    for got in got_refs:
        total += got[extra : extra + own_rows, :].astype(f32)
    dhid_ref[...] = total.astype(bf16)
    sums = [own_ref[:extra, :].astype(bf16).astype(f32)]
    sums += [got[:extra, :].astype(f32) for got in got_refs]
    while len(sums) > 1:
        sums = [a + b for a, b in zip(sums[0::2], sums[1::2])]
    shared = sums[0].astype(bf16)
    shared = jnp.concatenate(
        [shared[:, i * length : (i + 1) * length] for i in range(groups)], axis=0
    )
    fwd = shared[: 2 * STATE]
    rev = turn_columns(shared[2 * STATE :], flip).astype(bf16)
    pairs = dot(jnp.concatenate([fwd, rev], axis=0), h_ref[...])
    turned = exact(split(pairs[2 * STATE :], 3), lambda part: turn_columns(part, flip))
    dwbct_ref[...] = (pairs[: 2 * STATE] + turned) * scaling


def spec(memory=pltpu.VMEM):
    return pl.BlockSpec(memory_space=memory)


def call(kernel, inputs, n_smem, outs, scratch, flops, moved):
    return pl.pallas_call(
        kernel,
        out_shape=outs,
        in_specs=[spec(pltpu.SMEM)] * n_smem + [spec()] * (len(inputs) - n_smem),
        out_specs=jax.tree.map(lambda _: spec(), outs),
        scratch_shapes=scratch,
        compiler_params=pltpu.CompilerParams(vmem_limit_bytes=VMEM_LIMIT),
        cost_estimate=pl.CostEstimate(flops=flops, bytes_accessed=moved, transcendentals=0),
    )(*inputs)


def shape(dims, dtype):
    return jax.ShapeDtypeStruct(dims, dtype)


def local(ctx_size, tp_size, hidden, w_in, w_bc, w_dt, dt_bias, a_log, d_skip, conv_w, w_out, d_out):
    own_rows, width = hidden.shape
    length = own_rows * tp_size * ctx_size
    head = w_out.shape[0]
    nz = tp_size // 4
    chunks = length // BLOCK
    t = lax.axis_index("tp")
    ids = jnp.stack([t >> 2, (t >> 1) & 1, t & 1, lax.axis_index("ctx")]).astype(jnp.int32)
    params = [dt_bias, a_log, d_skip]
    wall, wallt, gall, taps = call(
        prep_kernel,
        [w_in, w_bc.T, w_dt, w_out, conv_w],
        0,
        (
            shape((width, 4 * LANES), bf16),
            shape((4 * LANES, width), bf16),
            shape((width, 2 * LANES), bf16),
            shape((CONV, LANES), f32),
        ),
        [],
        6 * width * BLOCK * BLOCK,
        20 * width * LANES,
    )

    def across(value, flip_bits):
        return lax.ppermute(value, "tp", [(i, i ^ flip_bits) for i in range(tp_size)])

    def along(value, offset):
        return lax.ppermute(
            value, "ctx", [((i + offset) % ctx_size, i) for i in range(ctx_size)]
        )

    def pack(parts):
        rows = sum(part.shape[0] for part in parts)
        return pl.pallas_call(
            pack_kernel,
            out_shape=shape((rows, width), bf16),
            in_specs=[spec()] * len(parts) + [spec(pl.ANY)],
            out_specs=spec(),
        )(*parts, taps)

    def column(own, count):
        if count == 1:
            return [own]
        half = count // 2
        return column(own, half) + column(across(own, 4 * half), half)

    if own_rows % TILE_ROWS == 0:
        zs = column(jnp.concatenate([hidden, d_out], axis=0), nz)
        coords, pieces = [], []
        for g, blocks in enumerate([range(0, nz // 2), range(nz // 2, nz)]):
            parts = [zs[j] for j in blocks]
            chunk = pack(parts) if g else jnp.concatenate(parts, axis=0)
            beside = across(chunk, 2)
            plane = [((0, 0), chunk), ((0, 1), beside)]
            for dc in range(1, ctx_size):
                ahead = along(chunk, dc)
                diagonal = along(beside, dc) if g else across(ahead, 2)
                plane += [((dc, 0), ahead), ((dc, 1), diagonal)]
            for (dc, dx), piece in plane:
                coords += [(dc, dx, 0, tuple(blocks)), (dc, dx, 1, tuple(blocks))]
                pieces += [piece, across(piece, 1)]
        layout = (tp_size, own_rows, tuple(coords))
        rows = [pltpu.VMEM((length, width), bf16)]
    else:
        pieces = [lax.all_gather(a, ("ctx", "tp"), axis=0, tiled=True) for a in (hidden, d_out)]
        layout, rows = (tp_size, own_rows, None), []
    h_pieces = pieces if rows else pieces[:1]
    n_pieces = len(pieces)
    extra = 4 * STATE * length // width
    half = tp_size * own_rows // 2
    send, keep, gcat, gated = call(
        functools.partial(core_kernel, n_pieces, layout),
        [ids, *params, *pieces, wall, wallt, gall, taps],
        4,
        (
            shape((extra + half, width), bf16),
            shape((extra + half, width), f32),
            shape((length, 4 * LANES), bf16),
            shape((length, 2 * LANES), bf16),
        ),
        rows * 2,
        8 * length * width * BLOCK,
        8 * length * width,
    )
    scaling = 1.0 / math.sqrt(length)
    got = across(send, 1)
    d_w_in, d_w_out = call(
        functools.partial(weight_kernel, n_pieces, layout, scaling),
        [ids, *pieces, gcat, gated],
        1,
        (
            shape((width, LANES), f32),
            shape((head, width), f32),
        ),
        rows * 2,
        8 * length * width * BLOCK,
        8 * length * width,
    )
    quarter = half // 2
    summed = keep + got.astype(f32)
    send = summed[: extra + quarter].astype(bf16)
    keep = jnp.concatenate(
        [summed[:extra].astype(bf16).astype(f32), summed[extra + quarter :]], axis=0
    )
    summed = keep + across(send, 2).astype(f32)
    got = []
    for j in range(1, nz):
        at = extra + j * own_rows
        piece = jnp.concatenate([summed[:extra], summed[at : at + own_rows]], axis=0)
        got.append(across(piece.astype(bf16), 4 * j))
    d_hidden, d_w_bc = call(
        functools.partial(last_kernel, len(got), len(h_pieces), layout, scaling),
        [ids, summed[: extra + own_rows], *got, *h_pieces],
        1,
        (shape((own_rows, width), bf16), shape((2 * STATE, width), f32)),
        rows,
        2 * length * width * LANES,
        4 * length * width,
    )
    return (d_hidden, d_w_in, d_w_out, d_w_bc.T)


def solution(mesh):
    in_specs = (
        P(("ctx", "tp"), None),
        P(None, "tp"),
        P(),
        P("tp", None),
        P("tp"),
        P("tp"),
        P("tp"),
        P(None, "tp"),
        P("tp", None),
        P(("ctx", "tp"), None),
    )
    out_specs = (P(("ctx", "tp"), None), P(None, "tp"), P("tp", None), P())
    body = functools.partial(local, mesh.shape["ctx"], mesh.shape["tp"])
    return jax.shard_map(body, mesh=mesh, in_specs=in_specs, out_specs=out_specs, check_vma=False)
```

```python
import functools
import math

import jax
import jax.numpy as jnp
from jax import lax
from jax.experimental import pallas as pl
from jax.experimental.pallas import tpu as pltpu
from jax.sharding import PartitionSpec as P

STATE = 16
CONV = 4
LANES = 128
BLOCK = 256
TILE_ROWS = 16
f32 = jnp.float32
bf16 = jnp.bfloat16


def dot(a, b):
    return jnp.dot(a, b, preferred_element_type=f32)


def dot_nt(a, b):
    return lax.dot_general(a, b, (((1,), (1,)), ((), ())), preferred_element_type=f32)


def dot_tn(a, b):
    return lax.dot_general(a, b, (((0,), (0,)), ((), ())), preferred_element_type=f32)


def iota(shape, dim):
    return lax.broadcasted_iota(jnp.int32, shape, dim)


def mirror(size):
    return jnp.where(iota((size, size), 0) + iota((size, size), 1) == size - 1, 1.0, 0.0).astype(
        bf16
    )


def split(value, terms):
    parts = []
    for _ in range(terms):
        part = value.astype(bf16)
        parts.append(part)
        value = value - part.astype(f32)
    return parts


def flip_rows(value, flip):
    count = value.shape[0] // BLOCK
    return jnp.concatenate(
        [dot(flip, value[(count - 1 - i) * BLOCK : (count - i) * BLOCK]) for i in range(count)],
        axis=0,
    )


def owners(ids_ref, layout):
    tp_size, own_rows, coords = layout
    z, x, core, ctx = (ids_ref[i] for i in range(4))
    ctx_size = max(c[0] for c in coords) + 1
    for p, (dc, dx, dcore, blocks) in enumerate(coords):
        from_ctx = lax.rem(ctx + dc, ctx_size)
        for k, j in enumerate(blocks):
            owner = ((z ^ j) * 2 + (x ^ dx)) * 2 + (core ^ dcore)
            at = pl.multiple_of((from_ctx * tp_size + owner) * own_rows, own_rows)
            yield p, k, at


def assemble(ids_ref, pieces, h_ref, d_ref, layout):
    own_rows = layout[1]
    for p, k, at in owners(ids_ref, layout):
        piece = pieces[p]
        half = piece.shape[0] // 2
        h_rows = slice(k * own_rows, (k + 1) * own_rows)
        d_rows = slice(half + k * own_rows, half + (k + 1) * own_rows)
        h_ref[pl.ds(at, own_rows), :] = piece[h_rows, :]
        d_ref[pl.ds(at, own_rows), :] = piece[d_rows, :]


def project(pieces, wall_ref, gall_ref):
    half = pieces[0].shape[0] // 2
    h = jnp.concatenate([piece[:half, :] for piece in pieces], axis=0)
    d = jnp.concatenate([piece[half:, :] for piece in pieces], axis=0)
    return dot(h, wall_ref[...]), dot(d, gall_ref[...])


def pack_kernel(n_parts, own_rows, *refs):
    parts, out_ref = refs[:n_parts], refs[-1]
    half = n_parts * own_rows
    for k, ref in enumerate(parts):
        out_ref[k * own_rows : (k + 1) * own_rows, :] = ref[:own_rows, :]
        if ref.shape[0] > own_rows:
            rows = slice(half + k * own_rows, half + (k + 1) * own_rows)
            out_ref[rows, :] = ref[own_rows:, :]


def early_kernel(*refs):
    pieces = refs[:-4]
    wall_ref, gall_ref, proj_ref, grad_ref = refs[-4:]
    proj_ref[...], grad_ref[...] = project(pieces, wall_ref, gall_ref)


def turn_columns(value, flip):
    count = value.shape[1] // BLOCK
    return jnp.concatenate(
        [dot(value[:, (count - 1 - i) * BLOCK : (count - i) * BLOCK], flip) for i in range(count)],
        axis=1,
    )


def prep_kernel(ids_ref, win_ref, wbct_ref, wdt_ref, wout_ref, conv_ref, *refs):
    wall_ref, wallt_ref, gall_ref, taps_ref = refs[-4:]
    flip = mirror(BLOCK)
    width = win_ref.shape[0]
    head = wout_ref.shape[0]
    count = width // BLOCK
    shared = 2 * STATE + 1
    for i in range(count):
        cols = slice(i * BLOCK, (i + 1) * BLOCK)
        rows = jnp.concatenate(
            [
                wbct_ref[:, cols].astype(f32),
                wdt_ref[:, cols].astype(f32),
                jnp.zeros((LANES - shared, BLOCK), f32),
            ],
            axis=0,
        )
        block = win_ref[cols, :]
        wall_ref[cols, :LANES] = block
        wall_ref[cols, LANES : 2 * LANES] = jnp.transpose(rows).astype(bf16)
        wallt_ref[:LANES, cols] = jnp.transpose(block.astype(f32)).astype(bf16)
        wallt_ref[LANES : 2 * LANES, cols] = rows.astype(bf16)
        out = jnp.concatenate(
            [wout_ref[:, cols].astype(f32), jnp.zeros((LANES - head, BLOCK), f32)], axis=0
        )
        gall_ref[cols, :LANES] = jnp.transpose(out).astype(bf16)
    for i in range(count):
        cols = slice(i * BLOCK, (i + 1) * BLOCK)
        back = slice((count - 1 - i) * BLOCK, (count - i) * BLOCK)
        wall_ref[cols, 2 * LANES :] = dot(flip, wall_ref[back, : 2 * LANES]).astype(bf16)
        gall_ref[cols, LANES:] = dot(flip, gall_ref[back, :LANES]).astype(bf16)
        wallt_ref[2 * LANES :, cols] = dot(wallt_ref[: 2 * LANES, back], flip).astype(bf16)
    tap = iota((CONV, LANES - head), 0)
    taps_ref[:, :head] = conv_ref[...]
    taps_ref[:, head:] = jnp.where(tap == CONV - 1, 1.0, 0.0)


def own_source(shape, dim, ids_ref, tp_size, own_rows):
    z, x, core, ctx = (ids_ref[i] for i in range(4))
    nz = tp_size // 4
    row = iota(shape, dim)
    block = row // own_rows
    j = block % nz
    dx = 1 - (block // nz) % 2
    dcore = 1 - block // (2 * nz)
    owner = ((z ^ j) * 2 + (x ^ dx)) * 2 + (core ^ dcore)
    return (ctx * tp_size + owner) * own_rows + row % own_rows


def exact(parts, apply):
    return sum(apply(part) for part in parts)


def decay_rate(par_refs):
    return -jnp.exp(jnp.full((1, LANES), par_refs[1][0], f32))


def core_kernel(n_pieces, layout, *refs):
    ids_ref, par_refs = refs[0], refs[1:4]
    pieces = refs[4 : 4 + n_pieces]
    early_refs = refs[4 + n_pieces : 6 + n_pieces]
    wall_ref, wallt_ref, gall_ref, taps_ref = refs[6 + n_pieces : 10 + n_pieces]
    send_ref, keep_ref, gcat_ref, gated_ref = refs[10 + n_pieces : 14 + n_pieces]
    tp_size, own_rows, coords = layout
    if coords is None:
        proj, grads = early_refs[0][...], early_refs[1][...]
    else:
        proj_ref, grad_ref = refs[14 + n_pieces :]
        halves = [[ref[...] for ref in early_refs], project(pieces, wall_ref, gall_ref)]
        for p, k, at in owners(ids_ref, layout):
            blocks = len(coords[p][3])
            source = halves[p // n_pieces]
            first = ((p % n_pieces) * blocks + k) * own_rows
            proj_ref[pl.ds(at, own_rows), :] = source[0][first : first + own_rows]
            grad_ref[pl.ds(at, own_rows), :] = source[1][first : first + own_rows]
        proj, grads = proj_ref[...], grad_ref[...]
    length, width = proj.shape[0], wall_ref.shape[0]
    chunks = length // BLOCK
    flip = mirror(BLOCK)
    bias, rate, skip = par_refs[0][0], decay_rate(par_refs), par_refs[2][0]
    lane = iota((1, LANES), 1)
    low = lane < LANES // 2
    causal = iota((BLOCK, BLOCK), 0) >= iota((BLOCK, BLOCK), 1)
    tri = jnp.where(causal, 1.0, 0.0).astype(bf16)
    row_at = iota((length, LANES), 0)

    turned = [proj[:, 2 * LANES : 3 * LANES].astype(bf16)]
    turned += split(proj[:, 3 * LANES :], 3) + split(grads[:, LANES:], 2)
    turned = flip_rows(jnp.concatenate(turned, axis=1), flip)
    turned = [turned[:, i * LANES : (i + 1) * LANES] for i in range(6)]
    strands = (
        (
            proj[:, :LANES].astype(bf16).astype(f32),
            proj[:, LANES : 2 * LANES],
            grads[:, :LANES],
        ),
        (turned[0], turned[1] + turned[2] + turned[3], turned[4] + turned[5]),
    )

    def gates(xz, rest, grad_g):
        pre = taps_ref[CONV - 1 : CONV, :] * xz
        for shift in range(1, CONV):
            moved = jnp.where(row_at >= shift, pltpu.roll(xz, shift, 0), 0.0)
            pre += taps_ref[CONV - 1 - shift : CONV - shift, :] * moved
        sig = jax.nn.sigmoid(pre)
        u = pre * sig
        slope = sig * (1.0 + pre * (1.0 - sig))
        u_other = pltpu.roll(u, LANES // 2, 1)
        raw = jnp.broadcast_to(rest[:, 2 * STATE : 2 * STATE + 1], (length, LANES)) + bias
        dt = jnp.maximum(raw, 0.0) + jnp.log1p(jnp.exp(-jnp.abs(raw)))
        b_all = jnp.where(lane < STATE, rest, 0.0)
        c_all = jnp.where(lane < STATE, pltpu.roll(rest, LANES - STATE, 1), 0.0)
        g_y = jnp.where(low, grad_g * u_other, 0.0)
        return u, slope, u_other, dt, jax.nn.sigmoid(raw), b_all, c_all, dt * u, g_y, grad_g

    def enter_chunk(c, gate, state):
        rows = slice(c * BLOCK, (c + 1) * BLOCK)
        dt, b_all, c_all, w_all = gate[3][rows], gate[5][rows], gate[6][rows], gate[7][rows]
        log_keep = dot(tri, jnp.concatenate(split(dt * rate, 3), axis=1))
        log_keep = log_keep[:, :LANES] + log_keep[:, LANES : 2 * LANES] + log_keep[:, 2 * LANES :]
        across = jnp.transpose(log_keep)[0:1, :]
        gap = jnp.concatenate([log_keep] * (BLOCK // LANES), axis=1) - across
        decay = jnp.exp(jnp.where(causal, gap, -jnp.inf))
        b_low, c_low, w_low = b_all.astype(bf16), c_all.astype(bf16), w_all.astype(bf16)
        mixed = (dot_nt(c_low, b_low) * decay).astype(bf16)
        last = log_keep[BLOCK - 1 : BLOCK, :]
        enter = jnp.exp(log_keep)
        leave = jnp.exp(last - log_keep)
        b_left = (leave * b_all).astype(bf16)
        out = dot(mixed, w_low) + enter * dot(c_low, state.astype(bf16))
        after = jnp.exp(last) * state + dot_tn(b_left, w_low)
        return out, decay, mixed, b_low, c_low, w_low, b_left, enter, leave, last, state, after

    def leave_chunk(c, gate, saved, d_state):
        rows = slice(c * BLOCK, (c + 1) * BLOCK)
        u, c_all, w_all, gy = gate[0][rows], gate[6][rows], gate[7][rows], gate[8][rows]
        out, decay, mixed, b_low, c_low, w_low, b_left, enter, leave, last, before, after = saved
        gy_low = gy.astype(bf16)
        ds_low = d_state.astype(bf16)
        dw = dot_tn(mixed, gy_low) + dot(b_left, ds_low)
        d_scores = (dot_nt(gy_low, w_low) * decay).astype(bf16)
        g_c = dot(d_scores, b_low) + enter * dot_nt(gy_low, before.astype(bf16))
        g_b = dot_tn(d_scores, c_low) + leave * dot_nt(w_low, ds_low)
        d_log = jnp.sum(jnp.where(low, gy * out - w_all * dw, 0.0), axis=1, keepdims=True)
        at_end = jnp.sum(jnp.where(low, after * d_state, 0.0))
        d_log = jnp.broadcast_to(d_log, (BLOCK, LANES))
        d_sum = dot_tn(tri, jnp.concatenate(split(d_log, 2), axis=1))
        d_sum = d_sum[:, :LANES] + d_sum[:, LANES:] + at_end
        g_a = rate * d_sum + jnp.sum(jnp.where(low, u * dw, 0.0), axis=1, keepdims=True)
        carried = (enter * c_all).astype(bf16)
        return dw, g_b, g_c, g_a, jnp.exp(last) * d_state + dot_tn(carried, gy_low)

    gate = [gates(*strand) for strand in strands]
    saved = [[], []]
    state = [jnp.zeros((LANES, LANES), f32)] * 2
    for c in range(chunks):
        for s in range(2):
            saved[s].append(enter_chunk(c, gate[s], state[s]))
            state[s] = saved[s][c][-1]
    state = [jnp.zeros((LANES, LANES), f32)] * 2
    grads = [[None] * chunks, [None] * chunks]
    for c in reversed(range(chunks)):
        for s in range(2):
            *grads[s][c], state[s] = leave_chunk(c, gate[s], saved[s][c], state[s])
    small = []
    for s in range(2):
        u, slope, u_other, dt, dt_slope, _, _, _, g_y, grad_g = gate[s]
        y = jnp.concatenate([part[0] for part in saved[s]], axis=0) + skip * u
        gated = jnp.where(low, y * u_other, 0.0).astype(bf16)
        g_gate = jnp.where(low, grad_g * y, 0.0)
        d_w, g_b, g_c, g_a = (
            jnp.concatenate([part[i] for part in grads[s]], axis=0) for i in range(4)
        )
        g_raw = g_a * dt_slope
        d_u = jnp.where(low, skip * g_y + dt * d_w, pltpu.roll(g_gate, LANES // 2, 1))
        d_pre = d_u * slope
        g_xz = taps_ref[CONV - 1 : CONV, :] * d_pre
        for shift in range(1, CONV):
            moved = jnp.where(
                row_at < length - shift, pltpu.roll(d_pre, length - shift, 0), 0.0
            )
            g_xz += taps_ref[CONV - 1 - shift : CONV - shift, :] * moved
        shared = jnp.where(lane < STATE, g_b, 0.0) + jnp.where(
            (lane >= STATE) & (lane < 2 * STATE), pltpu.roll(g_c, STATE, 1), 0.0
        )
        g_rest = shared + jnp.where(lane == 2 * STATE, g_raw, 0.0)
        result = jnp.concatenate([g_xz.astype(bf16), g_rest.astype(bf16), gated], axis=1)
        small.append(shared)
        if s == 1:
            result = flip_rows(result, flip).astype(bf16)
        gcat_ref[:, 2 * s * LANES : 2 * (s + 1) * LANES] = result[:, : 2 * LANES]
        gated_ref[:, s * LANES : (s + 1) * LANES] = result[:, 2 * LANES :]

    pair = small[0] + pltpu.roll(small[1], 2 * STATE, 1)
    shared_t = jnp.transpose(pair)[: 4 * STATE].astype(bf16)
    groups = width // length
    step = 4 * STATE // groups
    for i in range(groups):
        part = shared_t[i * step : (i + 1) * step, :]
        send_ref[0:step, i * length : (i + 1) * length] = part
        keep_ref[0:step, i * length : (i + 1) * length] = part.astype(f32)
    own = tp_size * own_rows
    source = own_source((own, length), 0, ids_ref, tp_size, own_rows)
    pick = jnp.where(source == iota((own, length), 1), 1.0, 0.0).astype(bf16)
    picked = dot(pick, gcat_ref[...]).astype(bf16)
    half = own // 2
    part = dot(picked, wallt_ref[...])
    send_ref[step:, :] = part[:half].astype(bf16)
    keep_ref[step:, :] = part[half:]


def weight_kernel(n_pieces, layout, scaling, *refs):
    ids_ref = refs[0]
    pieces = refs[1 : 1 + n_pieces]
    gcat_ref, gated_ref, _, dwin_ref, dwout_ref = refs[1 + n_pieces : 6 + n_pieces]
    if layout[2] is None:
        h_ref, d_ref = pieces
    else:
        h_ref, d_ref = refs[6 + n_pieces :]
        assemble(ids_ref, pieces, h_ref, d_ref, layout)
    flip = mirror(BLOCK)
    columns = h_ref.shape[1] // BLOCK
    head = dwout_ref.shape[0]
    g_f = gcat_ref[:, 0:LANES]
    g_r = gcat_ref[:, 2 * LANES : 3 * LANES]
    y_f = gated_ref[:, 0:LANES]
    y_r = gated_ref[:, LANES:]
    for i in range(columns):
        cols = slice(i * BLOCK, (i + 1) * BLOCK)
        back = slice((columns - 1 - i) * BLOCK, (columns - i) * BLOCK)
        turned = dot(h_ref[:, back], flip).astype(bf16)
        grad = dot_tn(g_f, h_ref[:, cols]) + dot_tn(g_r, turned)
        dwin_ref[cols, :] = jnp.transpose(grad * scaling)
        turned = dot(d_ref[:, back], flip).astype(bf16)
        grad = dot_tn(y_f, d_ref[:, cols]) + dot_tn(y_r, turned)
        dwout_ref[:, cols] = grad[:head] * scaling


def stage_kernel(extra, own_rows, keep_ref, got_ref, _, own_ref, *piece_refs):
    shared = keep_ref[:extra, :] + got_ref[:extra, :].astype(f32)
    own_ref[:extra, :] = shared
    for j, ref in enumerate([own_ref, *piece_refs]):
        rows = slice(extra + j * own_rows, extra + (j + 1) * own_rows)
        value = keep_ref[rows, :] + got_ref[rows, :].astype(f32)
        ref[extra:, :] = value.astype(ref.dtype)
        if j:
            ref[:extra, :] = shared.astype(bf16)


def last_kernel(own_rows, scaling, own_ref, h_ref, *refs):
    got_refs, (dhid_ref, dwbct_ref) = refs[:-2], refs[-2:]
    flip = mirror(BLOCK)
    length, width = h_ref.shape
    groups = width // length
    extra = 4 * STATE // groups
    total = own_ref[extra : extra + own_rows, :]
    for got in got_refs:
        total += got[extra : extra + own_rows, :].astype(f32)
    dhid_ref[...] = total.astype(bf16)
    sums = [own_ref[:extra, :].astype(bf16).astype(f32)]
    sums += [got[:extra, :].astype(f32) for got in got_refs]
    while len(sums) > 1:
        sums = [a + b for a, b in zip(sums[0::2], sums[1::2])]
    shared = sums[0].astype(bf16)
    shared = jnp.concatenate(
        [shared[:, i * length : (i + 1) * length] for i in range(groups)], axis=0
    )
    fwd = shared[: 2 * STATE]
    rev = turn_columns(shared[2 * STATE :], flip).astype(bf16)
    pairs = dot(jnp.concatenate([fwd, rev], axis=0), h_ref[...])
    turned = exact(split(pairs[2 * STATE :], 3), lambda part: turn_columns(part, flip))
    dwbct_ref[...] = (pairs[: 2 * STATE] + turned) * scaling


def spec(memory=pltpu.VMEM):
    return pl.BlockSpec(memory_space=memory)


def call(kernel, inputs, n_smem, outs, scratch, flops, moved, unread=0, vmem=32):
    return pl.pallas_call(
        kernel,
        out_shape=outs,
        in_specs=[spec(pltpu.SMEM)] * n_smem
        + [spec()] * (len(inputs) - n_smem - unread)
        + [spec(pl.ANY)] * unread,
        out_specs=jax.tree.map(lambda _: spec(), outs),
        scratch_shapes=scratch,
        compiler_params=pltpu.CompilerParams(vmem_limit_bytes=vmem * 1024 * 1024),
        cost_estimate=pl.CostEstimate(flops=flops, bytes_accessed=moved, transcendentals=0),
    )(*inputs)


def shape(dims, dtype):
    return jax.ShapeDtypeStruct(dims, dtype)


def local(ctx_size, tp_size, hidden, w_in, w_bc, w_dt, dt_bias, a_log, d_skip, conv_w, w_out, d_out):
    own_rows, width = hidden.shape
    length = own_rows * tp_size * ctx_size
    head = w_out.shape[0]
    nz = tp_size // 4
    chunks = length // BLOCK
    t = lax.axis_index("tp")
    ids = jnp.stack([t >> 2, (t >> 1) & 1, t & 1, lax.axis_index("ctx")]).astype(jnp.int32)
    params = [dt_bias, a_log, d_skip]
    def across(value, flip_bits):
        return lax.ppermute(value, "tp", [(i, i ^ flip_bits) for i in range(tp_size)])

    def along(value, offset):
        return lax.ppermute(
            value, "ctx", [((i + offset) % ctx_size, i) for i in range(ctx_size)]
        )

    def prepare(*begun):
        return call(
            prep_kernel,
            [ids, w_in, w_bc.T, w_dt, w_out, conv_w, *begun],
            1,
            (
                shape((width, 4 * LANES), bf16),
                shape((4 * LANES, width), bf16),
                shape((width, 2 * LANES), bf16),
                shape((CONV, LANES), f32),
            ),
            [],
            6 * width * BLOCK * BLOCK,
            20 * width * LANES,
            len(begun),
        )

    def pack(parts, rows, *after):
        return call(
            functools.partial(pack_kernel, len(parts), own_rows),
            [*parts, *after],
            0,
            shape((rows, width), bf16),
            [],
            0,
            4 * rows * width,
            len(after),
        )

    def column(own, count):
        if count == 1:
            return [own]
        half = count // 2
        return column(own, half) + column(across(own, 4 * half), half)

    if own_rows % TILE_ROWS == 0:
        zs = column(pack([hidden, d_out], 2 * own_rows), nz)
        coords, pieces = [], []
        for g, blocks in enumerate([range(0, nz // 2), range(nz // 2, nz)]):
            chunk = pack([zs[j] for j in blocks], nz * own_rows, *([taps] if g else []))
            if g == 0:
                wall, wallt, gall, taps = prepare(chunk, zs[nz // 2])
            beside = across(chunk, 2)
            plane = [((0, 0), chunk), ((0, 1), beside)]
            for dc in range(1, ctx_size):
                ahead = along(chunk, dc)
                diagonal = along(beside, dc) if g else across(ahead, 2)
                plane += [((dc, 0), ahead), ((dc, 1), diagonal)]
            for (dc, dx), piece in plane:
                coords += [(dc, dx, 0, tuple(blocks)), (dc, dx, 1, tuple(blocks))]
                pieces += [piece, across(piece, 1)]
        layout = (tp_size, own_rows, tuple(coords))
        early, late = pieces[: len(pieces) // 2], pieces[len(pieces) // 2 :]
    else:
        pieces = [lax.all_gather(a, ("ctx", "tp"), axis=0, tiled=True) for a in (hidden, d_out)]
        layout = (tp_size, own_rows, None)
        wall, wallt, gall, taps = prepare()
        early, late = [jnp.concatenate(pieces, axis=0)], []
    ordered = layout[2] is None
    vmem = 60 if ordered else 32
    early_rows = sum(piece.shape[0] for piece in early) // 2
    early = call(
        early_kernel,
        [*early, wall, gall],
        0,
        (shape((early_rows, 4 * LANES), f32), shape((early_rows, 2 * LANES), f32)),
        [],
        2 * early_rows * width * 6 * LANES,
        4 * early_rows * width,
        vmem=vmem,
    )
    extra = 4 * STATE * length // width
    half = tp_size * own_rows // 2
    send, keep, gcat, gated = call(
        functools.partial(core_kernel, len(late), layout),
        [ids, *params, *late, *early, wall, wallt, gall, taps],
        4,
        (
            shape((extra + half, width), bf16),
            shape((extra + half, width), f32),
            shape((length, 4 * LANES), bf16),
            shape((length, 2 * LANES), bf16),
        ),
        []
        if ordered
        else [pltpu.VMEM((length, 4 * LANES), f32), pltpu.VMEM((length, 2 * LANES), f32)],
        8 * length * width * BLOCK,
        8 * length * width,
        vmem=vmem,
    )
    scaling = 1.0 / math.sqrt(length)
    got = across(send, 1)
    quarter = half // 2
    summed = keep + got.astype(f32)
    send = summed[: extra + quarter].astype(bf16)
    keep = jnp.concatenate(
        [summed[:extra].astype(bf16).astype(f32), summed[extra + quarter :]], axis=0
    )
    got = across(send, 2)
    outs = (shape((width, LANES), f32), shape((head, width), f32))
    if not ordered:
        outs += (shape((length, width), bf16),)
    d_w_in, d_w_out, *in_order = call(
        functools.partial(weight_kernel, len(pieces), layout, scaling),
        [ids, *pieces, gcat, gated, send],
        1,
        outs,
        [] if ordered else [pltpu.VMEM((length, width), bf16)],
        8 * length * width * BLOCK,
        8 * length * width,
        1,
        vmem=vmem,
    )
    in_order = in_order[0] if in_order else pieces[0]
    own, *send = call(
        functools.partial(stage_kernel, extra, own_rows),
        [keep, got, d_w_out],
        0,
        (shape((extra + own_rows, width), f32),)
        + (shape((extra + own_rows, width), bf16),) * (nz - 1),
        [],
        4 * quarter * width,
        10 * quarter * width,
        1,
    )
    got = [across(piece, 4 * (j + 1)) for j, piece in enumerate(send)]
    d_hidden, d_w_bc = call(
        functools.partial(last_kernel, own_rows, scaling),
        [own, in_order, *got],
        0,
        (shape((own_rows, width), bf16), shape((2 * STATE, width), f32)),
        [],
        2 * length * width * LANES,
        4 * length * width,
    )
    return (d_hidden, d_w_in, d_w_out, d_w_bc.T)


def solution(mesh):
    in_specs = (
        P(("ctx", "tp"), None),
        P(None, "tp"),
        P(),
        P("tp", None),
        P("tp"),
        P("tp"),
        P("tp"),
        P(None, "tp"),
        P("tp", None),
        P(("ctx", "tp"), None),
    )
    out_specs = (P(("ctx", "tp"), None), P(None, "tp"), P("tp", None), P())
    body = functools.partial(local, mesh.shape["ctx"], mesh.shape["tp"])
    return jax.shard_map(body, mesh=mesh, in_specs=in_specs, out_specs=out_specs, check_vma=False)
```

```python
import functools
import math

import jax
import jax.numpy as jnp
from jax import lax
from jax.experimental import pallas as pl
from jax.experimental.pallas import tpu as pltpu
from jax.sharding import PartitionSpec as P

STATE = 16
CONV = 4
LANES = 128
BLOCK = 256
TILE_ROWS = 16
f32 = jnp.float32
bf16 = jnp.bfloat16


def dot(a, b):
    return jnp.dot(a, b, preferred_element_type=f32)


def dot_nt(a, b):
    return lax.dot_general(a, b, (((1,), (1,)), ((), ())), preferred_element_type=f32)


def dot_tn(a, b):
    return lax.dot_general(a, b, (((0,), (0,)), ((), ())), preferred_element_type=f32)


def iota(shape, dim):
    return lax.broadcasted_iota(jnp.int32, shape, dim)


def mirror(size):
    return jnp.where(iota((size, size), 0) + iota((size, size), 1) == size - 1, 1.0, 0.0).astype(
        bf16
    )


def split(value, terms):
    parts = []
    for _ in range(terms):
        part = value.astype(bf16)
        parts.append(part)
        value = value - part.astype(f32)
    return parts


def flip_rows(value, flip):
    count = value.shape[0] // BLOCK
    return jnp.concatenate(
        [dot(flip, value[(count - 1 - i) * BLOCK : (count - i) * BLOCK]) for i in range(count)],
        axis=0,
    )


def owners(ids_ref, layout):
    tp_size, own_rows, coords = layout
    z, x, core, ctx = (ids_ref[i] for i in range(4))
    ctx_size = max(c[0] for c in coords) + 1
    for p, (dc, dx, dcore, blocks) in enumerate(coords):
        from_ctx = lax.rem(ctx + dc, ctx_size)
        for k, j in enumerate(blocks):
            owner = ((z ^ j) * 2 + (x ^ dx)) * 2 + (core ^ dcore)
            at = pl.multiple_of((from_ctx * tp_size + owner) * own_rows, own_rows)
            yield p, k, at


def assemble(ids_ref, pieces, h_ref, d_ref, layout):
    own_rows = layout[1]
    for p, k, at in owners(ids_ref, layout):
        piece = pieces[p]
        half = piece.shape[0] // 2
        h_rows = slice(k * own_rows, (k + 1) * own_rows)
        d_rows = slice(half + k * own_rows, half + (k + 1) * own_rows)
        h_ref[pl.ds(at, own_rows), :] = piece[h_rows, :]
        d_ref[pl.ds(at, own_rows), :] = piece[d_rows, :]


def project(pieces, wall_ref, gall_ref):
    half = pieces[0].shape[0] // 2
    h = jnp.concatenate([piece[:half, :] for piece in pieces], axis=0)
    d = jnp.concatenate([piece[half:, :] for piece in pieces], axis=0)
    return dot(h, wall_ref[...]), dot(d, gall_ref[...])


def pack_kernel(n_parts, own_rows, *refs):
    parts, out_ref = refs[:n_parts], refs[-1]
    half = n_parts * own_rows
    for k, ref in enumerate(parts):
        out_ref[k * own_rows : (k + 1) * own_rows, :] = ref[:own_rows, :]
        if ref.shape[0] > own_rows:
            rows = slice(half + k * own_rows, half + (k + 1) * own_rows)
            out_ref[rows, :] = ref[own_rows:, :]


def first_kernel(hidden_ref, dout_ref, out_ref, sem):
    rows = hidden_ref.shape[0]
    fetch([hidden_ref, dout_ref], [out_ref.at[:rows], out_ref.at[rows:]], sem)


def copy_kernel(value_ref, _, out_ref):
    out_ref[...] = value_ref[...]


def early_kernel(*refs):
    pieces = refs[:-4]
    wall_ref, gall_ref, proj_ref, grad_ref = refs[-4:]
    proj_ref[...], grad_ref[...] = project(pieces, wall_ref, gall_ref)


def turn_columns(value, flip):
    count = value.shape[1] // BLOCK
    return jnp.concatenate(
        [dot(value[:, (count - 1 - i) * BLOCK : (count - i) * BLOCK], flip) for i in range(count)],
        axis=1,
    )


def fetch(sources, targets, sem):
    copies = [
        pltpu.make_async_copy(source, target, sem.at[i])
        for i, (source, target) in enumerate(zip(sources, targets))
    ]
    for copy in copies:
        copy.start()
    for copy in copies:
        copy.wait()


def prep_kernel(ids_ref, *refs):
    win_ref, wbct_ref, wdt_ref, wout_ref, conv_ref = refs[:5]
    wall_ref, wallt_ref, gall_ref, taps_ref = refs[-4:]
    flip = mirror(BLOCK)
    width = win_ref.shape[0]
    head = wout_ref.shape[0]
    count = width // BLOCK
    shared = 2 * STATE + 1
    for i in range(count):
        cols = slice(i * BLOCK, (i + 1) * BLOCK)
        rows = jnp.concatenate(
            [
                wbct_ref[:, cols].astype(f32),
                wdt_ref[:, cols].astype(f32),
                jnp.zeros((LANES - shared, BLOCK), f32),
            ],
            axis=0,
        )
        block = win_ref[cols, :]
        wall_ref[cols, :LANES] = block
        wall_ref[cols, LANES : 2 * LANES] = jnp.transpose(rows).astype(bf16)
        wallt_ref[:LANES, cols] = jnp.transpose(block.astype(f32)).astype(bf16)
        wallt_ref[LANES : 2 * LANES, cols] = rows.astype(bf16)
        out = jnp.concatenate(
            [wout_ref[:, cols].astype(f32), jnp.zeros((LANES - head, BLOCK), f32)], axis=0
        )
        gall_ref[cols, :LANES] = jnp.transpose(out).astype(bf16)
    for i in range(count):
        cols = slice(i * BLOCK, (i + 1) * BLOCK)
        back = slice((count - 1 - i) * BLOCK, (count - i) * BLOCK)
        wall_ref[cols, 2 * LANES :] = dot(flip, wall_ref[back, : 2 * LANES]).astype(bf16)
        gall_ref[cols, LANES:] = dot(flip, gall_ref[back, :LANES]).astype(bf16)
        wallt_ref[2 * LANES :, cols] = dot(wallt_ref[: 2 * LANES, back], flip).astype(bf16)
    tap = iota((CONV, LANES - head), 0)
    taps_ref[:, :head] = conv_ref[...]
    taps_ref[:, head:] = jnp.where(tap == CONV - 1, 1.0, 0.0)


def own_source(shape, dim, ids_ref, tp_size, own_rows):
    z, x, core, ctx = (ids_ref[i] for i in range(4))
    nz = tp_size // 4
    row = iota(shape, dim)
    block = row // own_rows
    j = block % nz
    dx = 1 - (block // nz) % 2
    dcore = 1 - block // (2 * nz)
    owner = ((z ^ j) * 2 + (x ^ dx)) * 2 + (core ^ dcore)
    return (ctx * tp_size + owner) * own_rows + row % own_rows


def exact(parts, apply):
    return sum(apply(part) for part in parts)


def decay_rate(par_refs):
    return -jnp.exp(jnp.full((1, LANES), par_refs[1][0], f32))


def core_kernel(n_pieces, layout, *refs):
    ids_ref, par_refs = refs[0], refs[1:4]
    pieces = refs[4 : 4 + n_pieces]
    early_refs = refs[4 + n_pieces : 6 + n_pieces]
    wall_ref, wallt_ref, gall_ref, taps_ref = refs[6 + n_pieces : 10 + n_pieces]
    send_ref, keep_ref, gcat_ref, gated_ref = refs[10 + n_pieces : 14 + n_pieces]
    tp_size, own_rows, coords = layout
    if coords is None:
        proj, grads = early_refs[0][...], early_refs[1][...]
    else:
        proj_ref, grad_ref = refs[14 + n_pieces :]
        halves = [[ref[...] for ref in early_refs], project(pieces, wall_ref, gall_ref)]
        for p, k, at in owners(ids_ref, layout):
            blocks = len(coords[p][3])
            source = halves[p // n_pieces]
            first = ((p % n_pieces) * blocks + k) * own_rows
            proj_ref[pl.ds(at, own_rows), :] = source[0][first : first + own_rows]
            grad_ref[pl.ds(at, own_rows), :] = source[1][first : first + own_rows]
        proj, grads = proj_ref[...], grad_ref[...]
    length, width = proj.shape[0], wall_ref.shape[0]
    chunks = length // BLOCK
    flip = mirror(BLOCK)
    bias, rate, skip = par_refs[0][0], decay_rate(par_refs), par_refs[2][0]
    lane = iota((1, LANES), 1)
    low = lane < LANES // 2
    causal = iota((BLOCK, BLOCK), 0) >= iota((BLOCK, BLOCK), 1)
    tri = jnp.where(causal, 1.0, 0.0).astype(bf16)
    row_at = iota((length, LANES), 0)

    turned = [proj[:, 2 * LANES : 3 * LANES].astype(bf16)]
    turned += split(proj[:, 3 * LANES :], 3) + split(grads[:, LANES:], 2)
    turned = flip_rows(jnp.concatenate(turned, axis=1), flip)
    turned = [turned[:, i * LANES : (i + 1) * LANES] for i in range(6)]
    strands = (
        (
            proj[:, :LANES].astype(bf16).astype(f32),
            proj[:, LANES : 2 * LANES],
            grads[:, :LANES],
        ),
        (turned[0], turned[1] + turned[2] + turned[3], turned[4] + turned[5]),
    )

    def gates(xz, rest, grad_g):
        pre = taps_ref[CONV - 1 : CONV, :] * xz
        for shift in range(1, CONV):
            moved = jnp.where(row_at >= shift, pltpu.roll(xz, shift, 0), 0.0)
            pre += taps_ref[CONV - 1 - shift : CONV - shift, :] * moved
        sig = jax.nn.sigmoid(pre)
        u = pre * sig
        slope = sig * (1.0 + pre * (1.0 - sig))
        u_other = pltpu.roll(u, LANES // 2, 1)
        raw = jnp.broadcast_to(rest[:, 2 * STATE : 2 * STATE + 1], (length, LANES)) + bias
        dt = jnp.maximum(raw, 0.0) + jnp.log1p(jnp.exp(-jnp.abs(raw)))
        b_all = jnp.where(lane < STATE, rest, 0.0)
        c_all = jnp.where(lane < STATE, pltpu.roll(rest, LANES - STATE, 1), 0.0)
        g_y = jnp.where(low, grad_g * u_other, 0.0)
        return u, slope, u_other, dt, jax.nn.sigmoid(raw), b_all, c_all, dt * u, g_y, grad_g

    def enter_chunk(c, gate, state):
        rows = slice(c * BLOCK, (c + 1) * BLOCK)
        dt, b_all, c_all, w_all = gate[3][rows], gate[5][rows], gate[6][rows], gate[7][rows]
        log_keep = dot(tri, jnp.concatenate(split(dt * rate, 3), axis=1))
        log_keep = log_keep[:, :LANES] + log_keep[:, LANES : 2 * LANES] + log_keep[:, 2 * LANES :]
        across = jnp.transpose(log_keep)[0:1, :]
        gap = jnp.concatenate([log_keep] * (BLOCK // LANES), axis=1) - across
        decay = jnp.exp(jnp.where(causal, gap, -jnp.inf))
        b_low, c_low, w_low = b_all.astype(bf16), c_all.astype(bf16), w_all.astype(bf16)
        mixed = (dot_nt(c_low, b_low) * decay).astype(bf16)
        last = log_keep[BLOCK - 1 : BLOCK, :]
        enter = jnp.exp(log_keep)
        leave = jnp.exp(last - log_keep)
        b_left = (leave * b_all).astype(bf16)
        out = dot(mixed, w_low) + enter * dot(c_low, state.astype(bf16))
        after = jnp.exp(last) * state + dot_tn(b_left, w_low)
        return out, decay, mixed, b_low, c_low, w_low, b_left, enter, leave, last, state, after

    def leave_chunk(c, gate, saved, d_state):
        rows = slice(c * BLOCK, (c + 1) * BLOCK)
        u, c_all, w_all, gy = gate[0][rows], gate[6][rows], gate[7][rows], gate[8][rows]
        out, decay, mixed, b_low, c_low, w_low, b_left, enter, leave, last, before, after = saved
        gy_low = gy.astype(bf16)
        ds_low = d_state.astype(bf16)
        dw = dot_tn(mixed, gy_low) + dot(b_left, ds_low)
        d_scores = (dot_nt(gy_low, w_low) * decay).astype(bf16)
        g_c = dot(d_scores, b_low) + enter * dot_nt(gy_low, before.astype(bf16))
        g_b = dot_tn(d_scores, c_low) + leave * dot_nt(w_low, ds_low)
        d_log = jnp.sum(jnp.where(low, gy * out - w_all * dw, 0.0), axis=1, keepdims=True)
        at_end = jnp.sum(jnp.where(low, after * d_state, 0.0))
        d_log = jnp.broadcast_to(d_log, (BLOCK, LANES))
        d_sum = dot_tn(tri, jnp.concatenate(split(d_log, 2), axis=1))
        d_sum = d_sum[:, :LANES] + d_sum[:, LANES:] + at_end
        g_a = rate * d_sum + jnp.sum(jnp.where(low, u * dw, 0.0), axis=1, keepdims=True)
        carried = (enter * c_all).astype(bf16)
        return dw, g_b, g_c, g_a, jnp.exp(last) * d_state + dot_tn(carried, gy_low)

    gate = [gates(*strand) for strand in strands]
    saved = [[], []]
    state = [jnp.zeros((LANES, LANES), f32)] * 2
    for c in range(chunks):
        for s in range(2):
            saved[s].append(enter_chunk(c, gate[s], state[s]))
            state[s] = saved[s][c][-1]
    state = [jnp.zeros((LANES, LANES), f32)] * 2
    grads = [[None] * chunks, [None] * chunks]
    for c in reversed(range(chunks)):
        for s in range(2):
            *grads[s][c], state[s] = leave_chunk(c, gate[s], saved[s][c], state[s])
    small = []
    for s in range(2):
        u, slope, u_other, dt, dt_slope, _, _, _, g_y, grad_g = gate[s]
        y = jnp.concatenate([part[0] for part in saved[s]], axis=0) + skip * u
        gated = jnp.where(low, y * u_other, 0.0).astype(bf16)
        g_gate = jnp.where(low, grad_g * y, 0.0)
        d_w, g_b, g_c, g_a = (
            jnp.concatenate([part[i] for part in grads[s]], axis=0) for i in range(4)
        )
        g_raw = g_a * dt_slope
        d_u = jnp.where(low, skip * g_y + dt * d_w, pltpu.roll(g_gate, LANES // 2, 1))
        d_pre = d_u * slope
        g_xz = taps_ref[CONV - 1 : CONV, :] * d_pre
        for shift in range(1, CONV):
            moved = jnp.where(
                row_at < length - shift, pltpu.roll(d_pre, length - shift, 0), 0.0
            )
            g_xz += taps_ref[CONV - 1 - shift : CONV - shift, :] * moved
        shared = jnp.where(lane < STATE, g_b, 0.0) + jnp.where(
            (lane >= STATE) & (lane < 2 * STATE), pltpu.roll(g_c, STATE, 1), 0.0
        )
        g_rest = shared + jnp.where(lane == 2 * STATE, g_raw, 0.0)
        result = jnp.concatenate([g_xz.astype(bf16), g_rest.astype(bf16), gated], axis=1)
        small.append(shared)
        if s == 1:
            result = flip_rows(result, flip).astype(bf16)
        gcat_ref[:, 2 * s * LANES : 2 * (s + 1) * LANES] = result[:, : 2 * LANES]
        gated_ref[:, s * LANES : (s + 1) * LANES] = result[:, 2 * LANES :]

    pair = small[0] + pltpu.roll(small[1], 2 * STATE, 1)
    shared_t = jnp.transpose(pair)[: 4 * STATE].astype(bf16)
    groups = width // length
    step = 4 * STATE // groups
    for i in range(groups):
        part = shared_t[i * step : (i + 1) * step, :]
        send_ref[0:step, i * length : (i + 1) * length] = part
        keep_ref[0:step, i * length : (i + 1) * length] = part.astype(f32)
    own = tp_size * own_rows
    source = own_source((own, length), 0, ids_ref, tp_size, own_rows)
    pick = jnp.where(source == iota((own, length), 1), 1.0, 0.0).astype(bf16)
    picked = dot(pick, gcat_ref[...]).astype(bf16)
    half = own // 2
    part = dot(picked, wallt_ref[...])
    send_ref[step:, :] = part[:half].astype(bf16)
    keep_ref[step:, :] = part[half:]


def weight_kernel(n_pieces, layout, scaling, *refs):
    ids_ref = refs[0]
    pieces = refs[1 : 1 + n_pieces]
    gcat_ref, gated_ref, _, dwin_ref, dwout_ref = refs[1 + n_pieces : 6 + n_pieces]
    if layout[2] is None:
        h_ref, d_ref = pieces
    else:
        h_ref, d_ref = refs[6 + n_pieces :]
        assemble(ids_ref, pieces, h_ref, d_ref, layout)
    flip = mirror(BLOCK)
    columns = h_ref.shape[1] // BLOCK
    head = dwout_ref.shape[0]
    g_f = gcat_ref[:, 0:LANES]
    g_r = gcat_ref[:, 2 * LANES : 3 * LANES]
    y_f = gated_ref[:, 0:LANES]
    y_r = gated_ref[:, LANES:]
    for i in range(columns):
        cols = slice(i * BLOCK, (i + 1) * BLOCK)
        back = slice((columns - 1 - i) * BLOCK, (columns - i) * BLOCK)
        turned = dot(h_ref[:, back], flip).astype(bf16)
        grad = dot_tn(g_f, h_ref[:, cols]) + dot_tn(g_r, turned)
        dwin_ref[cols, :] = jnp.transpose(grad * scaling)
        turned = dot(d_ref[:, back], flip).astype(bf16)
        grad = dot_tn(y_f, d_ref[:, cols]) + dot_tn(y_r, turned)
        dwout_ref[:, cols] = grad[:head] * scaling


def stage_kernel(own_rows, keep_ref, got_ref, _, own_ref, *piece_refs):
    for j, ref in enumerate([own_ref, *piece_refs]):
        rows = slice(j * own_rows, (j + 1) * own_rows)
        value = keep_ref[rows, :] + got_ref[rows, :].astype(f32)
        ref[...] = value.astype(ref.dtype)


def last_kernel(scaling, own_ref, h_ref, shared_ref, other_ref, *refs):
    got_refs, (dhid_ref, dwbct_ref) = refs[:-2], refs[-2:]
    flip = mirror(BLOCK)
    length, width = h_ref.shape
    groups = width // length
    total = own_ref[...]
    for got in got_refs:
        total += got[...].astype(f32)
    dhid_ref[...] = total.astype(bf16)
    shared = (shared_ref[...].astype(f32) + other_ref[...].astype(f32)).astype(bf16)
    shared = jnp.concatenate(
        [shared[:, i * length : (i + 1) * length] for i in range(groups)], axis=0
    )
    fwd = shared[: 2 * STATE]
    rev = turn_columns(shared[2 * STATE :], flip).astype(bf16)
    pairs = dot(jnp.concatenate([fwd, rev], axis=0), h_ref[...])
    turned = exact(split(pairs[2 * STATE :], 3), lambda part: turn_columns(part, flip))
    dwbct_ref[...] = (pairs[: 2 * STATE] + turned) * scaling


def spec(memory=pltpu.VMEM):
    return pl.BlockSpec(memory_space=memory)


def call(kernel, inputs, n_smem, outs, scratch, flops, moved, unread=0, vmem=32, far=False):
    return pl.pallas_call(
        kernel,
        out_shape=outs,
        in_specs=[spec(pltpu.SMEM)] * n_smem
        + [spec()] * (len(inputs) - n_smem - unread)
        + [spec(pltpu.HBM if far else pl.ANY)] * unread,
        out_specs=jax.tree.map(lambda _: spec(), outs),
        scratch_shapes=scratch,
        compiler_params=pltpu.CompilerParams(vmem_limit_bytes=vmem * 1024 * 1024),
        cost_estimate=pl.CostEstimate(flops=flops, bytes_accessed=moved, transcendentals=0),
    )(*inputs)


def shape(dims, dtype):
    return jax.ShapeDtypeStruct(dims, dtype)


def local(ctx_size, tp_size, hidden, w_in, w_bc, w_dt, dt_bias, a_log, d_skip, conv_w, w_out, d_out):
    own_rows, width = hidden.shape
    length = own_rows * tp_size * ctx_size
    head = w_out.shape[0]
    nz = tp_size // 4
    chunks = length // BLOCK
    t = lax.axis_index("tp")
    ids = jnp.stack([t >> 2, (t >> 1) & 1, t & 1, lax.axis_index("ctx")]).astype(jnp.int32)
    params = [dt_bias, a_log, d_skip]
    def across(value, flip_bits):
        return lax.ppermute(value, "tp", [(i, i ^ flip_bits) for i in range(tp_size)])

    def along(value, offset):
        return lax.ppermute(
            value, "ctx", [((i + offset) % ctx_size, i) for i in range(ctx_size)]
        )

    def prepare(*begun):
        return call(
            prep_kernel,
            [ids, w_in, w_bc.T, w_dt, w_out, conv_w, *begun],
            1,
            (
                shape((width, 4 * LANES), bf16),
                shape((4 * LANES, width), bf16),
                shape((width, 2 * LANES), bf16),
                shape((CONV, LANES), f32),
            ),
            [],
            6 * width * BLOCK * BLOCK,
            20 * width * LANES,
            len(begun),
        )

    def pack(parts, rows):
        return call(
            functools.partial(pack_kernel, len(parts), own_rows),
            parts,
            0,
            shape((rows, width), bf16),
            [],
            0,
            4 * rows * width,
        )

    def column(own, count):
        if count == 1:
            return [own]
        half = count // 2
        return column(own, half) + column(across(own, 4 * half), half)

    def after(value):
        return call(
            copy_kernel, [value, taps], 0, shape(value.shape, bf16), [], 0, 4 * value.size, 1
        )

    if own_rows % TILE_ROWS == 0:
        both = call(
            first_kernel,
            [hidden, d_out],
            0,
            shape((2 * own_rows, width), bf16),
            [pltpu.SemaphoreType.DMA((2,))],
            0,
            8 * own_rows * width,
            2,
            vmem=48,
            far=True,
        )
        zs = column(both, nz)
        coords, pieces, planes = [], [], []
        for g, blocks in enumerate([range(0, nz // 2), range(nz // 2, nz)]):
            chunk = pack([zs[j] for j in blocks], nz * own_rows)
            beside = across(chunk, 2)
            plane = [((0, 0), chunk), ((0, 1), beside)]
            for dc in range(1, ctx_size):
                ahead = along(chunk, dc)
                diagonal = along(beside, dc) if g else across(ahead, 2)
                plane += [((dc, 0), ahead), ((dc, 1), diagonal)]
            planes.append((tuple(blocks), plane))
        wall, wallt, gall, taps = prepare(chunk)
        for g, (blocks, plane) in enumerate(planes):
            for (dc, dx), piece in plane:
                coords += [(dc, dx, 0, blocks), (dc, dx, 1, blocks)]
                pieces += [piece, across(after(piece) if dc and dx and not g else piece, 1)]
        layout = (tp_size, own_rows, tuple(coords))
        early, late = pieces[: len(pieces) // 2], pieces[len(pieces) // 2 :]
    else:
        pieces = [lax.all_gather(a, ("ctx", "tp"), axis=0, tiled=True) for a in (hidden, d_out)]
        layout = (tp_size, own_rows, None)
        wall, wallt, gall, taps = prepare()
        early, late = [jnp.concatenate(pieces, axis=0)], []
    ordered = layout[2] is None
    vmem = 60 if ordered else 32
    early_rows = sum(piece.shape[0] for piece in early) // 2
    early = call(
        early_kernel,
        [*early, wall, gall],
        0,
        (shape((early_rows, 4 * LANES), f32), shape((early_rows, 2 * LANES), f32)),
        [],
        2 * early_rows * width * 6 * LANES,
        4 * early_rows * width,
        vmem=vmem,
    )
    extra = 4 * STATE * length // width
    half = tp_size * own_rows // 2
    send, keep, gcat, gated = call(
        functools.partial(core_kernel, len(late), layout),
        [ids, *params, *late, *early, wall, wallt, gall, taps],
        4,
        (
            shape((extra + half, width), bf16),
            shape((extra + half, width), f32),
            shape((length, 4 * LANES), bf16),
            shape((length, 2 * LANES), bf16),
        ),
        []
        if ordered
        else [pltpu.VMEM((length, 4 * LANES), f32), pltpu.VMEM((length, 2 * LANES), f32)],
        8 * length * width * BLOCK,
        8 * length * width,
        vmem=vmem,
    )
    scaling = 1.0 / math.sqrt(length)
    got = across(send, 1)
    quarter = half // 2
    summed = keep + got.astype(f32)
    shared = summed[:extra].astype(bf16)
    send = summed[extra : extra + quarter].astype(bf16)
    keep = summed[extra + quarter :]
    got = across(send, 2)
    step = nz // 2
    while step:
        shared = (shared.astype(f32) + across(shared, 4 * step).astype(f32)).astype(bf16)
        step //= 2
    outs = (shape((width, LANES), f32), shape((head, width), f32))
    if not ordered:
        outs += (shape((length, width), bf16),)
    d_w_in, d_w_out, *in_order = call(
        functools.partial(weight_kernel, len(pieces), layout, scaling),
        [ids, *pieces, gcat, gated, send],
        1,
        outs,
        [] if ordered else [pltpu.VMEM((length, width), bf16)],
        8 * length * width * BLOCK,
        8 * length * width,
        1,
        vmem=vmem,
    )
    in_order = in_order[0] if in_order else pieces[0]
    own, *send = call(
        functools.partial(stage_kernel, own_rows),
        [keep, got, d_w_out],
        0,
        (shape((own_rows, width), f32),) + (shape((own_rows, width), bf16),) * (nz - 1),
        [],
        4 * quarter * width,
        10 * quarter * width,
        1,
    )
    got = [across(piece, 4 * (j + 1)) for j, piece in enumerate(send)]
    d_hidden, d_w_bc = call(
        functools.partial(last_kernel, scaling),
        [own, in_order, shared, across(shared, 2), *got],
        0,
        (shape((own_rows, width), bf16), shape((2 * STATE, width), f32)),
        [],
        2 * length * width * LANES,
        4 * length * width,
    )
    return (d_hidden, d_w_in, d_w_out, d_w_bc.T)


def solution(mesh):
    in_specs = (
        P(("ctx", "tp"), None),
        P(None, "tp"),
        P(),
        P("tp", None),
        P("tp"),
        P("tp"),
        P("tp"),
        P(None, "tp"),
        P("tp", None),
        P(("ctx", "tp"), None),
    )
    out_specs = (P(("ctx", "tp"), None), P(None, "tp"), P("tp", None), P())
    body = functools.partial(local, mesh.shape["ctx"], mesh.shape["tp"])
    return jax.shard_map(body, mesh=mesh, in_specs=in_specs, out_specs=out_specs, check_vma=False)
```

```python
import functools
import math

import jax
import jax.numpy as jnp
from jax import lax
from jax.experimental import pallas as pl
from jax.experimental.pallas import tpu as pltpu
from jax.sharding import PartitionSpec as P

STATE = 16
CONV = 4
LANES = 128
BLOCK = 256
TILE_ROWS = 16
f32 = jnp.float32
bf16 = jnp.bfloat16


def dot(a, b):
    return jnp.dot(a, b, preferred_element_type=f32)


def dot_nt(a, b):
    return lax.dot_general(a, b, (((1,), (1,)), ((), ())), preferred_element_type=f32)


def dot_tn(a, b):
    return lax.dot_general(a, b, (((0,), (0,)), ((), ())), preferred_element_type=f32)


def iota(shape, dim):
    return lax.broadcasted_iota(jnp.int32, shape, dim)


def mirror(size):
    return jnp.where(iota((size, size), 0) + iota((size, size), 1) == size - 1, 1.0, 0.0).astype(
        bf16
    )


def split(value, terms):
    parts = []
    for _ in range(terms):
        part = value.astype(bf16)
        parts.append(part)
        value = value - part.astype(f32)
    return parts


def flip_rows(value, flip):
    count = value.shape[0] // BLOCK
    return jnp.concatenate(
        [dot(flip, value[(count - 1 - i) * BLOCK : (count - i) * BLOCK]) for i in range(count)],
        axis=0,
    )


def owners(ids_ref, layout):
    tp_size, own_rows, coords = layout
    z, x, core, ctx = (ids_ref[i] for i in range(4))
    ctx_size = max(c[0] for c in coords) + 1
    for p, (dc, dx, dcore, blocks) in enumerate(coords):
        from_ctx = lax.rem(ctx + dc, ctx_size)
        for k, j in enumerate(blocks):
            owner = ((z ^ j) * 2 + (x ^ dx)) * 2 + (core ^ dcore)
            at = pl.multiple_of((from_ctx * tp_size + owner) * own_rows, own_rows)
            yield p, k, at


def assemble(ids_ref, pieces, h_ref, d_ref, layout):
    own_rows = layout[1]
    for p, k, at in owners(ids_ref, layout):
        piece = pieces[p]
        half = piece.shape[0] // 2
        h_rows = slice(k * own_rows, (k + 1) * own_rows)
        d_rows = slice(half + k * own_rows, half + (k + 1) * own_rows)
        h_ref[pl.ds(at, own_rows), :] = piece[h_rows, :]
        d_ref[pl.ds(at, own_rows), :] = piece[d_rows, :]


def project(pieces, wall_ref, gall_ref):
    half = pieces[0].shape[0] // 2
    h = jnp.concatenate([piece[:half, :] for piece in pieces], axis=0)
    d = jnp.concatenate([piece[half:, :] for piece in pieces], axis=0)
    return dot(h, wall_ref[...]), dot(d, gall_ref[...])


def pack_kernel(n_parts, own_rows, *refs):
    parts, out_ref = refs[:n_parts], refs[-1]
    half = n_parts * own_rows
    for k, ref in enumerate(parts):
        out_ref[k * own_rows : (k + 1) * own_rows, :] = ref[:own_rows, :]
        if ref.shape[0] > own_rows:
            rows = slice(half + k * own_rows, half + (k + 1) * own_rows)
            out_ref[rows, :] = ref[own_rows:, :]


def copy_kernel(count, *refs):
    for value_ref, out_ref in zip(refs[:count], refs[len(refs) - count :]):
        out_ref[...] = value_ref[...]


def early_kernel(*refs):
    pieces = refs[:-4]
    wall_ref, gall_ref, proj_ref, grad_ref = refs[-4:]
    proj_ref[...], grad_ref[...] = project(pieces, wall_ref, gall_ref)


def turn_columns(value, flip):
    count = value.shape[1] // BLOCK
    return jnp.concatenate(
        [dot(value[:, (count - 1 - i) * BLOCK : (count - i) * BLOCK], flip) for i in range(count)],
        axis=1,
    )


def prep_kernel(ids_ref, *refs):
    win_ref, wbct_ref, wdt_ref, wout_ref, conv_ref = refs[:5]
    wall_ref, wallt_ref, gall_ref, taps_ref = refs[-4:]
    flip = mirror(BLOCK)
    width = win_ref.shape[0]
    head = wout_ref.shape[0]
    count = width // BLOCK
    shared = 2 * STATE + 1
    for i in range(count):
        cols = slice(i * BLOCK, (i + 1) * BLOCK)
        rows = jnp.concatenate(
            [
                wbct_ref[:, cols].astype(f32),
                wdt_ref[:, cols].astype(f32),
                jnp.zeros((LANES - shared, BLOCK), f32),
            ],
            axis=0,
        )
        block = win_ref[cols, :]
        wall_ref[cols, :LANES] = block
        wall_ref[cols, LANES : 2 * LANES] = jnp.transpose(rows).astype(bf16)
        wallt_ref[:LANES, cols] = jnp.transpose(block.astype(f32)).astype(bf16)
        wallt_ref[LANES : 2 * LANES, cols] = rows.astype(bf16)
        out = jnp.concatenate(
            [wout_ref[:, cols].astype(f32), jnp.zeros((LANES - head, BLOCK), f32)], axis=0
        )
        gall_ref[cols, :LANES] = jnp.transpose(out).astype(bf16)
    for i in range(count):
        cols = slice(i * BLOCK, (i + 1) * BLOCK)
        back = slice((count - 1 - i) * BLOCK, (count - i) * BLOCK)
        wall_ref[cols, 2 * LANES :] = dot(flip, wall_ref[back, : 2 * LANES]).astype(bf16)
        gall_ref[cols, LANES:] = dot(flip, gall_ref[back, :LANES]).astype(bf16)
        wallt_ref[2 * LANES :, cols] = dot(wallt_ref[: 2 * LANES, back], flip).astype(bf16)
    tap = iota((CONV, LANES - head), 0)
    taps_ref[:, :head] = conv_ref[...]
    taps_ref[:, head:] = jnp.where(tap == CONV - 1, 1.0, 0.0)


def own_source(shape, dim, ids_ref, tp_size, own_rows):
    z, x, core, ctx = (ids_ref[i] for i in range(4))
    nz = tp_size // 4
    row = iota(shape, dim)
    block = row // own_rows
    j = block % nz
    dx = 1 - (block // nz) % 2
    dcore = 1 - block // (2 * nz)
    owner = ((z ^ j) * 2 + (x ^ dx)) * 2 + (core ^ dcore)
    return (ctx * tp_size + owner) * own_rows + row % own_rows


def exact(parts, apply):
    return sum(apply(part) for part in parts)


def decay_rate(par_refs):
    return -jnp.exp(jnp.full((1, LANES), par_refs[1][0], f32))


def core_kernel(n_pieces, layout, *refs):
    ids_ref, par_refs = refs[0], refs[1:4]
    pieces = refs[4 : 4 + n_pieces]
    early_refs = refs[4 + n_pieces : 6 + n_pieces]
    wall_ref, wallt_ref, gall_ref, taps_ref = refs[6 + n_pieces : 10 + n_pieces]
    send_ref, keep_ref, gcat_ref, gated_ref = refs[10 + n_pieces : 14 + n_pieces]
    tp_size, own_rows, coords = layout
    if coords is None:
        proj, grads = early_refs[0][...], early_refs[1][...]
    else:
        proj_ref, grad_ref = refs[14 + n_pieces :]
        halves = [[ref[...] for ref in early_refs], project(pieces, wall_ref, gall_ref)]
        for p, k, at in owners(ids_ref, layout):
            blocks = len(coords[p][3])
            source = halves[p // n_pieces]
            first = ((p % n_pieces) * blocks + k) * own_rows
            proj_ref[pl.ds(at, own_rows), :] = source[0][first : first + own_rows]
            grad_ref[pl.ds(at, own_rows), :] = source[1][first : first + own_rows]
        proj, grads = proj_ref[...], grad_ref[...]
    length, width = proj.shape[0], wall_ref.shape[0]
    chunks = length // BLOCK
    flip = mirror(BLOCK)
    bias, rate, skip = par_refs[0][0], decay_rate(par_refs), par_refs[2][0]
    lane = iota((1, LANES), 1)
    low = lane < LANES // 2
    causal = iota((BLOCK, BLOCK), 0) >= iota((BLOCK, BLOCK), 1)
    tri = jnp.where(causal, 1.0, 0.0).astype(bf16)
    row_at = iota((length, LANES), 0)

    turned = [proj[:, 2 * LANES : 3 * LANES].astype(bf16)]
    turned += split(proj[:, 3 * LANES :], 3) + split(grads[:, LANES:], 2)
    turned = flip_rows(jnp.concatenate(turned, axis=1), flip)
    turned = [turned[:, i * LANES : (i + 1) * LANES] for i in range(6)]
    strands = (
        (
            proj[:, :LANES].astype(bf16).astype(f32),
            proj[:, LANES : 2 * LANES],
            grads[:, :LANES],
        ),
        (turned[0], turned[1] + turned[2] + turned[3], turned[4] + turned[5]),
    )

    def gates(xz, rest, grad_g):
        pre = taps_ref[CONV - 1 : CONV, :] * xz
        for shift in range(1, CONV):
            moved = jnp.where(row_at >= shift, pltpu.roll(xz, shift, 0), 0.0)
            pre += taps_ref[CONV - 1 - shift : CONV - shift, :] * moved
        sig = jax.nn.sigmoid(pre)
        u = pre * sig
        slope = sig * (1.0 + pre * (1.0 - sig))
        u_other = pltpu.roll(u, LANES // 2, 1)
        raw = jnp.broadcast_to(rest[:, 2 * STATE : 2 * STATE + 1], (length, LANES)) + bias
        dt = jnp.maximum(raw, 0.0) + jnp.log1p(jnp.exp(-jnp.abs(raw)))
        b_all = jnp.where(lane < STATE, rest, 0.0)
        c_all = jnp.where(lane < STATE, pltpu.roll(rest, LANES - STATE, 1), 0.0)
        g_y = jnp.where(low, grad_g * u_other, 0.0)
        return u, slope, u_other, dt, jax.nn.sigmoid(raw), b_all, c_all, dt * u, g_y, grad_g

    def enter_chunk(c, gate, state):
        rows = slice(c * BLOCK, (c + 1) * BLOCK)
        dt, b_all, c_all, w_all = gate[3][rows], gate[5][rows], gate[6][rows], gate[7][rows]
        log_keep = dot(tri, jnp.concatenate(split(dt * rate, 3), axis=1))
        log_keep = log_keep[:, :LANES] + log_keep[:, LANES : 2 * LANES] + log_keep[:, 2 * LANES :]
        across = jnp.transpose(log_keep)[0:1, :]
        gap = jnp.concatenate([log_keep] * (BLOCK // LANES), axis=1) - across
        decay = jnp.exp(jnp.where(causal, gap, -jnp.inf))
        b_low, c_low, w_low = b_all.astype(bf16), c_all.astype(bf16), w_all.astype(bf16)
        mixed = (dot_nt(c_low, b_low) * decay).astype(bf16)
        last = log_keep[BLOCK - 1 : BLOCK, :]
        enter = jnp.exp(log_keep)
        leave = jnp.exp(last - log_keep)
        b_left = (leave * b_all).astype(bf16)
        out = dot(mixed, w_low) + enter * dot(c_low, state.astype(bf16))
        after = jnp.exp(last) * state + dot_tn(b_left, w_low)
        return out, decay, mixed, b_low, c_low, w_low, b_left, enter, leave, last, state, after

    def leave_chunk(c, gate, saved, d_state):
        rows = slice(c * BLOCK, (c + 1) * BLOCK)
        u, c_all, w_all, gy = gate[0][rows], gate[6][rows], gate[7][rows], gate[8][rows]
        out, decay, mixed, b_low, c_low, w_low, b_left, enter, leave, last, before, after = saved
        gy_low = gy.astype(bf16)
        ds_low = d_state.astype(bf16)
        dw = dot_tn(mixed, gy_low) + dot(b_left, ds_low)
        d_scores = (dot_nt(gy_low, w_low) * decay).astype(bf16)
        g_c = dot(d_scores, b_low) + enter * dot_nt(gy_low, before.astype(bf16))
        g_b = dot_tn(d_scores, c_low) + leave * dot_nt(w_low, ds_low)
        d_log = jnp.sum(jnp.where(low, gy * out - w_all * dw, 0.0), axis=1, keepdims=True)
        at_end = jnp.sum(jnp.where(low, after * d_state, 0.0))
        d_log = jnp.broadcast_to(d_log, (BLOCK, LANES))
        d_sum = dot_tn(tri, jnp.concatenate(split(d_log, 2), axis=1))
        d_sum = d_sum[:, :LANES] + d_sum[:, LANES:] + at_end
        g_a = rate * d_sum + jnp.sum(jnp.where(low, u * dw, 0.0), axis=1, keepdims=True)
        carried = (enter * c_all).astype(bf16)
        return dw, g_b, g_c, g_a, jnp.exp(last) * d_state + dot_tn(carried, gy_low)

    gate = [gates(*strand) for strand in strands]
    saved = [[], []]
    state = [jnp.zeros((LANES, LANES), f32)] * 2
    for c in range(chunks):
        for s in range(2):
            saved[s].append(enter_chunk(c, gate[s], state[s]))
            state[s] = saved[s][c][-1]
    state = [jnp.zeros((LANES, LANES), f32)] * 2
    grads = [[None] * chunks, [None] * chunks]
    for c in reversed(range(chunks)):
        for s in range(2):
            *grads[s][c], state[s] = leave_chunk(c, gate[s], saved[s][c], state[s])
    small = []
    for s in range(2):
        u, slope, u_other, dt, dt_slope, _, _, _, g_y, grad_g = gate[s]
        y = jnp.concatenate([part[0] for part in saved[s]], axis=0) + skip * u
        gated = jnp.where(low, y * u_other, 0.0).astype(bf16)
        g_gate = jnp.where(low, grad_g * y, 0.0)
        d_w, g_b, g_c, g_a = (
            jnp.concatenate([part[i] for part in grads[s]], axis=0) for i in range(4)
        )
        g_raw = g_a * dt_slope
        d_u = jnp.where(low, skip * g_y + dt * d_w, pltpu.roll(g_gate, LANES // 2, 1))
        d_pre = d_u * slope
        g_xz = taps_ref[CONV - 1 : CONV, :] * d_pre
        for shift in range(1, CONV):
            moved = jnp.where(
                row_at < length - shift, pltpu.roll(d_pre, length - shift, 0), 0.0
            )
            g_xz += taps_ref[CONV - 1 - shift : CONV - shift, :] * moved
        shared = jnp.where(lane < STATE, g_b, 0.0) + jnp.where(
            (lane >= STATE) & (lane < 2 * STATE), pltpu.roll(g_c, STATE, 1), 0.0
        )
        g_rest = shared + jnp.where(lane == 2 * STATE, g_raw, 0.0)
        result = jnp.concatenate([g_xz.astype(bf16), g_rest.astype(bf16), gated], axis=1)
        small.append(shared)
        if s == 1:
            result = flip_rows(result, flip).astype(bf16)
        gcat_ref[:, 2 * s * LANES : 2 * (s + 1) * LANES] = result[:, : 2 * LANES]
        gated_ref[:, s * LANES : (s + 1) * LANES] = result[:, 2 * LANES :]

    pair = small[0] + pltpu.roll(small[1], 2 * STATE, 1)
    shared_t = jnp.transpose(pair)[: 4 * STATE].astype(bf16)
    groups = width // length
    step = 4 * STATE // groups
    for i in range(groups):
        part = shared_t[i * step : (i + 1) * step, :]
        send_ref[0:step, i * length : (i + 1) * length] = part
        keep_ref[0:step, i * length : (i + 1) * length] = part.astype(f32)
    own = tp_size * own_rows
    source = own_source((own, length), 0, ids_ref, tp_size, own_rows)
    pick = jnp.where(source == iota((own, length), 1), 1.0, 0.0).astype(bf16)
    picked = dot(pick, gcat_ref[...]).astype(bf16)
    half = own // 2
    part = dot(picked, wallt_ref[...])
    send_ref[step:, :] = part[:half].astype(bf16)
    keep_ref[step:, :] = part[half:]


def weight_kernel(n_pieces, layout, scaling, *refs):
    ids_ref = refs[0]
    pieces = refs[1 : 1 + n_pieces]
    gcat_ref, gated_ref, _, dwin_ref, dwout_ref, mark_ref = refs[1 + n_pieces : 7 + n_pieces]
    mark_ref[...] = jnp.zeros_like(mark_ref)
    if layout[2] is None:
        h_ref, d_ref = pieces
    else:
        h_ref, d_ref = refs[7 + n_pieces :]
        assemble(ids_ref, pieces, h_ref, d_ref, layout)
    flip = mirror(BLOCK)
    columns = h_ref.shape[1] // BLOCK
    head = dwout_ref.shape[0]
    g_f = gcat_ref[:, 0:LANES]
    g_r = gcat_ref[:, 2 * LANES : 3 * LANES]
    y_f = gated_ref[:, 0:LANES]
    y_r = gated_ref[:, LANES:]
    for i in range(columns):
        cols = slice(i * BLOCK, (i + 1) * BLOCK)
        back = slice((columns - 1 - i) * BLOCK, (columns - i) * BLOCK)
        turned = dot(h_ref[:, back], flip).astype(bf16)
        grad = dot_tn(g_f, h_ref[:, cols]) + dot_tn(g_r, turned)
        dwin_ref[cols, :] = jnp.transpose(grad * scaling)
        turned = dot(d_ref[:, back], flip).astype(bf16)
        grad = dot_tn(y_f, d_ref[:, cols]) + dot_tn(y_r, turned)
        dwout_ref[:, cols] = grad[:head] * scaling


def add_kernel(a_ref, b_ref, _, out_ref):
    rows = slice(0, out_ref.shape[0])
    out_ref[...] = (a_ref[rows, :].astype(f32) + b_ref[rows, :].astype(f32)).astype(bf16)


def stage_kernel(own_rows, keep_ref, got_ref, own_ref, *piece_refs):
    for j, ref in enumerate([own_ref, *piece_refs]):
        rows = slice(j * own_rows, (j + 1) * own_rows)
        value = keep_ref[rows, :] + got_ref[rows, :].astype(f32)
        ref[...] = value.astype(ref.dtype)


def last_kernel(scaling, own_ref, h_ref, shared_ref, other_ref, *refs):
    got_refs, (dhid_ref, dwbct_ref) = refs[:-2], refs[-2:]
    flip = mirror(BLOCK)
    length, width = h_ref.shape
    groups = width // length
    total = own_ref[...]
    for got in got_refs:
        total += got[...].astype(f32)
    dhid_ref[...] = total.astype(bf16)
    shared = (shared_ref[...].astype(f32) + other_ref[...].astype(f32)).astype(bf16)
    shared = jnp.concatenate(
        [shared[:, i * length : (i + 1) * length] for i in range(groups)], axis=0
    )
    fwd = shared[: 2 * STATE]
    rev = turn_columns(shared[2 * STATE :], flip).astype(bf16)
    pairs = dot(jnp.concatenate([fwd, rev], axis=0), h_ref[...])
    turned = exact(split(pairs[2 * STATE :], 3), lambda part: turn_columns(part, flip))
    dwbct_ref[...] = (pairs[: 2 * STATE] + turned) * scaling


def spec(memory=pltpu.VMEM):
    return pl.BlockSpec(memory_space=memory)


def call(kernel, inputs, n_smem, outs, scratch, flops, moved, unread=0, vmem=32):
    return pl.pallas_call(
        kernel,
        out_shape=outs,
        in_specs=[spec(pltpu.SMEM)] * n_smem
        + [spec()] * (len(inputs) - n_smem - unread)
        + [spec(pl.ANY)] * unread,
        out_specs=jax.tree.map(lambda _: spec(), outs),
        scratch_shapes=scratch,
        compiler_params=pltpu.CompilerParams(vmem_limit_bytes=vmem * 1024 * 1024),
        cost_estimate=pl.CostEstimate(flops=flops, bytes_accessed=moved, transcendentals=0),
    )(*inputs)


def shape(dims, dtype):
    return jax.ShapeDtypeStruct(dims, dtype)


def local(ctx_size, tp_size, hidden, w_in, w_bc, w_dt, dt_bias, a_log, d_skip, conv_w, w_out, d_out):
    own_rows, width = hidden.shape
    length = own_rows * tp_size * ctx_size
    head = w_out.shape[0]
    nz = tp_size // 4
    chunks = length // BLOCK
    t = lax.axis_index("tp")
    ids = jnp.stack([t >> 2, (t >> 1) & 1, t & 1, lax.axis_index("ctx")]).astype(jnp.int32)
    params = [dt_bias, a_log, d_skip]
    def across(value, flip_bits):
        return lax.ppermute(value, "tp", [(i, i ^ flip_bits) for i in range(tp_size)])

    def along(value, offset):
        return lax.ppermute(
            value, "ctx", [((i + offset) % ctx_size, i) for i in range(ctx_size)]
        )

    def prepare(*begun):
        return call(
            prep_kernel,
            [ids, w_in, w_bc.T, w_dt, w_out, conv_w, *begun],
            1,
            (
                shape((width, 4 * LANES), bf16),
                shape((4 * LANES, width), bf16),
                shape((width, 2 * LANES), bf16),
                shape((CONV, LANES), f32),
            ),
            [],
            6 * width * BLOCK * BLOCK,
            20 * width * LANES,
            len(begun),
        )

    def pack(parts, rows):
        return call(
            functools.partial(pack_kernel, len(parts), own_rows),
            parts,
            0,
            shape((rows, width), bf16),
            [],
            0,
            4 * rows * width,
        )

    def column(own, count):
        if count == 1:
            return [own]
        half = count // 2
        return column(own, half) + column(across(own, 4 * half), half)

    def after(first, value):
        outs = (shape(value.shape, bf16),)
        return call(
            functools.partial(copy_kernel, 1), [value, first], 0, outs, [], 0, 4 * value.size, 1
        )[0]

    if own_rows % TILE_ROWS == 0:
        low = jnp.array(-jnp.inf, bf16)
        both = jnp.maximum(
            lax.pad(hidden, low, [(0, own_rows, 0), (0, 0, 0)]),
            lax.pad(d_out, low, [(own_rows, 0, 0), (0, 0, 0)]),
        )
        zs = column(both, nz)
        coords, pieces, planes = [], [], []
        for blocks in (range(0, nz // 2), range(nz // 2, nz)):
            chunk = pack([zs[j] for j in blocks], nz * own_rows)
            ahead = [along(chunk, dc) for dc in range(1, ctx_size)]
            planes.append((chunk, across(chunk, 2), ahead, tuple(blocks)))
        (_, beside_a, ahead_a, _), (chunk_b, beside_b, ahead_b, _) = planes
        wall, wallt, gall, taps = prepare(chunk_b)
        count = len(ahead_a)
        *forward_a, forward_b = call(
            functools.partial(copy_kernel, count + 1),
            [*ahead_a, beside_b, *ahead_b, beside_a],
            0,
            (shape(beside_b.shape, bf16),) * (count + 1),
            [],
            0,
            8 * beside_b.size,
            count + 1,
        )
        diagonals = (
            [after(taps, across(piece, 2)) for piece in forward_a],
            [along(forward_b, dc + 1) for dc in range(count)],
        )
        for (chunk, beside, ahead, blocks), diagonal in zip(planes, diagonals):
            plane = [((0, 0), chunk), ((0, 1), beside)]
            for dc in range(count):
                plane += [((dc + 1, 0), ahead[dc]), ((dc + 1, 1), diagonal[dc])]
            for (dc, dx), piece in plane:
                coords += [(dc, dx, 0, blocks), (dc, dx, 1, blocks)]
                pieces += [piece, across(piece, 1)]
        layout = (tp_size, own_rows, tuple(coords))
        early, late = pieces[: len(pieces) // 2], pieces[len(pieces) // 2 :]
    else:
        pieces = [lax.all_gather(a, ("ctx", "tp"), axis=0, tiled=True) for a in (hidden, d_out)]
        layout = (tp_size, own_rows, None)
        wall, wallt, gall, taps = prepare()
        early, late = [jnp.concatenate(pieces, axis=0)], []
    ordered = layout[2] is None
    vmem = 60 if ordered else 32
    early_rows = sum(piece.shape[0] for piece in early) // 2
    early = call(
        early_kernel,
        [*early, wall, gall],
        0,
        (shape((early_rows, 4 * LANES), f32), shape((early_rows, 2 * LANES), f32)),
        [],
        2 * early_rows * width * 6 * LANES,
        4 * early_rows * width,
        vmem=vmem,
    )
    extra = 4 * STATE * length // width
    half = tp_size * own_rows // 2
    send, keep, gcat, gated = call(
        functools.partial(core_kernel, len(late), layout),
        [ids, *params, *late, *early, wall, wallt, gall, taps],
        4,
        (
            shape((extra + half, width), bf16),
            shape((extra + half, width), f32),
            shape((length, 4 * LANES), bf16),
            shape((length, 2 * LANES), bf16),
        ),
        []
        if ordered
        else [pltpu.VMEM((length, 4 * LANES), f32), pltpu.VMEM((length, 2 * LANES), f32)],
        8 * length * width * BLOCK,
        8 * length * width,
        vmem=vmem,
    )
    scaling = 1.0 / math.sqrt(length)
    got = across(send, 1)
    quarter = half // 2
    at = extra + quarter
    given, own_given = got, keep
    send = (keep[extra:at] + got[extra:at].astype(f32)).astype(bf16)
    keep = keep[at:] + got[at:].astype(f32)
    sent = send
    got = across(send, 2)

    def add_shared(a, b, *first):
        return call(
            add_kernel,
            [a, b, *first],
            0,
            shape((extra, width), bf16),
            [],
            extra * width,
            6 * extra * width,
            1,
        )

    outs = (shape((width, LANES), f32), shape((head, width), f32), shape((8, LANES), f32))
    if not ordered:
        outs += (shape((length, width), bf16),)
    d_w_in, d_w_out, mark, *in_order = call(
        functools.partial(weight_kernel, len(pieces), layout, scaling),
        [ids, *pieces, gcat, gated, send],
        1,
        outs,
        [] if ordered else [pltpu.VMEM((length, width), bf16)],
        8 * length * width * BLOCK,
        8 * length * width,
        1,
        vmem=vmem,
    )
    in_order = in_order[0] if in_order else pieces[0]
    own, *send = call(
        functools.partial(stage_kernel, own_rows),
        [keep, got],
        0,
        (shape((own_rows, width), f32),) + (shape((own_rows, width), bf16),) * (nz - 1),
        [],
        4 * quarter * width,
        10 * quarter * width,
    )
    shared = add_shared(own_given, given, sent)
    step = nz // 2
    while step:
        shared = add_shared(shared, across(shared, 4 * step), mark if step > 1 else own)
        step //= 2
    got = [across(piece, 4 * (j + 1)) for j, piece in enumerate(send)]
    d_hidden, d_w_bc = call(
        functools.partial(last_kernel, scaling),
        [own, in_order, shared, across(shared, 2), *got],
        0,
        (shape((own_rows, width), bf16), shape((2 * STATE, width), f32)),
        [],
        2 * length * width * LANES,
        4 * length * width,
    )
    return (d_hidden, d_w_in, d_w_out, d_w_bc.T)


def solution(mesh):
    in_specs = (
        P(("ctx", "tp"), None),
        P(None, "tp"),
        P(),
        P("tp", None),
        P("tp"),
        P("tp"),
        P("tp"),
        P(None, "tp"),
        P("tp", None),
        P(("ctx", "tp"), None),
    )
    out_specs = (P(("ctx", "tp"), None), P(None, "tp"), P("tp", None), P())
    body = functools.partial(local, mesh.shape["ctx"], mesh.shape["tp"])
    return jax.shard_map(body, mesh=mesh, in_specs=in_specs, out_specs=out_specs, check_vma=False)
```

```python
import functools
import math

import jax
import jax.numpy as jnp
from jax import lax
from jax.experimental import pallas as pl
from jax.experimental.pallas import tpu as pltpu
from jax.sharding import PartitionSpec as P

STATE = 16
CONV = 4
LANES = 128
BLOCK = 256
TILE_ROWS = 16
f32 = jnp.float32
bf16 = jnp.bfloat16


def dot(a, b):
    return jnp.dot(a, b, preferred_element_type=f32)


def dot_nt(a, b):
    return lax.dot_general(a, b, (((1,), (1,)), ((), ())), preferred_element_type=f32)


def dot_tn(a, b):
    return lax.dot_general(a, b, (((0,), (0,)), ((), ())), preferred_element_type=f32)


def iota(shape, dim):
    return lax.broadcasted_iota(jnp.int32, shape, dim)


def mirror(size):
    return jnp.where(iota((size, size), 0) + iota((size, size), 1) == size - 1, 1.0, 0.0).astype(
        bf16
    )


def split(value, terms):
    parts = []
    for _ in range(terms):
        part = value.astype(bf16)
        parts.append(part)
        value = value - part.astype(f32)
    return parts


def flip_rows(value, flip):
    count = value.shape[0] // BLOCK
    return jnp.concatenate(
        [dot(flip, value[(count - 1 - i) * BLOCK : (count - i) * BLOCK]) for i in range(count)],
        axis=0,
    )


def owners(ids_ref, layout):
    tp_size, own_rows, coords = layout
    z, x, core, ctx = (ids_ref[i] for i in range(4))
    ctx_size = max(c[0] for c in coords) + 1
    for p, (dc, dx, dcore, blocks) in enumerate(coords):
        from_ctx = lax.rem(ctx + dc, ctx_size)
        for k, j in enumerate(blocks):
            owner = ((z ^ j) * 2 + (x ^ dx)) * 2 + (core ^ dcore)
            at = pl.multiple_of((from_ctx * tp_size + owner) * own_rows, own_rows)
            yield p, k, at


def assemble(ids_ref, pieces, h_ref, d_ref, layout):
    own_rows = layout[1]
    for p, k, at in owners(ids_ref, layout):
        piece = pieces[p]
        half = piece.shape[0] // 2
        h_rows = slice(k * own_rows, (k + 1) * own_rows)
        d_rows = slice(half + k * own_rows, half + (k + 1) * own_rows)
        h_ref[pl.ds(at, own_rows), :] = piece[h_rows, :]
        d_ref[pl.ds(at, own_rows), :] = piece[d_rows, :]


def project(pieces, wall_ref, gall_ref):
    half = pieces[0].shape[0] // 2
    h = jnp.concatenate([piece[:half, :] for piece in pieces], axis=0)
    d = jnp.concatenate([piece[half:, :] for piece in pieces], axis=0)
    return dot(h, wall_ref[...]), dot(d, gall_ref[...])


def pack_kernel(n_parts, own_rows, *refs):
    parts, out_ref = refs[:n_parts], refs[-1]
    half = n_parts * own_rows
    for k, ref in enumerate(parts):
        out_ref[k * own_rows : (k + 1) * own_rows, :] = ref[:own_rows, :]
        if ref.shape[0] > own_rows:
            rows = slice(half + k * own_rows, half + (k + 1) * own_rows)
            out_ref[rows, :] = ref[own_rows:, :]


def copy_kernel(count, *refs):
    for value_ref, out_ref in zip(refs[:count], refs[len(refs) - count :]):
        out_ref[...] = value_ref[...]


def early_kernel(*refs):
    pieces = refs[:-4]
    wall_ref, gall_ref, proj_ref, grad_ref = refs[-4:]
    proj_ref[...], grad_ref[...] = project(pieces, wall_ref, gall_ref)


def turn_columns(value, flip):
    count = value.shape[1] // BLOCK
    return jnp.concatenate(
        [dot(value[:, (count - 1 - i) * BLOCK : (count - i) * BLOCK], flip) for i in range(count)],
        axis=1,
    )


def prep_kernel(ids_ref, *refs):
    win_ref, wbct_ref, wdt_ref, wout_ref, conv_ref = refs[:5]
    wall_ref, wallt_ref, gall_ref, taps_ref = refs[-4:]
    flip = mirror(BLOCK)
    width = win_ref.shape[0]
    head = wout_ref.shape[0]
    count = width // BLOCK
    shared = 2 * STATE + 1
    for i in range(count):
        cols = slice(i * BLOCK, (i + 1) * BLOCK)
        rows = jnp.concatenate(
            [
                wbct_ref[:, cols].astype(f32),
                wdt_ref[:, cols].astype(f32),
                jnp.zeros((LANES - shared, BLOCK), f32),
            ],
            axis=0,
        )
        block = win_ref[cols, :]
        wall_ref[cols, :LANES] = block
        wall_ref[cols, LANES : 2 * LANES] = jnp.transpose(rows).astype(bf16)
        wallt_ref[:LANES, cols] = jnp.transpose(block.astype(f32)).astype(bf16)
        wallt_ref[LANES : 2 * LANES, cols] = rows.astype(bf16)
        out = jnp.concatenate(
            [wout_ref[:, cols].astype(f32), jnp.zeros((LANES - head, BLOCK), f32)], axis=0
        )
        gall_ref[cols, :LANES] = jnp.transpose(out).astype(bf16)
    for i in range(count):
        cols = slice(i * BLOCK, (i + 1) * BLOCK)
        back = slice((count - 1 - i) * BLOCK, (count - i) * BLOCK)
        wall_ref[cols, 2 * LANES :] = dot(flip, wall_ref[back, : 2 * LANES]).astype(bf16)
        gall_ref[cols, LANES:] = dot(flip, gall_ref[back, :LANES]).astype(bf16)
        wallt_ref[2 * LANES :, cols] = dot(wallt_ref[: 2 * LANES, back], flip).astype(bf16)
    tap = iota((CONV, LANES - head), 0)
    taps_ref[:, :head] = conv_ref[...]
    taps_ref[:, head:] = jnp.where(tap == CONV - 1, 1.0, 0.0)


def own_source(shape, dim, ids_ref, tp_size, own_rows):
    core, ctx = ids_ref[2], ids_ref[3]
    row = iota(shape, dim)
    block = row // own_rows
    chips = tp_size // 2
    owner = (block % chips) * 2 + (core ^ (1 - block // chips))
    return (ctx * tp_size + owner) * own_rows + row % own_rows


def exact(parts, apply):
    return sum(apply(part) for part in parts)


def decay_rate(par_refs):
    return -jnp.exp(jnp.full((1, LANES), par_refs[1][0], f32))


def core_kernel(n_pieces, layout, *refs):
    ids_ref, par_refs = refs[0], refs[1:4]
    pieces = refs[4 : 4 + n_pieces]
    early_refs = refs[4 + n_pieces : 6 + n_pieces]
    wall_ref, wallt_ref, gall_ref, taps_ref = refs[6 + n_pieces : 10 + n_pieces]
    send_ref, keep_ref, gcat_ref, gated_ref = refs[10 + n_pieces : 14 + n_pieces]
    tp_size, own_rows, coords = layout
    if coords is None:
        proj, grads = early_refs[0][...], early_refs[1][...]
    else:
        proj_ref, grad_ref = refs[14 + n_pieces :]
        halves = [[ref[...] for ref in early_refs], project(pieces, wall_ref, gall_ref)]
        for p, k, at in owners(ids_ref, layout):
            blocks = len(coords[p][3])
            source = halves[p // n_pieces]
            first = ((p % n_pieces) * blocks + k) * own_rows
            proj_ref[pl.ds(at, own_rows), :] = source[0][first : first + own_rows]
            grad_ref[pl.ds(at, own_rows), :] = source[1][first : first + own_rows]
        proj, grads = proj_ref[...], grad_ref[...]
    length, width = proj.shape[0], wall_ref.shape[0]
    chunks = length // BLOCK
    flip = mirror(BLOCK)
    bias, rate, skip = par_refs[0][0], decay_rate(par_refs), par_refs[2][0]
    lane = iota((1, LANES), 1)
    low = lane < LANES // 2
    causal = iota((BLOCK, BLOCK), 0) >= iota((BLOCK, BLOCK), 1)
    tri = jnp.where(causal, 1.0, 0.0).astype(bf16)
    row_at = iota((length, LANES), 0)

    turned = [proj[:, 2 * LANES : 3 * LANES].astype(bf16)]
    turned += split(proj[:, 3 * LANES :], 3) + split(grads[:, LANES:], 2)
    turned = flip_rows(jnp.concatenate(turned, axis=1), flip)
    turned = [turned[:, i * LANES : (i + 1) * LANES] for i in range(6)]
    strands = (
        (
            proj[:, :LANES].astype(bf16).astype(f32),
            proj[:, LANES : 2 * LANES],
            grads[:, :LANES],
        ),
        (turned[0], turned[1] + turned[2] + turned[3], turned[4] + turned[5]),
    )

    def gates(xz, rest, grad_g):
        pre = taps_ref[CONV - 1 : CONV, :] * xz
        for shift in range(1, CONV):
            moved = jnp.where(row_at >= shift, pltpu.roll(xz, shift, 0), 0.0)
            pre += taps_ref[CONV - 1 - shift : CONV - shift, :] * moved
        sig = jax.nn.sigmoid(pre)
        u = pre * sig
        slope = sig * (1.0 + pre * (1.0 - sig))
        u_other = pltpu.roll(u, LANES // 2, 1)
        raw = jnp.broadcast_to(rest[:, 2 * STATE : 2 * STATE + 1], (length, LANES)) + bias
        dt = jnp.maximum(raw, 0.0) + jnp.log1p(jnp.exp(-jnp.abs(raw)))
        b_all = jnp.where(lane < STATE, rest, 0.0)
        c_all = jnp.where(lane < STATE, pltpu.roll(rest, LANES - STATE, 1), 0.0)
        g_y = jnp.where(low, grad_g * u_other, 0.0)
        return u, slope, u_other, dt, jax.nn.sigmoid(raw), b_all, c_all, dt * u, g_y, grad_g

    def enter_chunk(c, gate, state):
        rows = slice(c * BLOCK, (c + 1) * BLOCK)
        dt, b_all, c_all, w_all = gate[3][rows], gate[5][rows], gate[6][rows], gate[7][rows]
        log_keep = dot(tri, jnp.concatenate(split(dt * rate, 3), axis=1))
        log_keep = log_keep[:, :LANES] + log_keep[:, LANES : 2 * LANES] + log_keep[:, 2 * LANES :]
        across = jnp.transpose(log_keep)[0:1, :]
        gap = jnp.concatenate([log_keep] * (BLOCK // LANES), axis=1) - across
        decay = jnp.exp(jnp.where(causal, gap, -jnp.inf))
        b_low, c_low, w_low = b_all.astype(bf16), c_all.astype(bf16), w_all.astype(bf16)
        mixed = (dot_nt(c_low, b_low) * decay).astype(bf16)
        last = log_keep[BLOCK - 1 : BLOCK, :]
        enter = jnp.exp(log_keep)
        leave = jnp.exp(last - log_keep)
        b_left = (leave * b_all).astype(bf16)
        out = dot(mixed, w_low) + enter * dot(c_low, state.astype(bf16))
        after = jnp.exp(last) * state + dot_tn(b_left, w_low)
        return out, decay, mixed, b_low, c_low, w_low, b_left, enter, leave, last, state, after

    def leave_chunk(c, gate, saved, d_state):
        rows = slice(c * BLOCK, (c + 1) * BLOCK)
        u, c_all, w_all, gy = gate[0][rows], gate[6][rows], gate[7][rows], gate[8][rows]
        out, decay, mixed, b_low, c_low, w_low, b_left, enter, leave, last, before, after = saved
        gy_low = gy.astype(bf16)
        ds_low = d_state.astype(bf16)
        dw = dot_tn(mixed, gy_low) + dot(b_left, ds_low)
        d_scores = (dot_nt(gy_low, w_low) * decay).astype(bf16)
        g_c = dot(d_scores, b_low) + enter * dot_nt(gy_low, before.astype(bf16))
        g_b = dot_tn(d_scores, c_low) + leave * dot_nt(w_low, ds_low)
        d_log = jnp.sum(jnp.where(low, gy * out - w_all * dw, 0.0), axis=1, keepdims=True)
        at_end = jnp.sum(jnp.where(low, after * d_state, 0.0))
        d_log = jnp.broadcast_to(d_log, (BLOCK, LANES))
        d_sum = dot_tn(tri, jnp.concatenate(split(d_log, 2), axis=1))
        d_sum = d_sum[:, :LANES] + d_sum[:, LANES:] + at_end
        g_a = rate * d_sum + jnp.sum(jnp.where(low, u * dw, 0.0), axis=1, keepdims=True)
        carried = (enter * c_all).astype(bf16)
        return dw, g_b, g_c, g_a, jnp.exp(last) * d_state + dot_tn(carried, gy_low)

    gate = [gates(*strand) for strand in strands]
    saved = [[], []]
    state = [jnp.zeros((LANES, LANES), f32)] * 2
    for c in range(chunks):
        for s in range(2):
            saved[s].append(enter_chunk(c, gate[s], state[s]))
            state[s] = saved[s][c][-1]
    state = [jnp.zeros((LANES, LANES), f32)] * 2
    grads = [[None] * chunks, [None] * chunks]
    for c in reversed(range(chunks)):
        for s in range(2):
            *grads[s][c], state[s] = leave_chunk(c, gate[s], saved[s][c], state[s])
    small = []
    for s in range(2):
        u, slope, u_other, dt, dt_slope, _, _, _, g_y, grad_g = gate[s]
        y = jnp.concatenate([part[0] for part in saved[s]], axis=0) + skip * u
        gated = jnp.where(low, y * u_other, 0.0).astype(bf16)
        g_gate = jnp.where(low, grad_g * y, 0.0)
        d_w, g_b, g_c, g_a = (
            jnp.concatenate([part[i] for part in grads[s]], axis=0) for i in range(4)
        )
        g_raw = g_a * dt_slope
        d_u = jnp.where(low, skip * g_y + dt * d_w, pltpu.roll(g_gate, LANES // 2, 1))
        d_pre = d_u * slope
        g_xz = taps_ref[CONV - 1 : CONV, :] * d_pre
        for shift in range(1, CONV):
            moved = jnp.where(
                row_at < length - shift, pltpu.roll(d_pre, length - shift, 0), 0.0
            )
            g_xz += taps_ref[CONV - 1 - shift : CONV - shift, :] * moved
        shared = jnp.where(lane < STATE, g_b, 0.0) + jnp.where(
            (lane >= STATE) & (lane < 2 * STATE), pltpu.roll(g_c, STATE, 1), 0.0
        )
        g_rest = shared + jnp.where(lane == 2 * STATE, g_raw, 0.0)
        result = jnp.concatenate([g_xz.astype(bf16), g_rest.astype(bf16), gated], axis=1)
        small.append(shared)
        if s == 1:
            result = flip_rows(result, flip).astype(bf16)
        gcat_ref[:, 2 * s * LANES : 2 * (s + 1) * LANES] = result[:, : 2 * LANES]
        gated_ref[:, s * LANES : (s + 1) * LANES] = result[:, 2 * LANES :]

    pair = small[0] + pltpu.roll(small[1], 2 * STATE, 1)
    shared_t = jnp.transpose(pair)[: 4 * STATE].astype(bf16)
    groups = width // length
    step = 4 * STATE // groups
    for i in range(groups):
        part = shared_t[i * step : (i + 1) * step, :]
        send_ref[0:step, i * length : (i + 1) * length] = part
        keep_ref[0:step, i * length : (i + 1) * length] = part.astype(f32)
    own = tp_size * own_rows
    source = own_source((own, length), 0, ids_ref, tp_size, own_rows)
    pick = jnp.where(source == iota((own, length), 1), 1.0, 0.0).astype(bf16)
    picked = dot(pick, gcat_ref[...]).astype(bf16)
    half = own // 2
    part = dot(picked, wallt_ref[...])
    send_ref[step:, :] = part[:half].astype(bf16)
    keep_ref[step:, :] = part[half:]


def weight_kernel(n_pieces, layout, scaling, *refs):
    ids_ref = refs[0]
    pieces = refs[1 : 1 + n_pieces]
    gcat_ref, gated_ref, _, dwin_ref, dwout_ref, mark_ref = refs[1 + n_pieces : 7 + n_pieces]
    mark_ref[...] = jnp.zeros_like(mark_ref)
    if layout[2] is None:
        h_ref, d_ref = pieces
    else:
        h_ref, d_ref = refs[7 + n_pieces :]
        assemble(ids_ref, pieces, h_ref, d_ref, layout)
    flip = mirror(BLOCK)
    columns = h_ref.shape[1] // BLOCK
    head = dwout_ref.shape[0]
    g_f = gcat_ref[:, 0:LANES]
    g_r = gcat_ref[:, 2 * LANES : 3 * LANES]
    y_f = gated_ref[:, 0:LANES]
    y_r = gated_ref[:, LANES:]
    for i in range(columns):
        cols = slice(i * BLOCK, (i + 1) * BLOCK)
        back = slice((columns - 1 - i) * BLOCK, (columns - i) * BLOCK)
        turned = dot(h_ref[:, back], flip).astype(bf16)
        grad = dot_tn(g_f, h_ref[:, cols]) + dot_tn(g_r, turned)
        dwin_ref[cols, :] = jnp.transpose(grad * scaling)
        turned = dot(d_ref[:, back], flip).astype(bf16)
        grad = dot_tn(y_f, d_ref[:, cols]) + dot_tn(y_r, turned)
        dwout_ref[:, cols] = grad[:head] * scaling


def add_kernel(a_ref, b_ref, _, out_ref):
    rows = slice(0, out_ref.shape[0])
    out_ref[...] = (a_ref[rows, :].astype(f32) + b_ref[rows, :].astype(f32)).astype(bf16)


def last_kernel(own_rows, scaling, got_ref, h_ref, shared_ref, other_ref, dhid_ref, dwbct_ref):
    flip = mirror(BLOCK)
    length, width = h_ref.shape
    groups = width // length
    total = jnp.zeros((own_rows, width), f32)
    for i in range(got_ref.shape[0] // own_rows):
        total += got_ref[i * own_rows : (i + 1) * own_rows, :].astype(f32)
    dhid_ref[...] = total.astype(bf16)
    shared = (shared_ref[...].astype(f32) + other_ref[...].astype(f32)).astype(bf16)
    shared = jnp.concatenate(
        [shared[:, i * length : (i + 1) * length] for i in range(groups)], axis=0
    )
    fwd = shared[: 2 * STATE]
    rev = turn_columns(shared[2 * STATE :], flip).astype(bf16)
    pairs = dot(jnp.concatenate([fwd, rev], axis=0), h_ref[...])
    turned = exact(split(pairs[2 * STATE :], 3), lambda part: turn_columns(part, flip))
    dwbct_ref[...] = (pairs[: 2 * STATE] + turned) * scaling


def spec(memory=pltpu.VMEM):
    return pl.BlockSpec(memory_space=memory)


def call(kernel, inputs, n_smem, outs, scratch, flops, moved, unread=0, vmem=32):
    return pl.pallas_call(
        kernel,
        out_shape=outs,
        in_specs=[spec(pltpu.SMEM)] * n_smem
        + [spec()] * (len(inputs) - n_smem - unread)
        + [spec(pl.ANY)] * unread,
        out_specs=jax.tree.map(lambda _: spec(), outs),
        scratch_shapes=scratch,
        compiler_params=pltpu.CompilerParams(vmem_limit_bytes=vmem * 1024 * 1024),
        cost_estimate=pl.CostEstimate(flops=flops, bytes_accessed=moved, transcendentals=0),
    )(*inputs)


def shape(dims, dtype):
    return jax.ShapeDtypeStruct(dims, dtype)


def local(ctx_size, tp_size, hidden, w_in, w_bc, w_dt, dt_bias, a_log, d_skip, conv_w, w_out, d_out):
    own_rows, width = hidden.shape
    length = own_rows * tp_size * ctx_size
    head = w_out.shape[0]
    nz = tp_size // 4
    chunks = length // BLOCK
    t = lax.axis_index("tp")
    ids = jnp.stack([t >> 2, (t >> 1) & 1, t & 1, lax.axis_index("ctx")]).astype(jnp.int32)
    params = [dt_bias, a_log, d_skip]
    def across(value, flip_bits):
        return lax.ppermute(value, "tp", [(i, i ^ flip_bits) for i in range(tp_size)])

    def along(value, offset):
        return lax.ppermute(
            value, "ctx", [((i + offset) % ctx_size, i) for i in range(ctx_size)]
        )

    def prepare(*begun):
        return call(
            prep_kernel,
            [ids, w_in, w_bc.T, w_dt, w_out, conv_w, *begun],
            1,
            (
                shape((width, 4 * LANES), bf16),
                shape((4 * LANES, width), bf16),
                shape((width, 2 * LANES), bf16),
                shape((CONV, LANES), f32),
            ),
            [],
            6 * width * BLOCK * BLOCK,
            20 * width * LANES,
            len(begun),
        )

    def pack(parts, rows):
        return call(
            functools.partial(pack_kernel, len(parts), own_rows),
            parts,
            0,
            shape((rows, width), bf16),
            [],
            0,
            4 * rows * width,
        )

    def column(own, count):
        if count == 1:
            return [own]
        half = count // 2
        return column(own, half) + column(across(own, 4 * half), half)

    def after(first, value):
        outs = (shape(value.shape, bf16),)
        return call(
            functools.partial(copy_kernel, 1), [value, first], 0, outs, [], 0, 4 * value.size, 1
        )[0]

    if own_rows % TILE_ROWS == 0:
        low = jnp.array(-jnp.inf, bf16)
        both = jnp.maximum(
            lax.pad(hidden, low, [(0, own_rows, 0), (0, 0, 0)]),
            lax.pad(d_out, low, [(own_rows, 0, 0), (0, 0, 0)]),
        )
        zs = column(both, nz)
        coords, pieces, planes = [], [], []
        for blocks in (range(0, nz // 2), range(nz // 2, nz)):
            chunk = pack([zs[j] for j in blocks], nz * own_rows)
            ahead = [along(chunk, dc) for dc in range(1, ctx_size)]
            planes.append((chunk, across(chunk, 2), ahead, tuple(blocks)))
        (_, beside_a, ahead_a, _), (chunk_b, beside_b, ahead_b, _) = planes
        wall, wallt, gall, taps = prepare(chunk_b)
        count = len(ahead_a)
        *forward_a, forward_b = call(
            functools.partial(copy_kernel, count + 1),
            [*ahead_a, beside_b, *ahead_b, beside_a],
            0,
            (shape(beside_b.shape, bf16),) * (count + 1),
            [],
            0,
            8 * beside_b.size,
            count + 1,
        )
        diagonals = (
            [after(taps, across(piece, 2)) for piece in forward_a],
            [along(forward_b, dc + 1) for dc in range(count)],
        )
        for (chunk, beside, ahead, blocks), diagonal in zip(planes, diagonals):
            plane = [((0, 0), chunk), ((0, 1), beside)]
            for dc in range(count):
                plane += [((dc + 1, 0), ahead[dc]), ((dc + 1, 1), diagonal[dc])]
            for (dc, dx), piece in plane:
                coords += [(dc, dx, 0, blocks), (dc, dx, 1, blocks)]
                pieces += [piece, across(piece, 1)]
        layout = (tp_size, own_rows, tuple(coords))
        early, late = pieces[: len(pieces) // 2], pieces[len(pieces) // 2 :]
    else:
        pieces = [lax.all_gather(a, ("ctx", "tp"), axis=0, tiled=True) for a in (hidden, d_out)]
        layout = (tp_size, own_rows, None)
        wall, wallt, gall, taps = prepare()
        early, late = [jnp.concatenate(pieces, axis=0)], []
    ordered = layout[2] is None
    vmem = 60 if ordered else 32
    early_rows = sum(piece.shape[0] for piece in early) // 2
    early = call(
        early_kernel,
        [*early, wall, gall],
        0,
        (shape((early_rows, 4 * LANES), f32), shape((early_rows, 2 * LANES), f32)),
        [],
        2 * early_rows * width * 6 * LANES,
        4 * early_rows * width,
        vmem=vmem,
    )
    extra = 4 * STATE * length // width
    half = tp_size * own_rows // 2
    send, keep, gcat, gated = call(
        functools.partial(core_kernel, len(late), layout),
        [ids, *params, *late, *early, wall, wallt, gall, taps],
        4,
        (
            shape((extra + half, width), bf16),
            shape((extra + half, width), f32),
            shape((length, 4 * LANES), bf16),
            shape((length, 2 * LANES), bf16),
        ),
        []
        if ordered
        else [pltpu.VMEM((length, 4 * LANES), f32), pltpu.VMEM((length, 2 * LANES), f32)],
        8 * length * width * BLOCK,
        8 * length * width,
        vmem=vmem,
    )
    scaling = 1.0 / math.sqrt(length)
    got = across(send, 1)
    send_rows = (keep[extra:] + got[extra:].astype(f32)).astype(bf16)
    given, own_given = got, keep
    places = [[chip * 2 + core for chip in range(tp_size // 2)] for core in range(2)]
    got = lax.all_to_all(
        send_rows, "tp", split_axis=0, concat_axis=0, axis_index_groups=places, tiled=True
    )

    def add_shared(a, b, *first):
        return call(
            add_kernel,
            [a, b, *first],
            0,
            shape((extra, width), bf16),
            [],
            extra * width,
            6 * extra * width,
            1,
        )

    outs = (shape((width, LANES), f32), shape((head, width), f32), shape((8, LANES), f32))
    if not ordered:
        outs += (shape((length, width), bf16),)
    d_w_in, d_w_out, mark, *in_order = call(
        functools.partial(weight_kernel, len(pieces), layout, scaling),
        [ids, *pieces, gcat, gated, send_rows],
        1,
        outs,
        [] if ordered else [pltpu.VMEM((length, width), bf16)],
        8 * length * width * BLOCK,
        8 * length * width,
        1,
        vmem=vmem,
    )
    in_order = in_order[0] if in_order else pieces[0]
    shared = add_shared(own_given, given, send_rows)
    step = nz // 2
    while step:
        shared = add_shared(shared, across(shared, 4 * step), send_rows if step > 1 else mark)
        step //= 2
    d_hidden, d_w_bc = call(
        functools.partial(last_kernel, own_rows, scaling),
        [got, in_order, shared, across(shared, 2)],
        0,
        (shape((own_rows, width), bf16), shape((2 * STATE, width), f32)),
        [],
        2 * length * width * LANES,
        4 * length * width,
    )
    return (d_hidden, d_w_in, d_w_out, d_w_bc.T)


def solution(mesh):
    in_specs = (
        P(("ctx", "tp"), None),
        P(None, "tp"),
        P(),
        P("tp", None),
        P("tp"),
        P("tp"),
        P("tp"),
        P(None, "tp"),
        P("tp", None),
        P(("ctx", "tp"), None),
    )
    out_specs = (P(("ctx", "tp"), None), P(None, "tp"), P("tp", None), P())
    body = functools.partial(local, mesh.shape["ctx"], mesh.shape["tp"])
    return jax.shard_map(body, mesh=mesh, in_specs=in_specs, out_specs=out_specs, check_vma=False)
```

```python
import functools
import math

import jax
import jax.numpy as jnp
from jax import lax
from jax.experimental import pallas as pl
from jax.experimental.pallas import tpu as pltpu
from jax.sharding import PartitionSpec as P

STATE = 16
CONV = 4
LANES = 128
BLOCK = 256
TILE_ROWS = 16
f32 = jnp.float32
bf16 = jnp.bfloat16


def dot(a, b):
    return jnp.dot(a, b, preferred_element_type=f32)


def dot_nt(a, b):
    return lax.dot_general(a, b, (((1,), (1,)), ((), ())), preferred_element_type=f32)


def dot_tn(a, b):
    return lax.dot_general(a, b, (((0,), (0,)), ((), ())), preferred_element_type=f32)


def iota(shape, dim):
    return lax.broadcasted_iota(jnp.int32, shape, dim)


def mirror(size):
    return jnp.where(iota((size, size), 0) + iota((size, size), 1) == size - 1, 1.0, 0.0).astype(
        bf16
    )


def split(value, terms):
    parts = []
    for _ in range(terms):
        part = value.astype(bf16)
        parts.append(part)
        value = value - part.astype(f32)
    return parts


def flip_rows(value, flip):
    count = value.shape[0] // BLOCK
    return jnp.concatenate(
        [dot(flip, value[(count - 1 - i) * BLOCK : (count - i) * BLOCK]) for i in range(count)],
        axis=0,
    )


def owners(ids_ref, layout):
    tp_size, own_rows, coords, _ = layout
    z, x, core, ctx = (ids_ref[i] for i in range(4))
    ctx_size = max(c[0] for c in coords) + 1
    for p, (dc, dx, dcore, blocks) in enumerate(coords):
        from_ctx = lax.rem(ctx + dc, ctx_size)
        for k, j in enumerate(blocks):
            owner = ((z ^ j) * 2 + (x ^ dx)) * 2 + (core ^ dcore)
            at = pl.multiple_of((from_ctx * tp_size + owner) * own_rows, own_rows)
            yield p, k, at


def assemble(ids_ref, pieces, h_ref, d_ref, layout):
    own_rows = layout[1]
    for p, k, at in owners(ids_ref, layout):
        piece = pieces[p]
        half = piece.shape[0] // 2
        h_rows = slice(k * own_rows, (k + 1) * own_rows)
        d_rows = slice(half + k * own_rows, half + (k + 1) * own_rows)
        h_ref[pl.ds(at, own_rows), :] = piece[h_rows, :]
        d_ref[pl.ds(at, own_rows), :] = piece[d_rows, :]


def project(pieces, wall_ref, gall_ref):
    h = jnp.concatenate([piece[: piece.shape[0] // 2, :] for piece in pieces], axis=0)
    d = jnp.concatenate([piece[piece.shape[0] // 2 :, :] for piece in pieces], axis=0)
    return dot(h, wall_ref[...]), dot(d, gall_ref[...])


def pack_kernel(n_parts, own_rows, *refs):
    parts, out_ref = refs[:n_parts], refs[-1]
    half = n_parts * own_rows
    for k, ref in enumerate(parts):
        out_ref[k * own_rows : (k + 1) * own_rows, :] = ref[:own_rows, :]
        if ref.shape[0] > own_rows:
            rows = slice(half + k * own_rows, half + (k + 1) * own_rows)
            out_ref[rows, :] = ref[own_rows:, :]


def copy_kernel(value_ref, *refs):
    refs[-1][...] = value_ref[...]


def early_kernel(*refs):
    pieces = refs[:-4]
    wall_ref, gall_ref, proj_ref, grad_ref = refs[-4:]
    proj_ref[...], grad_ref[...] = project(pieces, wall_ref, gall_ref)


def turn_columns(value, flip):
    count = value.shape[1] // BLOCK
    return jnp.concatenate(
        [dot(value[:, (count - 1 - i) * BLOCK : (count - i) * BLOCK], flip) for i in range(count)],
        axis=1,
    )


def prep_kernel(ids_ref, *refs):
    win_ref, wbct_ref, wdt_ref, wout_ref, conv_ref = refs[:5]
    wall_ref, wallt_ref, gall_ref, taps_ref = refs[-4:]
    flip = mirror(BLOCK)
    width = win_ref.shape[0]
    head = wout_ref.shape[0]
    count = width // BLOCK
    shared = 2 * STATE + 1
    for i in range(count):
        cols = slice(i * BLOCK, (i + 1) * BLOCK)
        rows = jnp.concatenate(
            [
                wbct_ref[:, cols].astype(f32),
                wdt_ref[:, cols].astype(f32),
                jnp.zeros((LANES - shared, BLOCK), f32),
            ],
            axis=0,
        )
        block = win_ref[cols, :]
        wall_ref[cols, :LANES] = block
        wall_ref[cols, LANES : 2 * LANES] = jnp.transpose(rows).astype(bf16)
        wallt_ref[:LANES, cols] = jnp.transpose(block.astype(f32)).astype(bf16)
        wallt_ref[LANES : 2 * LANES, cols] = rows.astype(bf16)
        out = jnp.concatenate(
            [wout_ref[:, cols].astype(f32), jnp.zeros((LANES - head, BLOCK), f32)], axis=0
        )
        gall_ref[cols, :LANES] = jnp.transpose(out).astype(bf16)
    for i in range(count):
        cols = slice(i * BLOCK, (i + 1) * BLOCK)
        back = slice((count - 1 - i) * BLOCK, (count - i) * BLOCK)
        wall_ref[cols, 2 * LANES :] = dot(flip, wall_ref[back, : 2 * LANES]).astype(bf16)
        gall_ref[cols, LANES:] = dot(flip, gall_ref[back, :LANES]).astype(bf16)
        wallt_ref[2 * LANES :, cols] = dot(wallt_ref[: 2 * LANES, back], flip).astype(bf16)
    tap = iota((CONV, LANES - head), 0)
    taps_ref[:, :head] = conv_ref[...]
    taps_ref[:, head:] = jnp.where(tap == CONV - 1, 1.0, 0.0)


def own_source(shape, dim, ids_ref, tp_size, own_rows):
    z, x, core, ctx = (ids_ref[i] for i in range(4))
    nz = tp_size // 4
    row = iota(shape, dim)
    block = row // own_rows
    j = block % nz
    dx = 1 - (block // nz) % 2
    dcore = 1 - block // (2 * nz)
    owner = ((z ^ j) * 2 + (x ^ dx)) * 2 + (core ^ dcore)
    return (ctx * tp_size + owner) * own_rows + row % own_rows


def exact(parts, apply):
    return sum(apply(part) for part in parts)


def decay_rate(par_refs):
    return -jnp.exp(jnp.full((1, LANES), par_refs[1][0], f32))


def core_kernel(n_pieces, layout, *refs):
    ids_ref, par_refs = refs[0], refs[1:4]
    pieces = refs[4 : 4 + n_pieces]
    early_refs = refs[4 + n_pieces : 6 + n_pieces]
    wall_ref, wallt_ref, gall_ref, taps_ref = refs[6 + n_pieces : 10 + n_pieces]
    send_ref, keep_ref, gcat_ref, gated_ref = refs[10 + n_pieces : 14 + n_pieces]
    tp_size, own_rows, coords, n_early = layout
    if coords is None:
        proj, grads = early_refs[0][...], early_refs[1][...]
    else:
        proj_ref, grad_ref = refs[14 + n_pieces :]
        parts = [[ref[...] for ref in early_refs], project(pieces, wall_ref, gall_ref)]
        first = 0
        for p, k, at in owners(ids_ref, layout):
            if p == n_early and k == 0:
                first = 0
            source = parts[p >= n_early]
            proj_ref[pl.ds(at, own_rows), :] = source[0][first : first + own_rows]
            grad_ref[pl.ds(at, own_rows), :] = source[1][first : first + own_rows]
            first += own_rows
        proj, grads = proj_ref[...], grad_ref[...]
    length, width = proj.shape[0], wall_ref.shape[0]
    chunks = length // BLOCK
    flip = mirror(BLOCK)
    bias, rate, skip = par_refs[0][0], decay_rate(par_refs), par_refs[2][0]
    lane = iota((1, LANES), 1)
    low = lane < LANES // 2
    causal = iota((BLOCK, BLOCK), 0) >= iota((BLOCK, BLOCK), 1)
    tri = jnp.where(causal, 1.0, 0.0).astype(bf16)
    row_at = iota((length, LANES), 0)

    turned = [proj[:, 2 * LANES : 3 * LANES].astype(bf16)]
    turned += split(proj[:, 3 * LANES :], 3) + split(grads[:, LANES:], 2)
    turned = flip_rows(jnp.concatenate(turned, axis=1), flip)
    turned = [turned[:, i * LANES : (i + 1) * LANES] for i in range(6)]
    strands = (
        (
            proj[:, :LANES].astype(bf16).astype(f32),
            proj[:, LANES : 2 * LANES],
            grads[:, :LANES],
        ),
        (turned[0], turned[1] + turned[2] + turned[3], turned[4] + turned[5]),
    )

    def gates(xz, rest, grad_g):
        pre = taps_ref[CONV - 1 : CONV, :] * xz
        for shift in range(1, CONV):
            moved = jnp.where(row_at >= shift, pltpu.roll(xz, shift, 0), 0.0)
            pre += taps_ref[CONV - 1 - shift : CONV - shift, :] * moved
        sig = jax.nn.sigmoid(pre)
        u = pre * sig
        slope = sig * (1.0 + pre * (1.0 - sig))
        u_other = pltpu.roll(u, LANES // 2, 1)
        raw = jnp.broadcast_to(rest[:, 2 * STATE : 2 * STATE + 1], (length, LANES)) + bias
        dt = jnp.maximum(raw, 0.0) + jnp.log1p(jnp.exp(-jnp.abs(raw)))
        b_all = jnp.where(lane < STATE, rest, 0.0)
        c_all = jnp.where(lane < STATE, pltpu.roll(rest, LANES - STATE, 1), 0.0)
        g_y = jnp.where(low, grad_g * u_other, 0.0)
        return u, slope, u_other, dt, jax.nn.sigmoid(raw), b_all, c_all, dt * u, g_y, grad_g

    def enter_chunk(c, gate, state):
        rows = slice(c * BLOCK, (c + 1) * BLOCK)
        dt, b_all, c_all, w_all = gate[3][rows], gate[5][rows], gate[6][rows], gate[7][rows]
        log_keep = dot(tri, jnp.concatenate(split(dt * rate, 3), axis=1))
        log_keep = log_keep[:, :LANES] + log_keep[:, LANES : 2 * LANES] + log_keep[:, 2 * LANES :]
        across = jnp.transpose(log_keep)[0:1, :]
        gap = jnp.concatenate([log_keep] * (BLOCK // LANES), axis=1) - across
        decay = jnp.exp(jnp.where(causal, gap, -jnp.inf))
        b_low, c_low, w_low = b_all.astype(bf16), c_all.astype(bf16), w_all.astype(bf16)
        mixed = (dot_nt(c_low, b_low) * decay).astype(bf16)
        last = log_keep[BLOCK - 1 : BLOCK, :]
        enter = jnp.exp(log_keep)
        leave = jnp.exp(last - log_keep)
        b_left = (leave * b_all).astype(bf16)
        out = dot(mixed, w_low) + enter * dot(c_low, state.astype(bf16))
        after = jnp.exp(last) * state + dot_tn(b_left, w_low)
        return out, decay, mixed, b_low, c_low, w_low, b_left, enter, leave, last, state, after

    def leave_chunk(c, gate, saved, d_state):
        rows = slice(c * BLOCK, (c + 1) * BLOCK)
        u, c_all, w_all, gy = gate[0][rows], gate[6][rows], gate[7][rows], gate[8][rows]
        out, decay, mixed, b_low, c_low, w_low, b_left, enter, leave, last, before, after = saved
        gy_low = gy.astype(bf16)
        ds_low = d_state.astype(bf16)
        dw = dot_tn(mixed, gy_low) + dot(b_left, ds_low)
        d_scores = (dot_nt(gy_low, w_low) * decay).astype(bf16)
        g_c = dot(d_scores, b_low) + enter * dot_nt(gy_low, before.astype(bf16))
        g_b = dot_tn(d_scores, c_low) + leave * dot_nt(w_low, ds_low)
        d_log = jnp.sum(jnp.where(low, gy * out - w_all * dw, 0.0), axis=1, keepdims=True)
        at_end = jnp.sum(jnp.where(low, after * d_state, 0.0))
        d_log = jnp.broadcast_to(d_log, (BLOCK, LANES))
        d_sum = dot_tn(tri, jnp.concatenate(split(d_log, 2), axis=1))
        d_sum = d_sum[:, :LANES] + d_sum[:, LANES:] + at_end
        g_a = rate * d_sum + jnp.sum(jnp.where(low, u * dw, 0.0), axis=1, keepdims=True)
        carried = (enter * c_all).astype(bf16)
        return dw, g_b, g_c, g_a, jnp.exp(last) * d_state + dot_tn(carried, gy_low)

    gate = [gates(*strand) for strand in strands]
    saved = [[], []]
    state = [jnp.zeros((LANES, LANES), f32)] * 2
    for c in range(chunks):
        for s in range(2):
            saved[s].append(enter_chunk(c, gate[s], state[s]))
            state[s] = saved[s][c][-1]
    state = [jnp.zeros((LANES, LANES), f32)] * 2
    grads = [[None] * chunks, [None] * chunks]
    for c in reversed(range(chunks)):
        for s in range(2):
            *grads[s][c], state[s] = leave_chunk(c, gate[s], saved[s][c], state[s])
    small = []
    for s in range(2):
        u, slope, u_other, dt, dt_slope, _, _, _, g_y, grad_g = gate[s]
        y = jnp.concatenate([part[0] for part in saved[s]], axis=0) + skip * u
        gated = jnp.where(low, y * u_other, 0.0).astype(bf16)
        g_gate = jnp.where(low, grad_g * y, 0.0)
        d_w, g_b, g_c, g_a = (
            jnp.concatenate([part[i] for part in grads[s]], axis=0) for i in range(4)
        )
        g_raw = g_a * dt_slope
        d_u = jnp.where(low, skip * g_y + dt * d_w, pltpu.roll(g_gate, LANES // 2, 1))
        d_pre = d_u * slope
        g_xz = taps_ref[CONV - 1 : CONV, :] * d_pre
        for shift in range(1, CONV):
            moved = jnp.where(
                row_at < length - shift, pltpu.roll(d_pre, length - shift, 0), 0.0
            )
            g_xz += taps_ref[CONV - 1 - shift : CONV - shift, :] * moved
        shared = jnp.where(lane < STATE, g_b, 0.0) + jnp.where(
            (lane >= STATE) & (lane < 2 * STATE), pltpu.roll(g_c, STATE, 1), 0.0
        )
        g_rest = shared + jnp.where(lane == 2 * STATE, g_raw, 0.0)
        result = jnp.concatenate([g_xz.astype(bf16), g_rest.astype(bf16), gated], axis=1)
        small.append(shared)
        if s == 1:
            result = flip_rows(result, flip).astype(bf16)
        gcat_ref[:, 2 * s * LANES : 2 * (s + 1) * LANES] = result[:, : 2 * LANES]
        gated_ref[:, s * LANES : (s + 1) * LANES] = result[:, 2 * LANES :]

    pair = small[0] + pltpu.roll(small[1], 2 * STATE, 1)
    shared_t = jnp.transpose(pair)[: 4 * STATE].astype(bf16)
    groups = width // length
    step = 4 * STATE // groups
    for i in range(groups):
        part = shared_t[i * step : (i + 1) * step, :]
        send_ref[0:step, i * length : (i + 1) * length] = part
        keep_ref[0:step, i * length : (i + 1) * length] = part.astype(f32)
    own = tp_size * own_rows
    source = own_source((own, length), 0, ids_ref, tp_size, own_rows)
    pick = jnp.where(source == iota((own, length), 1), 1.0, 0.0).astype(bf16)
    picked = dot(pick, gcat_ref[...]).astype(bf16)
    half = own // 2
    part = dot(picked, wallt_ref[...])
    send_ref[step:, :] = part[:half].astype(bf16)
    keep_ref[step:, :] = part[half:]


def weight_kernel(n_pieces, layout, scaling, *refs):
    ids_ref = refs[0]
    pieces = refs[1 : 1 + n_pieces]
    gcat_ref, gated_ref, _, dwin_ref, dwout_ref, mark_ref = refs[1 + n_pieces : 7 + n_pieces]
    mark_ref[...] = jnp.zeros_like(mark_ref)
    if layout[2] is None:
        h_ref, d_ref = pieces
    else:
        h_ref, d_ref = refs[7 + n_pieces :]
        assemble(ids_ref, pieces, h_ref, d_ref, layout)
    flip = mirror(BLOCK)
    columns = h_ref.shape[1] // BLOCK
    head = dwout_ref.shape[0]
    g_f = gcat_ref[:, 0:LANES]
    g_r = gcat_ref[:, 2 * LANES : 3 * LANES]
    y_f = gated_ref[:, 0:LANES]
    y_r = gated_ref[:, LANES:]
    for i in range(columns):
        cols = slice(i * BLOCK, (i + 1) * BLOCK)
        back = slice((columns - 1 - i) * BLOCK, (columns - i) * BLOCK)
        turned = dot(h_ref[:, back], flip).astype(bf16)
        grad = dot_tn(g_f, h_ref[:, cols]) + dot_tn(g_r, turned)
        dwin_ref[cols, :] = jnp.transpose(grad * scaling)
        turned = dot(d_ref[:, back], flip).astype(bf16)
        grad = dot_tn(y_f, d_ref[:, cols]) + dot_tn(y_r, turned)
        dwout_ref[:, cols] = grad[:head] * scaling


def add_kernel(a_ref, b_ref, _, out_ref):
    rows = slice(0, out_ref.shape[0])
    out_ref[...] = (a_ref[rows, :].astype(f32) + b_ref[rows, :].astype(f32)).astype(bf16)


def stage_kernel(own_rows, keep_ref, got_ref, own_ref, *piece_refs):
    for j, ref in enumerate([own_ref, *piece_refs]):
        rows = slice(j * own_rows, (j + 1) * own_rows)
        value = keep_ref[rows, :] + got_ref[rows, :].astype(f32)
        ref[...] = value.astype(ref.dtype)


def last_kernel(scaling, own_ref, h_ref, shared_ref, other_ref, *refs):
    got_refs, (dhid_ref, dwbct_ref) = refs[:-2], refs[-2:]
    flip = mirror(BLOCK)
    length, width = h_ref.shape
    groups = width // length
    total = own_ref[...]
    for got in got_refs:
        total += got[...].astype(f32)
    dhid_ref[...] = total.astype(bf16)
    shared = (shared_ref[...].astype(f32) + other_ref[...].astype(f32)).astype(bf16)
    shared = jnp.concatenate(
        [shared[:, i * length : (i + 1) * length] for i in range(groups)], axis=0
    )
    fwd = shared[: 2 * STATE]
    rev = turn_columns(shared[2 * STATE :], flip).astype(bf16)
    pairs = dot(jnp.concatenate([fwd, rev], axis=0), h_ref[...])
    turned = exact(split(pairs[2 * STATE :], 3), lambda part: turn_columns(part, flip))
    dwbct_ref[...] = (pairs[: 2 * STATE] + turned) * scaling


def spec(memory=pltpu.VMEM):
    return pl.BlockSpec(memory_space=memory)


def call(kernel, inputs, n_smem, outs, scratch, flops, moved, unread=0, vmem=32):
    return pl.pallas_call(
        kernel,
        out_shape=outs,
        in_specs=[spec(pltpu.SMEM)] * n_smem
        + [spec()] * (len(inputs) - n_smem - unread)
        + [spec(pl.ANY)] * unread,
        out_specs=jax.tree.map(lambda _: spec(), outs),
        scratch_shapes=scratch,
        compiler_params=pltpu.CompilerParams(vmem_limit_bytes=vmem * 1024 * 1024),
        cost_estimate=pl.CostEstimate(flops=flops, bytes_accessed=moved, transcendentals=0),
    )(*inputs)


def shape(dims, dtype):
    return jax.ShapeDtypeStruct(dims, dtype)


def local(ctx_size, tp_size, hidden, w_in, w_bc, w_dt, dt_bias, a_log, d_skip, conv_w, w_out, d_out):
    own_rows, width = hidden.shape
    length = own_rows * tp_size * ctx_size
    head = w_out.shape[0]
    nz = tp_size // 4
    chunks = length // BLOCK
    t = lax.axis_index("tp")
    ids = jnp.stack([t >> 2, (t >> 1) & 1, t & 1, lax.axis_index("ctx")]).astype(jnp.int32)
    params = [dt_bias, a_log, d_skip]
    def across(value, flip_bits):
        return lax.ppermute(value, "tp", [(i, i ^ flip_bits) for i in range(tp_size)])

    def along(value):
        return lax.ppermute(value, "ctx", [(0, 1), (1, 0)])

    def prepare(*begun):
        return call(
            prep_kernel,
            [ids, w_in, w_bc.T, w_dt, w_out, conv_w, *begun],
            1,
            (
                shape((width, 4 * LANES), bf16),
                shape((4 * LANES, width), bf16),
                shape((width, 2 * LANES), bf16),
                shape((CONV, LANES), f32),
            ),
            [],
            6 * width * BLOCK * BLOCK,
            20 * width * LANES,
            len(begun),
        )

    def pack(parts, *first):
        rows = sum(part.shape[0] for part in parts)
        return call(
            functools.partial(pack_kernel, len(parts), own_rows),
            [*parts, *first],
            0,
            shape((rows, width), bf16),
            [],
            0,
            4 * rows * width,
            len(first),
        )

    def after(value, *first):
        return call(
            copy_kernel,
            [value, *first],
            0,
            shape(value.shape, bf16),
            [],
            0,
            4 * value.size,
            len(first),
        )

    if own_rows % TILE_ROWS == 0 and (ctx_size, nz) == (2, 4):
        low = jnp.array(-jnp.inf, bf16)
        own = jnp.maximum(
            lax.pad(hidden, low, [(0, own_rows, 0), (0, 0, 0)]),
            lax.pad(d_out, low, [(own_rows, 0, 0), (0, 0, 0)]),
        )
        z_near, z_far = across(own, 4), across(own, 8)
        chunk_a = pack([own, z_near])
        chunk_b = pack([z_far, across(z_far, 4)])
        direct = [[part, across(part, 2), along(part)] for part in (chunk_a, chunk_b)]
        (_, a_x, a_c), (_, b_x, b_c) = direct
        beside_a = [across(part, 1) for part in direct[0]]
        wall, wallt, gall, taps = prepare(chunk_b)
        a_d = across(after(a_c, a_x, b_x, b_c, *beside_a), 2)
        b_d = along(after(b_x, a_x, a_c, b_c, *beside_a))
        beside = [beside_a, [across(part, 1) for part in direct[1]]]
        early, coords = [], []
        blocks = ((0, 1), (2, 3))
        for g in range(2):
            for place, part, other in zip(((0, 0), (0, 1), (1, 0)), direct[g], beside[g]):
                early += [part, other]
                coords += [(*place, 0, blocks[g]), (*place, 1, blocks[g])]
        coords += [(1, 1, core, blocks[g]) for g in range(2) for core in range(2)]
        layout = (tp_size, own_rows, tuple(coords), len(early))
        late, pieces = None, None
    else:
        pieces = [lax.all_gather(a, ("ctx", "tp"), axis=0, tiled=True) for a in (hidden, d_out)]
        layout = (tp_size, own_rows, None, 0)
        wall, wallt, gall, taps = prepare()
        early, late = [jnp.concatenate(pieces, axis=0)], []
    ordered = layout[2] is None
    vmem = 60 if ordered else 32
    early_rows = sum(piece.shape[0] for piece in early) // 2
    projected = call(
        early_kernel,
        [*early, wall, gall],
        0,
        (shape((early_rows, 4 * LANES), f32), shape((early_rows, 2 * LANES), f32)),
        [],
        2 * early_rows * width * 6 * LANES,
        4 * early_rows * width,
        vmem=vmem,
    )
    if not ordered:
        late = [a_d, across(after(a_d, projected[0]), 1), b_d, across(b_d, 1)]
        pieces = early + late
    extra = 4 * STATE * length // width
    half = tp_size * own_rows // 2
    send, keep, gcat, gated = call(
        functools.partial(core_kernel, len(late), layout),
        [ids, *params, *late, *projected, wall, wallt, gall, taps],
        4,
        (
            shape((extra + half, width), bf16),
            shape((extra + half, width), f32),
            shape((length, 4 * LANES), bf16),
            shape((length, 2 * LANES), bf16),
        ),
        []
        if ordered
        else [pltpu.VMEM((length, 4 * LANES), f32), pltpu.VMEM((length, 2 * LANES), f32)],
        8 * length * width * BLOCK,
        8 * length * width,
        vmem=vmem,
    )
    scaling = 1.0 / math.sqrt(length)
    got = across(send, 1)
    quarter = half // 2
    at = extra + quarter
    given, own_given = got, keep
    send = (keep[extra:at] + got[extra:at].astype(f32)).astype(bf16)
    keep = keep[at:] + got[at:].astype(f32)
    sent = send
    got = across(send, 2)

    def add_shared(a, b, *first):
        return call(
            add_kernel,
            [a, b, *first],
            0,
            shape((extra, width), bf16),
            [],
            extra * width,
            6 * extra * width,
            1,
        )

    outs = (shape((width, LANES), f32), shape((head, width), f32), shape((8, LANES), f32))
    if not ordered:
        outs += (shape((length, width), bf16),)
    d_w_in, d_w_out, mark, *in_order = call(
        functools.partial(weight_kernel, len(pieces), layout, scaling),
        [ids, *pieces, gcat, gated, send],
        1,
        outs,
        [] if ordered else [pltpu.VMEM((length, width), bf16)],
        8 * length * width * BLOCK,
        8 * length * width,
        1,
        vmem=vmem,
    )
    in_order = in_order[0] if in_order else pieces[0]
    own, *send = call(
        functools.partial(stage_kernel, own_rows),
        [keep, got],
        0,
        (shape((own_rows, width), f32),) + (shape((own_rows, width), bf16),) * (nz - 1),
        [],
        4 * quarter * width,
        10 * quarter * width,
    )
    shared = add_shared(own_given, given, sent)
    step = nz // 2
    while step:
        shared = add_shared(shared, across(shared, 4 * step), mark if step > 1 else own)
        step //= 2
    got = [across(piece, 4 * (j + 1)) for j, piece in enumerate(send)]
    d_hidden, d_w_bc = call(
        functools.partial(last_kernel, scaling),
        [own, in_order, shared, across(shared, 2), *got],
        0,
        (shape((own_rows, width), bf16), shape((2 * STATE, width), f32)),
        [],
        2 * length * width * LANES,
        4 * length * width,
    )
    return (d_hidden, d_w_in, d_w_out, d_w_bc.T)


def solution(mesh):
    in_specs = (
        P(("ctx", "tp"), None),
        P(None, "tp"),
        P(),
        P("tp", None),
        P("tp"),
        P("tp"),
        P("tp"),
        P(None, "tp"),
        P("tp", None),
        P(("ctx", "tp"), None),
    )
    out_specs = (P(("ctx", "tp"), None), P(None, "tp"), P("tp", None), P())
    body = functools.partial(local, mesh.shape["ctx"], mesh.shape["tp"])
    return jax.shard_map(body, mesh=mesh, in_specs=in_specs, out_specs=out_specs, check_vma=False)
```

```python
import functools
import math

import jax
import jax.numpy as jnp
from jax import lax
from jax.experimental import pallas as pl
from jax.experimental.pallas import tpu as pltpu
from jax.sharding import PartitionSpec as P

STATE = 16
CONV = 4
LANES = 128
BLOCK = 256
TILE_ROWS = 16
f32 = jnp.float32
bf16 = jnp.bfloat16


def dot(a, b):
    return jnp.dot(a, b, preferred_element_type=f32)


def dot_nt(a, b):
    return lax.dot_general(a, b, (((1,), (1,)), ((), ())), preferred_element_type=f32)


def dot_tn(a, b):
    return lax.dot_general(a, b, (((0,), (0,)), ((), ())), preferred_element_type=f32)


def iota(shape, dim):
    return lax.broadcasted_iota(jnp.int32, shape, dim)


def mirror(size):
    return jnp.where(iota((size, size), 0) + iota((size, size), 1) == size - 1, 1.0, 0.0).astype(
        bf16
    )


def split(value, terms):
    parts = []
    for _ in range(terms):
        part = value.astype(bf16)
        parts.append(part)
        value = value - part.astype(f32)
    return parts


def flip_rows(value, flip):
    count = value.shape[0] // BLOCK
    return jnp.concatenate(
        [dot(flip, value[(count - 1 - i) * BLOCK : (count - i) * BLOCK]) for i in range(count)],
        axis=0,
    )


def owners(ids_ref, layout):
    tp_size, own_rows, coords, _ = layout
    z, x, core, ctx = (ids_ref[i] for i in range(4))
    ctx_size = max(c[0] for c in coords) + 1
    for p, (dc, dx, dcore, blocks) in enumerate(coords):
        from_ctx = lax.rem(ctx + dc, ctx_size)
        for k, j in enumerate(blocks):
            owner = ((z ^ j) * 2 + (x ^ dx)) * 2 + (core ^ dcore)
            at = pl.multiple_of((from_ctx * tp_size + owner) * own_rows, own_rows)
            yield p, k, at


def assemble(ids_ref, pieces, h_ref, d_ref, layout):
    own_rows = layout[1]
    for p, k, at in owners(ids_ref, layout):
        piece = pieces[p]
        half = piece.shape[0] // 2
        h_rows = slice(k * own_rows, (k + 1) * own_rows)
        d_rows = slice(half + k * own_rows, half + (k + 1) * own_rows)
        h_ref[pl.ds(at, own_rows), :] = piece[h_rows, :]
        d_ref[pl.ds(at, own_rows), :] = piece[d_rows, :]


def project(pieces, wall_ref, gall_ref):
    h = jnp.concatenate([piece[: piece.shape[0] // 2, :] for piece in pieces], axis=0)
    d = jnp.concatenate([piece[piece.shape[0] // 2 :, :] for piece in pieces], axis=0)
    return dot(h, wall_ref[...]), dot(d, gall_ref[...])


def pack_kernel(n_parts, own_rows, *refs):
    parts, out_ref = refs[:n_parts], refs[-1]
    half = n_parts * own_rows
    for k, ref in enumerate(parts):
        out_ref[k * own_rows : (k + 1) * own_rows, :] = ref[:own_rows, :]
        if ref.shape[0] > own_rows:
            rows = slice(half + k * own_rows, half + (k + 1) * own_rows)
            out_ref[rows, :] = ref[own_rows:, :]


def copy_kernel(value_ref, *refs):
    refs[-1][...] = value_ref[...]


def early_kernel(*refs):
    pieces = refs[:-4]
    wall_ref, gall_ref, proj_ref, grad_ref = refs[-4:]
    proj_ref[...], grad_ref[...] = project(pieces, wall_ref, gall_ref)


def turn_columns(value, flip):
    count = value.shape[1] // BLOCK
    return jnp.concatenate(
        [dot(value[:, (count - 1 - i) * BLOCK : (count - i) * BLOCK], flip) for i in range(count)],
        axis=1,
    )


def prep_kernel(ids_ref, *refs):
    win_ref, wbct_ref, wdt_ref, wout_ref, conv_ref = refs[:5]
    wall_ref, wallt_ref, gall_ref, taps_ref = refs[-4:]
    flip = mirror(BLOCK)
    width = win_ref.shape[0]
    head = wout_ref.shape[0]
    count = width // BLOCK
    shared = 2 * STATE + 1
    for i in range(count):
        cols = slice(i * BLOCK, (i + 1) * BLOCK)
        rows = jnp.concatenate(
            [
                wbct_ref[:, cols].astype(f32),
                wdt_ref[:, cols].astype(f32),
                jnp.zeros((LANES - shared, BLOCK), f32),
            ],
            axis=0,
        )
        block = win_ref[cols, :]
        wall_ref[cols, :LANES] = block
        wall_ref[cols, LANES : 2 * LANES] = jnp.transpose(rows).astype(bf16)
        wallt_ref[:LANES, cols] = jnp.transpose(block.astype(f32)).astype(bf16)
        wallt_ref[LANES : 2 * LANES, cols] = rows.astype(bf16)
        out = jnp.concatenate(
            [wout_ref[:, cols].astype(f32), jnp.zeros((LANES - head, BLOCK), f32)], axis=0
        )
        gall_ref[cols, :LANES] = jnp.transpose(out).astype(bf16)
    for i in range(count):
        cols = slice(i * BLOCK, (i + 1) * BLOCK)
        back = slice((count - 1 - i) * BLOCK, (count - i) * BLOCK)
        wall_ref[cols, 2 * LANES :] = dot(flip, wall_ref[back, : 2 * LANES]).astype(bf16)
        gall_ref[cols, LANES:] = dot(flip, gall_ref[back, :LANES]).astype(bf16)
        wallt_ref[2 * LANES :, cols] = dot(wallt_ref[: 2 * LANES, back], flip).astype(bf16)
    tap = iota((CONV, LANES - head), 0)
    taps_ref[:, :head] = conv_ref[...]
    taps_ref[:, head:] = jnp.where(tap == CONV - 1, 1.0, 0.0)


def own_source(shape, dim, ids_ref, tp_size, own_rows):
    z, x, core, ctx = (ids_ref[i] for i in range(4))
    nz = tp_size // 4
    row = iota(shape, dim)
    block = row // own_rows
    j = block % nz
    dx = 1 - (block // nz) % 2
    dcore = 1 - block // (2 * nz)
    owner = ((z ^ j) * 2 + (x ^ dx)) * 2 + (core ^ dcore)
    return (ctx * tp_size + owner) * own_rows + row % own_rows


def exact(parts, apply):
    return sum(apply(part) for part in parts)


def decay_rate(par_refs):
    return -jnp.exp(jnp.full((1, LANES), par_refs[1][0], f32))


def core_kernel(n_pieces, layout, *refs):
    ids_ref, par_refs = refs[0], refs[1:4]
    pieces = refs[4 : 4 + n_pieces]
    early_refs = refs[4 + n_pieces : 6 + n_pieces]
    wall_ref, wallt_ref, gall_ref, taps_ref = refs[6 + n_pieces : 10 + n_pieces]
    send_ref, keep_ref, gcat_ref, gated_ref = refs[10 + n_pieces : 14 + n_pieces]
    tp_size, own_rows, coords, n_early = layout
    if coords is None:
        proj, grads = early_refs[0][...], early_refs[1][...]
    else:
        proj_ref, grad_ref = refs[14 + n_pieces :]
        parts = [[ref[...] for ref in early_refs], project(pieces, wall_ref, gall_ref)]
        first = 0
        for p, k, at in owners(ids_ref, layout):
            if p == n_early and k == 0:
                first = 0
            source = parts[p >= n_early]
            proj_ref[pl.ds(at, own_rows), :] = source[0][first : first + own_rows]
            grad_ref[pl.ds(at, own_rows), :] = source[1][first : first + own_rows]
            first += own_rows
        proj, grads = proj_ref[...], grad_ref[...]
    length, width = proj.shape[0], wall_ref.shape[0]
    chunks = length // BLOCK
    flip = mirror(BLOCK)
    bias, rate, skip = par_refs[0][0], decay_rate(par_refs), par_refs[2][0]
    lane = iota((1, LANES), 1)
    low = lane < LANES // 2
    causal = iota((BLOCK, BLOCK), 0) >= iota((BLOCK, BLOCK), 1)
    tri = jnp.where(causal, 1.0, 0.0).astype(bf16)
    row_at = iota((length, LANES), 0)

    turned = [proj[:, 2 * LANES : 3 * LANES].astype(bf16)]
    turned += split(proj[:, 3 * LANES :], 3) + split(grads[:, LANES:], 2)
    turned = flip_rows(jnp.concatenate(turned, axis=1), flip)
    turned = [turned[:, i * LANES : (i + 1) * LANES] for i in range(6)]
    strands = (
        (
            proj[:, :LANES].astype(bf16).astype(f32),
            proj[:, LANES : 2 * LANES],
            grads[:, :LANES],
        ),
        (turned[0], turned[1] + turned[2] + turned[3], turned[4] + turned[5]),
    )

    def gates(xz, rest, grad_g):
        pre = taps_ref[CONV - 1 : CONV, :] * xz
        for shift in range(1, CONV):
            moved = jnp.where(row_at >= shift, pltpu.roll(xz, shift, 0), 0.0)
            pre += taps_ref[CONV - 1 - shift : CONV - shift, :] * moved
        sig = jax.nn.sigmoid(pre)
        u = pre * sig
        slope = sig * (1.0 + pre * (1.0 - sig))
        u_other = pltpu.roll(u, LANES // 2, 1)
        raw = jnp.broadcast_to(rest[:, 2 * STATE : 2 * STATE + 1], (length, LANES)) + bias
        dt = jnp.maximum(raw, 0.0) + jnp.log1p(jnp.exp(-jnp.abs(raw)))
        b_all = jnp.where(lane < STATE, rest, 0.0)
        c_all = jnp.where(lane < STATE, pltpu.roll(rest, LANES - STATE, 1), 0.0)
        g_y = jnp.where(low, grad_g * u_other, 0.0)
        return u, slope, u_other, dt, jax.nn.sigmoid(raw), b_all, c_all, dt * u, g_y, grad_g

    def enter_chunk(c, gate, state):
        rows = slice(c * BLOCK, (c + 1) * BLOCK)
        dt, b_all, c_all, w_all = gate[3][rows], gate[5][rows], gate[6][rows], gate[7][rows]
        log_keep = dot(tri, jnp.concatenate(split(dt * rate, 3), axis=1))
        log_keep = log_keep[:, :LANES] + log_keep[:, LANES : 2 * LANES] + log_keep[:, 2 * LANES :]
        across = jnp.transpose(log_keep)[0:1, :]
        gap = jnp.concatenate([log_keep] * (BLOCK // LANES), axis=1) - across
        decay = jnp.exp(jnp.where(causal, gap, -jnp.inf))
        b_low, c_low, w_low = b_all.astype(bf16), c_all.astype(bf16), w_all.astype(bf16)
        mixed = (dot_nt(c_low, b_low) * decay).astype(bf16)
        last = log_keep[BLOCK - 1 : BLOCK, :]
        enter = jnp.exp(log_keep)
        leave = jnp.exp(last - log_keep)
        b_left = (leave * b_all).astype(bf16)
        out = dot(mixed, w_low) + enter * dot(c_low, state.astype(bf16))
        after = jnp.exp(last) * state + dot_tn(b_left, w_low)
        return out, decay, mixed, b_low, c_low, w_low, b_left, enter, leave, last, state, after

    def leave_chunk(c, gate, saved, d_state):
        rows = slice(c * BLOCK, (c + 1) * BLOCK)
        u, c_all, w_all, gy = gate[0][rows], gate[6][rows], gate[7][rows], gate[8][rows]
        out, decay, mixed, b_low, c_low, w_low, b_left, enter, leave, last, before, after = saved
        gy_low = gy.astype(bf16)
        ds_low = d_state.astype(bf16)
        dw = dot_tn(mixed, gy_low) + dot(b_left, ds_low)
        d_scores = (dot_nt(gy_low, w_low) * decay).astype(bf16)
        g_c = dot(d_scores, b_low) + enter * dot_nt(gy_low, before.astype(bf16))
        g_b = dot_tn(d_scores, c_low) + leave * dot_nt(w_low, ds_low)
        d_log = jnp.sum(jnp.where(low, gy * out - w_all * dw, 0.0), axis=1, keepdims=True)
        at_end = jnp.sum(jnp.where(low, after * d_state, 0.0))
        d_log = jnp.broadcast_to(d_log, (BLOCK, LANES))
        d_sum = dot_tn(tri, jnp.concatenate(split(d_log, 2), axis=1))
        d_sum = d_sum[:, :LANES] + d_sum[:, LANES:] + at_end
        g_a = rate * d_sum + jnp.sum(jnp.where(low, u * dw, 0.0), axis=1, keepdims=True)
        carried = (enter * c_all).astype(bf16)
        return dw, g_b, g_c, g_a, jnp.exp(last) * d_state + dot_tn(carried, gy_low)

    gate = [gates(*strand) for strand in strands]
    saved = [[], []]
    state = [jnp.zeros((LANES, LANES), f32)] * 2
    for c in range(chunks):
        for s in range(2):
            saved[s].append(enter_chunk(c, gate[s], state[s]))
            state[s] = saved[s][c][-1]
    state = [jnp.zeros((LANES, LANES), f32)] * 2
    grads = [[None] * chunks, [None] * chunks]
    for c in reversed(range(chunks)):
        for s in range(2):
            *grads[s][c], state[s] = leave_chunk(c, gate[s], saved[s][c], state[s])
    small = []
    for s in range(2):
        u, slope, u_other, dt, dt_slope, _, _, _, g_y, grad_g = gate[s]
        y = jnp.concatenate([part[0] for part in saved[s]], axis=0) + skip * u
        gated = jnp.where(low, y * u_other, 0.0).astype(bf16)
        g_gate = jnp.where(low, grad_g * y, 0.0)
        d_w, g_b, g_c, g_a = (
            jnp.concatenate([part[i] for part in grads[s]], axis=0) for i in range(4)
        )
        g_raw = g_a * dt_slope
        d_u = jnp.where(low, skip * g_y + dt * d_w, pltpu.roll(g_gate, LANES // 2, 1))
        d_pre = d_u * slope
        g_xz = taps_ref[CONV - 1 : CONV, :] * d_pre
        for shift in range(1, CONV):
            moved = jnp.where(
                row_at < length - shift, pltpu.roll(d_pre, length - shift, 0), 0.0
            )
            g_xz += taps_ref[CONV - 1 - shift : CONV - shift, :] * moved
        shared = jnp.where(lane < STATE, g_b, 0.0) + jnp.where(
            (lane >= STATE) & (lane < 2 * STATE), pltpu.roll(g_c, STATE, 1), 0.0
        )
        g_rest = shared + jnp.where(lane == 2 * STATE, g_raw, 0.0)
        result = jnp.concatenate([g_xz.astype(bf16), g_rest.astype(bf16), gated], axis=1)
        small.append(shared)
        if s == 1:
            result = flip_rows(result, flip).astype(bf16)
        gcat_ref[:, 2 * s * LANES : 2 * (s + 1) * LANES] = result[:, : 2 * LANES]
        gated_ref[:, s * LANES : (s + 1) * LANES] = result[:, 2 * LANES :]

    pair = small[0] + pltpu.roll(small[1], 2 * STATE, 1)
    shared_t = jnp.transpose(pair)[: 4 * STATE].astype(bf16)
    groups = width // length
    step = 4 * STATE // groups
    for i in range(groups):
        part = shared_t[i * step : (i + 1) * step, :]
        send_ref[0:step, i * length : (i + 1) * length] = part
        keep_ref[0:step, i * length : (i + 1) * length] = part.astype(f32)
    own = tp_size * own_rows
    source = own_source((own, length), 0, ids_ref, tp_size, own_rows)
    pick = jnp.where(source == iota((own, length), 1), 1.0, 0.0).astype(bf16)
    picked = dot(pick, gcat_ref[...]).astype(bf16)
    half = own // 2
    part = dot(picked, wallt_ref[...])
    send_ref[step:, :] = part[:half].astype(bf16)
    keep_ref[step:, :] = part[half:]


def weight_kernel(n_pieces, layout, scaling, *refs):
    ids_ref = refs[0]
    pieces = refs[1 : 1 + n_pieces]
    gcat_ref, gated_ref, _, dwin_ref, dwout_ref, mark_ref = refs[1 + n_pieces : 7 + n_pieces]
    mark_ref[...] = jnp.zeros_like(mark_ref)
    if layout[2] is None:
        h_ref, d_ref = pieces
    else:
        h_ref, d_ref = refs[7 + n_pieces :]
        assemble(ids_ref, pieces, h_ref, d_ref, layout)
    flip = mirror(BLOCK)
    columns = h_ref.shape[1] // BLOCK
    head = dwout_ref.shape[0]
    g_f = gcat_ref[:, 0:LANES]
    g_r = gcat_ref[:, 2 * LANES : 3 * LANES]
    y_f = gated_ref[:, 0:LANES]
    y_r = gated_ref[:, LANES:]
    for i in range(columns):
        cols = slice(i * BLOCK, (i + 1) * BLOCK)
        back = slice((columns - 1 - i) * BLOCK, (columns - i) * BLOCK)
        turned = dot(h_ref[:, back], flip).astype(bf16)
        grad = dot_tn(g_f, h_ref[:, cols]) + dot_tn(g_r, turned)
        dwin_ref[cols, :] = jnp.transpose(grad * scaling)
        turned = dot(d_ref[:, back], flip).astype(bf16)
        grad = dot_tn(y_f, d_ref[:, cols]) + dot_tn(y_r, turned)
        dwout_ref[:, cols] = grad[:head] * scaling


def add_kernel(a_ref, b_ref, _, out_ref):
    rows = slice(0, out_ref.shape[0])
    out_ref[...] = (a_ref[rows, :].astype(f32) + b_ref[rows, :].astype(f32)).astype(bf16)


def stage_kernel(own_rows, keep_ref, got_ref, own_ref, *piece_refs):
    for j, ref in enumerate([own_ref, *piece_refs]):
        rows = slice(j * own_rows, (j + 1) * own_rows)
        value = keep_ref[rows, :] + got_ref[rows, :].astype(f32)
        ref[...] = value.astype(ref.dtype)


def last_kernel(scaling, own_ref, h_ref, shared_ref, other_ref, *refs):
    got_refs, (dhid_ref, dwbct_ref) = refs[:-2], refs[-2:]
    flip = mirror(BLOCK)
    length, width = h_ref.shape
    groups = width // length
    total = own_ref[...]
    for got in got_refs:
        total += got[...].astype(f32)
    dhid_ref[...] = total.astype(bf16)
    shared = (shared_ref[...].astype(f32) + other_ref[...].astype(f32)).astype(bf16)
    shared = jnp.concatenate(
        [shared[:, i * length : (i + 1) * length] for i in range(groups)], axis=0
    )
    fwd = shared[: 2 * STATE]
    rev = turn_columns(shared[2 * STATE :], flip).astype(bf16)
    pairs = dot(jnp.concatenate([fwd, rev], axis=0), h_ref[...])
    turned = exact(split(pairs[2 * STATE :], 3), lambda part: turn_columns(part, flip))
    dwbct_ref[...] = (pairs[: 2 * STATE] + turned) * scaling


def spec(memory=pltpu.VMEM):
    return pl.BlockSpec(memory_space=memory)


def call(kernel, inputs, n_smem, outs, scratch, flops, moved, unread=0, vmem=32):
    return pl.pallas_call(
        kernel,
        out_shape=outs,
        in_specs=[spec(pltpu.SMEM)] * n_smem
        + [spec()] * (len(inputs) - n_smem - unread)
        + [spec(pl.ANY)] * unread,
        out_specs=jax.tree.map(lambda _: spec(), outs),
        scratch_shapes=scratch,
        compiler_params=pltpu.CompilerParams(vmem_limit_bytes=vmem * 1024 * 1024),
        cost_estimate=pl.CostEstimate(flops=flops, bytes_accessed=moved, transcendentals=0),
    )(*inputs)


def shape(dims, dtype):
    return jax.ShapeDtypeStruct(dims, dtype)


def local(ctx_size, tp_size, hidden, w_in, w_bc, w_dt, dt_bias, a_log, d_skip, conv_w, w_out, d_out):
    own_rows, width = hidden.shape
    length = own_rows * tp_size * ctx_size
    head = w_out.shape[0]
    nz = tp_size // 4
    chunks = length // BLOCK
    t = lax.axis_index("tp")
    ids = jnp.stack([t >> 2, (t >> 1) & 1, t & 1, lax.axis_index("ctx")]).astype(jnp.int32)
    params = [dt_bias, a_log, d_skip]
    def across(value, flip_bits):
        return lax.ppermute(value, "tp", [(i, i ^ flip_bits) for i in range(tp_size)])

    def along(value):
        return lax.ppermute(value, "ctx", [(0, 1), (1, 0)])

    def prepare(*begun):
        return call(
            prep_kernel,
            [ids, w_in, w_bc.T, w_dt, w_out, conv_w, *begun],
            1,
            (
                shape((width, 4 * LANES), bf16),
                shape((4 * LANES, width), bf16),
                shape((width, 2 * LANES), bf16),
                shape((CONV, LANES), f32),
            ),
            [],
            6 * width * BLOCK * BLOCK,
            20 * width * LANES,
            len(begun),
        )

    def pack(parts, *first):
        rows = sum(part.shape[0] for part in parts)
        return call(
            functools.partial(pack_kernel, len(parts), own_rows),
            [*parts, *first],
            0,
            shape((rows, width), bf16),
            [],
            0,
            4 * rows * width,
            len(first),
        )

    def after(value, *first):
        return call(
            copy_kernel,
            [value, *first],
            0,
            shape(value.shape, bf16),
            [],
            0,
            4 * value.size,
            len(first),
        )

    if own_rows % TILE_ROWS == 0 and (ctx_size, nz) == (2, 4):
        low = jnp.array(-jnp.inf, bf16)
        own = jnp.maximum(
            lax.pad(hidden, low, [(0, own_rows, 0), (0, 0, 0)]),
            lax.pad(d_out, low, [(own_rows, 0, 0), (0, 0, 0)]),
        )
        z_near, z_far = across(own, 4), across(own, 8)
        own_x, own_c = across(own, 2), along(own)
        own_d = along(own_x)
        last = across(z_far, 4)
        pair = pack([z_near, z_far], own_d, own_c)
        pair_c, pair_x = along(pair), across(pair, 2)
        last_x, last_c = across(last, 2), along(last)
        groups = (
            ((0,), (own, own_x, own_c, own_d)),
            ((1, 2), (pair, pair_x, pair_c)),
            ((3,), (last, last_x, last_c)),
        )
        early, coords = [], []
        for blocks, parts in groups:
            for place, part in zip(((0, 0), (0, 1), (1, 0), (1, 1)), parts):
                early += [part, across(part, 1)]
                coords += [(*place, core, blocks) for core in range(2)]
        wall, wallt, gall, taps = prepare(pair)
        pair_d = across(after(pair_c, pair_x, *early[1:8:2]), 2)
        last_d = along(after(last_x, pair_x, pair_c, *early[1:8:2]))
        coords += [(1, 1, core, blocks) for blocks, _ in groups[1:] for core in range(2)]
        layout = (tp_size, own_rows, tuple(coords), len(early))
        late, pieces = None, None
    else:
        pieces = [lax.all_gather(a, ("ctx", "tp"), axis=0, tiled=True) for a in (hidden, d_out)]
        layout = (tp_size, own_rows, None, 0)
        wall, wallt, gall, taps = prepare()
        early, late = [jnp.concatenate(pieces, axis=0)], []
    ordered = layout[2] is None
    vmem = 60 if ordered else 32
    early_rows = sum(piece.shape[0] for piece in early) // 2
    projected = call(
        early_kernel,
        [*early, wall, gall],
        0,
        (shape((early_rows, 4 * LANES), f32), shape((early_rows, 2 * LANES), f32)),
        [],
        2 * early_rows * width * 6 * LANES,
        4 * early_rows * width,
        vmem=vmem,
    )
    if not ordered:
        last_other = across(after(last_d, projected[0]), 1)
        late = [pair_d, across(pair_d, 1), last_d, last_other]
        pieces = early + late
    extra = 4 * STATE * length // width
    half = tp_size * own_rows // 2
    send, keep, gcat, gated = call(
        functools.partial(core_kernel, len(late), layout),
        [ids, *params, *late, *projected, wall, wallt, gall, taps],
        4,
        (
            shape((extra + half, width), bf16),
            shape((extra + half, width), f32),
            shape((length, 4 * LANES), bf16),
            shape((length, 2 * LANES), bf16),
        ),
        []
        if ordered
        else [pltpu.VMEM((length, 4 * LANES), f32), pltpu.VMEM((length, 2 * LANES), f32)],
        8 * length * width * BLOCK,
        8 * length * width,
        vmem=vmem,
    )
    scaling = 1.0 / math.sqrt(length)
    got = across(send, 1)
    quarter = half // 2
    at = extra + quarter
    given, own_given = got, keep
    send = (keep[extra:at] + got[extra:at].astype(f32)).astype(bf16)
    keep = keep[at:] + got[at:].astype(f32)
    sent = send
    got = across(send, 2)

    def add_shared(a, b, *first):
        return call(
            add_kernel,
            [a, b, *first],
            0,
            shape((extra, width), bf16),
            [],
            extra * width,
            6 * extra * width,
            1,
        )

    outs = (shape((width, LANES), f32), shape((head, width), f32), shape((8, LANES), f32))
    if not ordered:
        outs += (shape((length, width), bf16),)
    d_w_in, d_w_out, mark, *in_order = call(
        functools.partial(weight_kernel, len(pieces), layout, scaling),
        [ids, *pieces, gcat, gated, send],
        1,
        outs,
        [] if ordered else [pltpu.VMEM((length, width), bf16)],
        8 * length * width * BLOCK,
        8 * length * width,
        1,
        vmem=vmem,
    )
    in_order = in_order[0] if in_order else pieces[0]
    own, *send = call(
        functools.partial(stage_kernel, own_rows),
        [keep, got],
        0,
        (shape((own_rows, width), f32),) + (shape((own_rows, width), bf16),) * (nz - 1),
        [],
        4 * quarter * width,
        10 * quarter * width,
    )
    shared = add_shared(own_given, given, sent)
    step = nz // 2
    while step:
        shared = add_shared(shared, across(shared, 4 * step), mark if step > 1 else own)
        step //= 2
    got = [across(piece, 4 * (j + 1)) for j, piece in enumerate(send)]
    d_hidden, d_w_bc = call(
        functools.partial(last_kernel, scaling),
        [own, in_order, shared, across(shared, 2), *got],
        0,
        (shape((own_rows, width), bf16), shape((2 * STATE, width), f32)),
        [],
        2 * length * width * LANES,
        4 * length * width,
    )
    return (d_hidden, d_w_in, d_w_out, d_w_bc.T)


def solution(mesh):
    in_specs = (
        P(("ctx", "tp"), None),
        P(None, "tp"),
        P(),
        P("tp", None),
        P("tp"),
        P("tp"),
        P("tp"),
        P(None, "tp"),
        P("tp", None),
        P(("ctx", "tp"), None),
    )
    out_specs = (P(("ctx", "tp"), None), P(None, "tp"), P("tp", None), P())
    body = functools.partial(local, mesh.shape["ctx"], mesh.shape["tp"])
    return jax.shard_map(body, mesh=mesh, in_specs=in_specs, out_specs=out_specs, check_vma=False)
```

```python
import functools
import math

import jax
import jax.numpy as jnp
from jax import lax
from jax.experimental import pallas as pl
from jax.experimental.pallas import tpu as pltpu
from jax.sharding import PartitionSpec as P

STATE = 16
CONV = 4
LANES = 128
BLOCK = 256
TILE_ROWS = 16
f32 = jnp.float32
bf16 = jnp.bfloat16


def dot(a, b):
    return jnp.dot(a, b, preferred_element_type=f32)


def dot_nt(a, b):
    return lax.dot_general(a, b, (((1,), (1,)), ((), ())), preferred_element_type=f32)


def dot_tn(a, b):
    return lax.dot_general(a, b, (((0,), (0,)), ((), ())), preferred_element_type=f32)


def iota(shape, dim):
    return lax.broadcasted_iota(jnp.int32, shape, dim)


def mirror(size):
    return jnp.where(iota((size, size), 0) + iota((size, size), 1) == size - 1, 1.0, 0.0).astype(
        bf16
    )


def split(value, terms):
    parts = []
    for _ in range(terms):
        part = value.astype(bf16)
        parts.append(part)
        value = value - part.astype(f32)
    return parts


def flip_rows(value, flip):
    count = value.shape[0] // BLOCK
    return jnp.concatenate(
        [dot(flip, value[(count - 1 - i) * BLOCK : (count - i) * BLOCK]) for i in range(count)],
        axis=0,
    )


def owners(ids_ref, layout):
    tp_size, own_rows, coords, _ = layout
    z, x, core, ctx = (ids_ref[i] for i in range(4))
    ctx_size = max(c[0] for c in coords) + 1
    for p, (dc, dx, dcore, blocks) in enumerate(coords):
        from_ctx = lax.rem(ctx + dc, ctx_size)
        for k, j in enumerate(blocks):
            owner = ((z ^ j) * 2 + (x ^ dx)) * 2 + (core ^ dcore)
            at = pl.multiple_of((from_ctx * tp_size + owner) * own_rows, own_rows)
            yield p, k, at


def assemble(ids_ref, pieces, h_ref, d_ref, layout):
    own_rows = layout[1]
    for p, k, at in owners(ids_ref, layout):
        piece = pieces[p]
        half = piece.shape[0] // 2
        h_rows = slice(k * own_rows, (k + 1) * own_rows)
        d_rows = slice(half + k * own_rows, half + (k + 1) * own_rows)
        h_ref[pl.ds(at, own_rows), :] = piece[h_rows, :]
        d_ref[pl.ds(at, own_rows), :] = piece[d_rows, :]


def project(pieces, wall_ref, gall_ref):
    h = jnp.concatenate([piece[: piece.shape[0] // 2, :] for piece in pieces], axis=0)
    d = jnp.concatenate([piece[piece.shape[0] // 2 :, :] for piece in pieces], axis=0)
    return dot(h, wall_ref[...]), dot(d, gall_ref[...])


def pack_kernel(n_parts, own_rows, *refs):
    parts, out_ref = refs[:n_parts], refs[-1]
    half = n_parts * own_rows
    for k, ref in enumerate(parts):
        out_ref[k * own_rows : (k + 1) * own_rows, :] = ref[:own_rows, :]
        if ref.shape[0] > own_rows:
            rows = slice(half + k * own_rows, half + (k + 1) * own_rows)
            out_ref[rows, :] = ref[own_rows:, :]


def copy_kernel(value_ref, *refs):
    refs[-1][...] = value_ref[...]


def early_kernel(*refs):
    pieces = refs[:-4]
    wall_ref, gall_ref, proj_ref, grad_ref = refs[-4:]
    proj_ref[...], grad_ref[...] = project(pieces, wall_ref, gall_ref)


def turn_columns(value, flip):
    count = value.shape[1] // BLOCK
    return jnp.concatenate(
        [dot(value[:, (count - 1 - i) * BLOCK : (count - i) * BLOCK], flip) for i in range(count)],
        axis=1,
    )


def prep_kernel(ids_ref, *refs):
    win_ref, wbct_ref, wdt_ref, wout_ref, conv_ref = refs[:5]
    wall_ref, wallt_ref, gall_ref, taps_ref = refs[-4:]
    flip = mirror(BLOCK)
    width = win_ref.shape[0]
    head = wout_ref.shape[0]
    count = width // BLOCK
    shared = 2 * STATE + 1
    for i in range(count):
        cols = slice(i * BLOCK, (i + 1) * BLOCK)
        rows = jnp.concatenate(
            [
                wbct_ref[:, cols].astype(f32),
                wdt_ref[:, cols].astype(f32),
                jnp.zeros((LANES - shared, BLOCK), f32),
            ],
            axis=0,
        )
        block = win_ref[cols, :]
        wall_ref[cols, :LANES] = block
        wall_ref[cols, LANES : 2 * LANES] = jnp.transpose(rows).astype(bf16)
        wallt_ref[:LANES, cols] = jnp.transpose(block.astype(f32)).astype(bf16)
        wallt_ref[LANES : 2 * LANES, cols] = rows.astype(bf16)
        out = jnp.concatenate(
            [wout_ref[:, cols].astype(f32), jnp.zeros((LANES - head, BLOCK), f32)], axis=0
        )
        gall_ref[cols, :LANES] = jnp.transpose(out).astype(bf16)
    for i in range(count):
        cols = slice(i * BLOCK, (i + 1) * BLOCK)
        back = slice((count - 1 - i) * BLOCK, (count - i) * BLOCK)
        wall_ref[cols, 2 * LANES :] = dot(flip, wall_ref[back, : 2 * LANES]).astype(bf16)
        gall_ref[cols, LANES:] = dot(flip, gall_ref[back, :LANES]).astype(bf16)
        wallt_ref[2 * LANES :, cols] = dot(wallt_ref[: 2 * LANES, back], flip).astype(bf16)
    tap = iota((CONV, LANES - head), 0)
    taps_ref[:, :head] = conv_ref[...]
    taps_ref[:, head:] = jnp.where(tap == CONV - 1, 1.0, 0.0)


def own_source(shape, dim, ids_ref, tp_size, own_rows):
    z, x, core, ctx = (ids_ref[i] for i in range(4))
    nz = tp_size // 4
    row = iota(shape, dim)
    block = row // own_rows
    j = block % nz
    dx = 1 - (block // nz) % 2
    dcore = 1 - block // (2 * nz)
    owner = ((z ^ j) * 2 + (x ^ dx)) * 2 + (core ^ dcore)
    return (ctx * tp_size + owner) * own_rows + row % own_rows


def exact(parts, apply):
    return sum(apply(part) for part in parts)


def decay_rate(par_refs):
    return -jnp.exp(jnp.full((1, LANES), par_refs[1][0], f32))


def core_kernel(n_pieces, layout, *refs):
    ids_ref, par_refs = refs[0], refs[1:4]
    pieces = refs[4 : 4 + n_pieces]
    early_refs = refs[4 + n_pieces : 6 + n_pieces]
    wall_ref, wallt_ref, gall_ref, taps_ref = refs[6 + n_pieces : 10 + n_pieces]
    send_ref, keep_ref, gcat_ref, gated_ref = refs[10 + n_pieces : 14 + n_pieces]
    tp_size, own_rows, coords, n_early = layout
    if coords is None:
        proj, grads = early_refs[0][...], early_refs[1][...]
    else:
        proj_ref, grad_ref = refs[14 + n_pieces :]
        parts = [[ref[...] for ref in early_refs], project(pieces, wall_ref, gall_ref)]
        first = 0
        for p, k, at in owners(ids_ref, layout):
            if p == n_early and k == 0:
                first = 0
            source = parts[p >= n_early]
            proj_ref[pl.ds(at, own_rows), :] = source[0][first : first + own_rows]
            grad_ref[pl.ds(at, own_rows), :] = source[1][first : first + own_rows]
            first += own_rows
        proj, grads = proj_ref[...], grad_ref[...]
    length, width = proj.shape[0], wall_ref.shape[0]
    chunks = length // BLOCK
    flip = mirror(BLOCK)
    bias, rate, skip = par_refs[0][0], decay_rate(par_refs), par_refs[2][0]
    lane = iota((1, LANES), 1)
    low = lane < LANES // 2
    causal = iota((BLOCK, BLOCK), 0) >= iota((BLOCK, BLOCK), 1)
    tri = jnp.where(causal, 1.0, 0.0).astype(bf16)
    row_at = iota((length, LANES), 0)

    turned = [proj[:, 2 * LANES : 3 * LANES].astype(bf16)]
    turned += split(proj[:, 3 * LANES :], 2) + split(grads[:, LANES:], 2)
    turned = flip_rows(jnp.concatenate(turned, axis=1), flip)
    turned = [turned[:, i * LANES : (i + 1) * LANES] for i in range(5)]
    strands = (
        (
            proj[:, :LANES].astype(bf16).astype(f32),
            proj[:, LANES : 2 * LANES],
            grads[:, :LANES],
        ),
        (turned[0], turned[1] + turned[2], turned[3] + turned[4]),
    )

    def gates(xz, rest, grad_g):
        pre = taps_ref[CONV - 1 : CONV, :] * xz
        for shift in range(1, CONV):
            moved = jnp.where(row_at >= shift, pltpu.roll(xz, shift, 0), 0.0)
            pre += taps_ref[CONV - 1 - shift : CONV - shift, :] * moved
        sig = jax.nn.sigmoid(pre)
        u = pre * sig
        slope = sig * (1.0 + pre * (1.0 - sig))
        u_other = pltpu.roll(u, LANES // 2, 1)
        raw = jnp.broadcast_to(rest[:, 2 * STATE : 2 * STATE + 1], (length, LANES)) + bias
        dt = jnp.maximum(raw, 0.0) + jnp.log1p(jnp.exp(-jnp.abs(raw)))
        b_all = jnp.where(lane < STATE, rest, 0.0)
        c_all = jnp.where(lane < STATE, pltpu.roll(rest, LANES - STATE, 1), 0.0)
        g_y = jnp.where(low, grad_g * u_other, 0.0)
        return u, slope, u_other, dt, jax.nn.sigmoid(raw), b_all, c_all, dt * u, g_y, grad_g

    def enter_chunk(c, gate, state):
        rows = slice(c * BLOCK, (c + 1) * BLOCK)
        dt, b_all, c_all, w_all = gate[3][rows], gate[5][rows], gate[6][rows], gate[7][rows]
        log_keep = dot(tri, jnp.concatenate(split(dt * rate, 2), axis=1))
        log_keep = log_keep[:, :LANES] + log_keep[:, LANES:]
        across = jnp.transpose(log_keep)[0:1, :]
        gap = jnp.concatenate([log_keep] * (BLOCK // LANES), axis=1) - across
        decay = jnp.exp(jnp.where(causal, gap, -jnp.inf))
        b_low, c_low, w_low = b_all.astype(bf16), c_all.astype(bf16), w_all.astype(bf16)
        mixed = (dot_nt(c_low, b_low) * decay).astype(bf16)
        last = log_keep[BLOCK - 1 : BLOCK, :]
        enter = jnp.exp(log_keep)
        leave = jnp.exp(last - log_keep)
        b_left = (leave * b_all).astype(bf16)
        out = dot(mixed, w_low) + enter * dot(c_low, state.astype(bf16))
        after = jnp.exp(last) * state + dot_tn(b_left, w_low)
        return out, decay, mixed, b_low, c_low, w_low, b_left, enter, leave, last, state, after

    def leave_chunk(c, gate, saved, d_state):
        rows = slice(c * BLOCK, (c + 1) * BLOCK)
        u, c_all, w_all, gy = gate[0][rows], gate[6][rows], gate[7][rows], gate[8][rows]
        out, decay, mixed, b_low, c_low, w_low, b_left, enter, leave, last, before, after = saved
        gy_low = gy.astype(bf16)
        ds_low = d_state.astype(bf16)
        dw = dot_tn(mixed, gy_low) + dot(b_left, ds_low)
        d_scores = (dot_nt(gy_low, w_low) * decay).astype(bf16)
        g_c = dot(d_scores, b_low) + enter * dot_nt(gy_low, before.astype(bf16))
        g_b = dot_tn(d_scores, c_low) + leave * dot_nt(w_low, ds_low)
        d_log = jnp.sum(jnp.where(low, gy * out - w_all * dw, 0.0), axis=1, keepdims=True)
        at_end = jnp.sum(jnp.where(low, after * d_state, 0.0))
        d_log = jnp.broadcast_to(d_log, (BLOCK, LANES))
        d_sum = dot_tn(tri, jnp.concatenate(split(d_log, 2), axis=1))
        d_sum = d_sum[:, :LANES] + d_sum[:, LANES:] + at_end
        g_a = rate * d_sum + jnp.sum(jnp.where(low, u * dw, 0.0), axis=1, keepdims=True)
        carried = (enter * c_all).astype(bf16)
        return dw, g_b, g_c, g_a, jnp.exp(last) * d_state + dot_tn(carried, gy_low)

    gate = [gates(*strand) for strand in strands]
    saved = [[], []]
    state = [jnp.zeros((LANES, LANES), f32)] * 2
    for c in range(chunks):
        for s in range(2):
            saved[s].append(enter_chunk(c, gate[s], state[s]))
            state[s] = saved[s][c][-1]
    state = [jnp.zeros((LANES, LANES), f32)] * 2
    grads = [[None] * chunks, [None] * chunks]
    for c in reversed(range(chunks)):
        for s in range(2):
            *grads[s][c], state[s] = leave_chunk(c, gate[s], saved[s][c], state[s])
    small = []
    for s in range(2):
        u, slope, u_other, dt, dt_slope, _, _, _, g_y, grad_g = gate[s]
        y = jnp.concatenate([part[0] for part in saved[s]], axis=0) + skip * u
        gated = jnp.where(low, y * u_other, 0.0).astype(bf16)
        g_gate = jnp.where(low, grad_g * y, 0.0)
        d_w, g_b, g_c, g_a = (
            jnp.concatenate([part[i] for part in grads[s]], axis=0) for i in range(4)
        )
        g_raw = g_a * dt_slope
        d_u = jnp.where(low, skip * g_y + dt * d_w, pltpu.roll(g_gate, LANES // 2, 1))
        d_pre = d_u * slope
        g_xz = taps_ref[CONV - 1 : CONV, :] * d_pre
        for shift in range(1, CONV):
            moved = jnp.where(
                row_at < length - shift, pltpu.roll(d_pre, length - shift, 0), 0.0
            )
            g_xz += taps_ref[CONV - 1 - shift : CONV - shift, :] * moved
        shared = jnp.where(lane < STATE, g_b, 0.0) + jnp.where(
            (lane >= STATE) & (lane < 2 * STATE), pltpu.roll(g_c, STATE, 1), 0.0
        )
        g_rest = shared + jnp.where(lane == 2 * STATE, g_raw, 0.0)
        result = jnp.concatenate([g_xz.astype(bf16), g_rest.astype(bf16), gated], axis=1)
        small.append(shared)
        if s == 1:
            result = flip_rows(result, flip).astype(bf16)
        gcat_ref[:, 2 * s * LANES : 2 * (s + 1) * LANES] = result[:, : 2 * LANES]
        gated_ref[:, s * LANES : (s + 1) * LANES] = result[:, 2 * LANES :]

    pair = small[0] + pltpu.roll(small[1], 2 * STATE, 1)
    shared_t = jnp.transpose(pair)[: 4 * STATE].astype(bf16)
    groups = width // length
    step = 4 * STATE // groups
    for i in range(groups):
        part = shared_t[i * step : (i + 1) * step, :]
        send_ref[0:step, i * length : (i + 1) * length] = part
        keep_ref[0:step, i * length : (i + 1) * length] = part.astype(f32)
    own = tp_size * own_rows
    source = own_source((own, length), 0, ids_ref, tp_size, own_rows)
    pick = jnp.where(source == iota((own, length), 1), 1.0, 0.0).astype(bf16)
    picked = dot(pick, gcat_ref[...]).astype(bf16)
    half = own // 2
    part = dot(picked, wallt_ref[...])
    send_ref[step:, :] = part[:half].astype(bf16)
    keep_ref[step:, :] = part[half:]


def weight_kernel(n_pieces, layout, scaling, *refs):
    ids_ref = refs[0]
    pieces = refs[1 : 1 + n_pieces]
    gcat_ref, gated_ref, _, dwin_ref, dwout_ref, mark_ref = refs[1 + n_pieces : 7 + n_pieces]
    mark_ref[...] = jnp.zeros_like(mark_ref)
    if layout[2] is None:
        h_ref, d_ref = pieces
    else:
        h_ref, d_ref = refs[7 + n_pieces :]
        assemble(ids_ref, pieces, h_ref, d_ref, layout)
    flip = mirror(BLOCK)
    columns = h_ref.shape[1] // BLOCK
    head = dwout_ref.shape[0]
    g_f = gcat_ref[:, 0:LANES]
    g_r = gcat_ref[:, 2 * LANES : 3 * LANES]
    y_f = gated_ref[:, 0:LANES]
    y_r = gated_ref[:, LANES:]
    for i in range(columns):
        cols = slice(i * BLOCK, (i + 1) * BLOCK)
        back = slice((columns - 1 - i) * BLOCK, (columns - i) * BLOCK)
        turned = dot(h_ref[:, back], flip).astype(bf16)
        grad = dot_tn(g_f, h_ref[:, cols]) + dot_tn(g_r, turned)
        dwin_ref[cols, :] = jnp.transpose(grad * scaling)
        turned = dot(d_ref[:, back], flip).astype(bf16)
        grad = dot_tn(y_f, d_ref[:, cols]) + dot_tn(y_r, turned)
        dwout_ref[:, cols] = grad[:head] * scaling


def add_kernel(a_ref, b_ref, _, out_ref):
    rows = slice(0, out_ref.shape[0])
    out_ref[...] = (a_ref[rows, :].astype(f32) + b_ref[rows, :].astype(f32)).astype(bf16)


def stage_kernel(own_rows, keep_ref, got_ref, own_ref, *piece_refs):
    for j, ref in enumerate([own_ref, *piece_refs]):
        rows = slice(j * own_rows, (j + 1) * own_rows)
        value = keep_ref[rows, :] + got_ref[rows, :].astype(f32)
        ref[...] = value.astype(ref.dtype)


def sum_kernel(own_ref, *refs):
    total = own_ref[...]
    for got in refs[:-2]:
        total += got[...].astype(f32)
    refs[-1][...] = total.astype(bf16)


def shared_kernel(scaling, h_ref, shared_ref, other_ref, dwbct_ref, mark_ref):
    mark_ref[...] = jnp.zeros_like(mark_ref)
    flip = mirror(BLOCK)
    length, width = h_ref.shape
    groups = width // length
    shared = (shared_ref[...].astype(f32) + other_ref[...].astype(f32)).astype(bf16)
    shared = jnp.concatenate(
        [shared[:, i * length : (i + 1) * length] for i in range(groups)], axis=0
    )
    fwd = shared[: 2 * STATE]
    rev = turn_columns(shared[2 * STATE :], flip).astype(bf16)
    pairs = dot(jnp.concatenate([fwd, rev], axis=0), h_ref[...])
    turned = exact(split(pairs[2 * STATE :], 2), lambda part: turn_columns(part, flip))
    dwbct_ref[...] = (pairs[: 2 * STATE] + turned) * scaling


def spec(memory=pltpu.VMEM):
    return pl.BlockSpec(memory_space=memory)


def call(kernel, inputs, n_smem, outs, scratch, flops, moved, unread=0, vmem=32):
    return pl.pallas_call(
        kernel,
        out_shape=outs,
        in_specs=[spec(pltpu.SMEM)] * n_smem
        + [spec()] * (len(inputs) - n_smem - unread)
        + [spec(pl.ANY)] * unread,
        out_specs=jax.tree.map(lambda _: spec(), outs),
        scratch_shapes=scratch,
        compiler_params=pltpu.CompilerParams(vmem_limit_bytes=vmem * 1024 * 1024),
        cost_estimate=pl.CostEstimate(flops=flops, bytes_accessed=moved, transcendentals=0),
    )(*inputs)


def shape(dims, dtype):
    return jax.ShapeDtypeStruct(dims, dtype)


def local(ctx_size, tp_size, hidden, w_in, w_bc, w_dt, dt_bias, a_log, d_skip, conv_w, w_out, d_out):
    own_rows, width = hidden.shape
    length = own_rows * tp_size * ctx_size
    head = w_out.shape[0]
    nz = tp_size // 4
    chunks = length // BLOCK
    t = lax.axis_index("tp")
    ids = jnp.stack([t >> 2, (t >> 1) & 1, t & 1, lax.axis_index("ctx")]).astype(jnp.int32)
    params = [dt_bias, a_log, d_skip]
    def across(value, flip_bits):
        return lax.ppermute(value, "tp", [(i, i ^ flip_bits) for i in range(tp_size)])

    def along(value):
        return lax.ppermute(value, "ctx", [(0, 1), (1, 0)])

    def prepare(*begun):
        return call(
            prep_kernel,
            [ids, w_in, w_bc.T, w_dt, w_out, conv_w, *begun],
            1,
            (
                shape((width, 4 * LANES), bf16),
                shape((4 * LANES, width), bf16),
                shape((width, 2 * LANES), bf16),
                shape((CONV, LANES), f32),
            ),
            [],
            6 * width * BLOCK * BLOCK,
            20 * width * LANES,
            len(begun),
        )

    def pack(parts, *first):
        rows = sum(part.shape[0] for part in parts)
        return call(
            functools.partial(pack_kernel, len(parts), own_rows),
            [*parts, *first],
            0,
            shape((rows, width), bf16),
            [],
            0,
            4 * rows * width,
            len(first),
        )

    def after(value, *first):
        return call(
            copy_kernel,
            [value, *first],
            0,
            shape(value.shape, bf16),
            [],
            0,
            4 * value.size,
            len(first),
        )

    if own_rows % TILE_ROWS == 0 and (ctx_size, nz) == (2, 4):
        low = jnp.array(-jnp.inf, bf16)
        own = jnp.maximum(
            lax.pad(hidden, low, [(0, own_rows, 0), (0, 0, 0)]),
            lax.pad(d_out, low, [(own_rows, 0, 0), (0, 0, 0)]),
        )
        z_near, z_far = across(own, 4), across(own, 8)
        chunk_a = pack([own, z_near])
        chunk_b = pack([z_far, across(z_far, 4)])
        direct = [[part, across(part, 2), along(part)] for part in (chunk_a, chunk_b)]
        (_, a_x, a_c), (_, b_x, b_c) = direct
        beside_a = [across(part, 1) for part in direct[0]]
        wall, wallt, gall, taps = prepare(chunk_b)
        a_d = across(after(a_c, a_x, b_x, b_c, *beside_a), 2)
        b_d = along(after(b_x, a_x, a_c, b_c, *beside_a))
        beside = [beside_a, [across(part, 1) for part in direct[1]]]
        early, coords = [], []
        blocks = ((0, 1), (2, 3))
        for g in range(2):
            for place, part, other in zip(((0, 0), (0, 1), (1, 0)), direct[g], beside[g]):
                early += [part, other]
                coords += [(*place, 0, blocks[g]), (*place, 1, blocks[g])]
        coords += [(1, 1, core, blocks[g]) for g in range(2) for core in range(2)]
        layout = (tp_size, own_rows, tuple(coords), len(early))
        late, pieces = None, None
    else:
        pieces = [lax.all_gather(a, ("ctx", "tp"), axis=0, tiled=True) for a in (hidden, d_out)]
        layout = (tp_size, own_rows, None, 0)
        wall, wallt, gall, taps = prepare()
        early, late = [jnp.concatenate(pieces, axis=0)], []
    ordered = layout[2] is None
    vmem = 60 if ordered else 32
    early_rows = sum(piece.shape[0] for piece in early) // 2
    projected = call(
        early_kernel,
        [*early, wall, gall],
        0,
        (shape((early_rows, 4 * LANES), f32), shape((early_rows, 2 * LANES), f32)),
        [],
        2 * early_rows * width * 6 * LANES,
        4 * early_rows * width,
        vmem=vmem,
    )
    if not ordered:
        late = [a_d, across(after(a_d, projected[0]), 1), b_d, across(b_d, 1)]
        pieces = early + late
    extra = 4 * STATE * length // width
    half = tp_size * own_rows // 2
    send, keep, gcat, gated = call(
        functools.partial(core_kernel, len(late), layout),
        [ids, *params, *late, *projected, wall, wallt, gall, taps],
        4,
        (
            shape((extra + half, width), bf16),
            shape((extra + half, width), f32),
            shape((length, 4 * LANES), bf16),
            shape((length, 2 * LANES), bf16),
        ),
        []
        if ordered
        else [pltpu.VMEM((length, 4 * LANES), f32), pltpu.VMEM((length, 2 * LANES), f32)],
        8 * length * width * BLOCK,
        8 * length * width,
        vmem=vmem,
    )
    scaling = 1.0 / math.sqrt(length)
    got = across(send, 1)
    quarter = half // 2
    at = extra + quarter
    given, own_given = got, keep
    send = (keep[extra:at] + got[extra:at].astype(f32)).astype(bf16)
    keep = keep[at:] + got[at:].astype(f32)
    sent = send
    got = across(send, 2)

    def add_shared(a, b, *first):
        return call(
            add_kernel,
            [a, b, *first],
            0,
            shape((extra, width), bf16),
            [],
            extra * width,
            6 * extra * width,
            1,
        )

    outs = (shape((width, LANES), f32), shape((head, width), f32), shape((8, LANES), f32))
    if not ordered:
        outs += (shape((length, width), bf16),)
    d_w_in, d_w_out, mark, *in_order = call(
        functools.partial(weight_kernel, len(pieces), layout, scaling),
        [ids, *pieces, gcat, gated, send],
        1,
        outs,
        [] if ordered else [pltpu.VMEM((length, width), bf16)],
        8 * length * width * BLOCK,
        8 * length * width,
        1,
        vmem=vmem,
    )
    in_order = in_order[0] if in_order else pieces[0]
    own, *send = call(
        functools.partial(stage_kernel, own_rows),
        [keep, got],
        0,
        (shape((own_rows, width), f32),) + (shape((own_rows, width), bf16),) * (nz - 1),
        [],
        4 * quarter * width,
        10 * quarter * width,
    )
    got = [across(piece, 4 * (j + 1)) for j, piece in enumerate(send)]
    shared = add_shared(own_given, given, sent)
    step = nz // 2
    while step:
        shared = add_shared(shared, across(shared, 4 * step), mark if step > 1 else got[0])
        step //= 2
    d_w_bc, mark = call(
        functools.partial(shared_kernel, scaling),
        [in_order, shared, across(shared, 2)],
        0,
        (shape((2 * STATE, width), f32), shape((8, LANES), f32)),
        [],
        2 * length * width * LANES,
        4 * length * width,
    )
    d_hidden = call(
        sum_kernel,
        [own, *got, mark],
        0,
        shape((own_rows, width), bf16),
        [],
        4 * own_rows * width,
        12 * own_rows * width,
        1,
    )
    return (d_hidden, d_w_in, d_w_out, d_w_bc.T)


def solution(mesh):
    in_specs = (
        P(("ctx", "tp"), None),
        P(None, "tp"),
        P(),
        P("tp", None),
        P("tp"),
        P("tp"),
        P("tp"),
        P(None, "tp"),
        P("tp", None),
        P(("ctx", "tp"), None),
    )
    out_specs = (P(("ctx", "tp"), None), P(None, "tp"), P("tp", None), P())
    body = functools.partial(local, mesh.shape["ctx"], mesh.shape["tp"])
    return jax.shard_map(body, mesh=mesh, in_specs=in_specs, out_specs=out_specs, check_vma=False)
```

```python
import functools
import math

import jax
import jax.numpy as jnp
from jax import lax
from jax.experimental import pallas as pl
from jax.experimental.pallas import tpu as pltpu
from jax.sharding import PartitionSpec as P

STATE = 16
CONV = 4
LANES = 128
BLOCK = 256
TILE_ROWS = 16
f32 = jnp.float32
bf16 = jnp.bfloat16


def dot(a, b):
    return jnp.dot(a, b, preferred_element_type=f32)


def dot_nt(a, b):
    return lax.dot_general(a, b, (((1,), (1,)), ((), ())), preferred_element_type=f32)


def dot_tn(a, b):
    return lax.dot_general(a, b, (((0,), (0,)), ((), ())), preferred_element_type=f32)


def iota(shape, dim):
    return lax.broadcasted_iota(jnp.int32, shape, dim)


def mirror(size):
    return jnp.where(iota((size, size), 0) + iota((size, size), 1) == size - 1, 1.0, 0.0).astype(
        bf16
    )


def split(value, terms):
    parts = []
    for _ in range(terms):
        part = value.astype(bf16)
        parts.append(part)
        value = value - part.astype(f32)
    return parts


def flip_rows(value, flip):
    count = value.shape[0] // BLOCK
    return jnp.concatenate(
        [dot(flip, value[(count - 1 - i) * BLOCK : (count - i) * BLOCK]) for i in range(count)],
        axis=0,
    )


def owners(ids_ref, layout):
    tp_size, own_rows, coords, _ = layout
    z, x, core, ctx = (ids_ref[i] for i in range(4))
    ctx_size = max(c[0] for c in coords) + 1
    for p, (dc, dx, dcore, blocks) in enumerate(coords):
        from_ctx = lax.rem(ctx + dc, ctx_size)
        for k, j in enumerate(blocks):
            owner = ((z ^ j) * 2 + (x ^ dx)) * 2 + (core ^ dcore)
            at = pl.multiple_of((from_ctx * tp_size + owner) * own_rows, own_rows)
            yield p, k, at


def assemble(ids_ref, pieces, h_ref, d_ref, layout):
    own_rows = layout[1]
    for p, k, at in owners(ids_ref, layout):
        piece = pieces[p]
        half = piece.shape[0] // 2
        h_rows = slice(k * own_rows, (k + 1) * own_rows)
        d_rows = slice(half + k * own_rows, half + (k + 1) * own_rows)
        h_ref[pl.ds(at, own_rows), :] = piece[h_rows, :]
        d_ref[pl.ds(at, own_rows), :] = piece[d_rows, :]


def project(pieces, wall_ref, gall_ref):
    h = jnp.concatenate([piece[: piece.shape[0] // 2, :] for piece in pieces], axis=0)
    d = jnp.concatenate([piece[piece.shape[0] // 2 :, :] for piece in pieces], axis=0)
    return dot(h, wall_ref[...]), dot(d, gall_ref[...])


def pack_kernel(n_parts, own_rows, *refs):
    parts, out_ref = refs[:n_parts], refs[-1]
    half = n_parts * own_rows
    for k, ref in enumerate(parts):
        out_ref[k * own_rows : (k + 1) * own_rows, :] = ref[:own_rows, :]
        if ref.shape[0] > own_rows:
            rows = slice(half + k * own_rows, half + (k + 1) * own_rows)
            out_ref[rows, :] = ref[own_rows:, :]


def copy_kernel(value_ref, *refs):
    refs[-1][...] = value_ref[...]


def early_kernel(*refs):
    pieces = refs[:-4]
    wall_ref, gall_ref, proj_ref, grad_ref = refs[-4:]
    proj_ref[...], grad_ref[...] = project(pieces, wall_ref, gall_ref)


def turn_columns(value, flip):
    count = value.shape[1] // BLOCK
    return jnp.concatenate(
        [dot(value[:, (count - 1 - i) * BLOCK : (count - i) * BLOCK], flip) for i in range(count)],
        axis=1,
    )


def prep_kernel(ids_ref, *refs):
    win_ref, wbct_ref, wdt_ref, wout_ref, conv_ref = refs[:5]
    wall_ref, wallt_ref, gall_ref, taps_ref = refs[-4:]
    flip = mirror(BLOCK)
    width = win_ref.shape[0]
    head = wout_ref.shape[0]
    count = width // BLOCK
    shared = 2 * STATE + 1
    for i in range(count):
        cols = slice(i * BLOCK, (i + 1) * BLOCK)
        rows = jnp.concatenate(
            [
                wbct_ref[:, cols].astype(f32),
                wdt_ref[:, cols].astype(f32),
                jnp.zeros((LANES - shared, BLOCK), f32),
            ],
            axis=0,
        )
        block = win_ref[cols, :]
        wall_ref[cols, :LANES] = block
        wall_ref[cols, LANES : 2 * LANES] = jnp.transpose(rows).astype(bf16)
        wallt_ref[:LANES, cols] = jnp.transpose(block.astype(f32)).astype(bf16)
        wallt_ref[LANES : 2 * LANES, cols] = rows.astype(bf16)
        out = jnp.concatenate(
            [wout_ref[:, cols].astype(f32), jnp.zeros((LANES - head, BLOCK), f32)], axis=0
        )
        gall_ref[cols, :LANES] = jnp.transpose(out).astype(bf16)
    for i in range(count):
        cols = slice(i * BLOCK, (i + 1) * BLOCK)
        back = slice((count - 1 - i) * BLOCK, (count - i) * BLOCK)
        wall_ref[cols, 2 * LANES :] = dot(flip, wall_ref[back, : 2 * LANES]).astype(bf16)
        gall_ref[cols, LANES:] = dot(flip, gall_ref[back, :LANES]).astype(bf16)
        wallt_ref[2 * LANES :, cols] = dot(wallt_ref[: 2 * LANES, back], flip).astype(bf16)
    tap = iota((CONV, LANES - head), 0)
    taps_ref[:, :head] = conv_ref[...]
    taps_ref[:, head:] = jnp.where(tap == CONV - 1, 1.0, 0.0)


def own_source(shape, dim, ids_ref, tp_size, own_rows):
    z, x, core, ctx = (ids_ref[i] for i in range(4))
    nz = tp_size // 4
    row = iota(shape, dim)
    block = row // own_rows
    j = block % nz
    dx = 1 - (block // nz) % 2
    dcore = 1 - block // (2 * nz)
    owner = ((z ^ j) * 2 + (x ^ dx)) * 2 + (core ^ dcore)
    return (ctx * tp_size + owner) * own_rows + row % own_rows


def exact(parts, apply):
    return sum(apply(part) for part in parts)


def decay_rate(par_refs):
    return -jnp.exp(jnp.full((1, LANES), par_refs[1][0], f32))


def core_kernel(n_pieces, layout, *refs):
    ids_ref, par_refs = refs[0], refs[1:4]
    pieces = refs[4 : 4 + n_pieces]
    early_refs = refs[4 + n_pieces : 6 + n_pieces]
    wall_ref, wallt_ref, gall_ref, taps_ref = refs[6 + n_pieces : 10 + n_pieces]
    send_ref, keep_ref, gcat_ref, gated_ref = refs[10 + n_pieces : 14 + n_pieces]
    tp_size, own_rows, coords, n_early = layout
    if coords is None:
        proj, grads = early_refs[0][...], early_refs[1][...]
    else:
        proj_ref, grad_ref = refs[14 + n_pieces :]
        parts = [[ref[...] for ref in early_refs], project(pieces, wall_ref, gall_ref)]
        first = 0
        for p, k, at in owners(ids_ref, layout):
            if p == n_early and k == 0:
                first = 0
            source = parts[p >= n_early]
            proj_ref[pl.ds(at, own_rows), :] = source[0][first : first + own_rows]
            grad_ref[pl.ds(at, own_rows), :] = source[1][first : first + own_rows]
            first += own_rows
        proj, grads = proj_ref[...], grad_ref[...]
    length, width = proj.shape[0], wall_ref.shape[0]
    chunks = length // BLOCK
    flip = mirror(BLOCK)
    bias, rate, skip = par_refs[0][0], decay_rate(par_refs), par_refs[2][0]
    lane = iota((1, LANES), 1)
    low = lane < LANES // 2
    causal = iota((BLOCK, BLOCK), 0) >= iota((BLOCK, BLOCK), 1)
    tri = jnp.where(causal, 1.0, 0.0).astype(bf16)
    row_at = iota((length, LANES), 0)

    turned = [proj[:, 2 * LANES : 3 * LANES].astype(bf16)]
    turned += split(proj[:, 3 * LANES :], 2) + split(grads[:, LANES:], 2)
    turned = flip_rows(jnp.concatenate(turned, axis=1), flip)
    turned = [turned[:, i * LANES : (i + 1) * LANES] for i in range(5)]
    strands = (
        (
            proj[:, :LANES].astype(bf16).astype(f32),
            proj[:, LANES : 2 * LANES],
            grads[:, :LANES],
        ),
        (turned[0], turned[1] + turned[2], turned[3] + turned[4]),
    )

    def gates(xz, rest, grad_g):
        pre = taps_ref[CONV - 1 : CONV, :] * xz
        for shift in range(1, CONV):
            moved = jnp.where(row_at >= shift, pltpu.roll(xz, shift, 0), 0.0)
            pre += taps_ref[CONV - 1 - shift : CONV - shift, :] * moved
        sig = jax.nn.sigmoid(pre)
        u = pre * sig
        slope = sig * (1.0 + pre * (1.0 - sig))
        u_other = pltpu.roll(u, LANES // 2, 1)
        raw = jnp.broadcast_to(rest[:, 2 * STATE : 2 * STATE + 1], (length, LANES)) + bias
        dt = jnp.maximum(raw, 0.0) + jnp.log1p(jnp.exp(-jnp.abs(raw)))
        b_all = jnp.where(lane < STATE, rest, 0.0)
        c_all = jnp.where(lane < STATE, pltpu.roll(rest, LANES - STATE, 1), 0.0)
        g_y = jnp.where(low, grad_g * u_other, 0.0)
        return u, slope, u_other, dt, jax.nn.sigmoid(raw), b_all, c_all, dt * u, g_y, grad_g

    def enter_chunk(c, gate, state):
        rows = slice(c * BLOCK, (c + 1) * BLOCK)
        dt, b_all, c_all, w_all = gate[3][rows], gate[5][rows], gate[6][rows], gate[7][rows]
        log_keep = dot(tri, jnp.concatenate(split(dt * rate, 2), axis=1))
        log_keep = log_keep[:, :LANES] + log_keep[:, LANES:]
        across = jnp.transpose(log_keep)[0:1, :]
        gap = jnp.concatenate([log_keep] * (BLOCK // LANES), axis=1) - across
        decay = jnp.exp(jnp.where(causal, gap, -jnp.inf))
        b_low, c_low, w_low = b_all.astype(bf16), c_all.astype(bf16), w_all.astype(bf16)
        mixed = (dot_nt(c_low, b_low) * decay).astype(bf16)
        last = log_keep[BLOCK - 1 : BLOCK, :]
        enter = jnp.exp(log_keep)
        leave = jnp.exp(last - log_keep)
        b_left = (leave * b_all).astype(bf16)
        out = dot(mixed, w_low) + enter * dot(c_low, state.astype(bf16))
        after = jnp.exp(last) * state + dot_tn(b_left, w_low)
        return out, decay, mixed, b_low, c_low, w_low, b_left, enter, leave, last, state, after

    def leave_chunk(c, gate, saved, d_state):
        rows = slice(c * BLOCK, (c + 1) * BLOCK)
        u, c_all, w_all, gy = gate[0][rows], gate[6][rows], gate[7][rows], gate[8][rows]
        out, decay, mixed, b_low, c_low, w_low, b_left, enter, leave, last, before, after = saved
        gy_low = gy.astype(bf16)
        ds_low = d_state.astype(bf16)
        dw = dot_tn(mixed, gy_low) + dot(b_left, ds_low)
        d_scores = (dot_nt(gy_low, w_low) * decay).astype(bf16)
        g_c = dot(d_scores, b_low) + enter * dot_nt(gy_low, before.astype(bf16))
        g_b = dot_tn(d_scores, c_low) + leave * dot_nt(w_low, ds_low)
        d_log = jnp.sum(jnp.where(low, gy * out - w_all * dw, 0.0), axis=1, keepdims=True)
        at_end = jnp.sum(jnp.where(low, after * d_state, 0.0))
        d_log = jnp.broadcast_to(d_log, (BLOCK, LANES))
        d_sum = dot_tn(tri, jnp.concatenate(split(d_log, 2), axis=1))
        d_sum = d_sum[:, :LANES] + d_sum[:, LANES:] + at_end
        g_a = rate * d_sum + jnp.sum(jnp.where(low, u * dw, 0.0), axis=1, keepdims=True)
        carried = (enter * c_all).astype(bf16)
        return dw, g_b, g_c, g_a, jnp.exp(last) * d_state + dot_tn(carried, gy_low)

    gate = [gates(*strand) for strand in strands]
    saved = [[], []]
    state = [jnp.zeros((LANES, LANES), f32)] * 2
    for c in range(chunks):
        for s in range(2):
            saved[s].append(enter_chunk(c, gate[s], state[s]))
            state[s] = saved[s][c][-1]
    state = [jnp.zeros((LANES, LANES), f32)] * 2
    grads = [[None] * chunks, [None] * chunks]
    for c in reversed(range(chunks)):
        for s in range(2):
            *grads[s][c], state[s] = leave_chunk(c, gate[s], saved[s][c], state[s])
    small = []
    for s in range(2):
        u, slope, u_other, dt, dt_slope, _, _, _, g_y, grad_g = gate[s]
        y = jnp.concatenate([part[0] for part in saved[s]], axis=0) + skip * u
        gated = jnp.where(low, y * u_other, 0.0).astype(bf16)
        g_gate = jnp.where(low, grad_g * y, 0.0)
        d_w, g_b, g_c, g_a = (
            jnp.concatenate([part[i] for part in grads[s]], axis=0) for i in range(4)
        )
        g_raw = g_a * dt_slope
        d_u = jnp.where(low, skip * g_y + dt * d_w, pltpu.roll(g_gate, LANES // 2, 1))
        d_pre = d_u * slope
        g_xz = taps_ref[CONV - 1 : CONV, :] * d_pre
        for shift in range(1, CONV):
            moved = jnp.where(
                row_at < length - shift, pltpu.roll(d_pre, length - shift, 0), 0.0
            )
            g_xz += taps_ref[CONV - 1 - shift : CONV - shift, :] * moved
        shared = jnp.where(lane < STATE, g_b, 0.0) + jnp.where(
            (lane >= STATE) & (lane < 2 * STATE), pltpu.roll(g_c, STATE, 1), 0.0
        )
        g_rest = shared + jnp.where(lane == 2 * STATE, g_raw, 0.0)
        result = jnp.concatenate([g_xz.astype(bf16), g_rest.astype(bf16), gated], axis=1)
        small.append(shared)
        if s == 1:
            result = flip_rows(result, flip).astype(bf16)
        gcat_ref[:, 2 * s * LANES : 2 * (s + 1) * LANES] = result[:, : 2 * LANES]
        gated_ref[:, s * LANES : (s + 1) * LANES] = result[:, 2 * LANES :]

    pair = small[0] + pltpu.roll(small[1], 2 * STATE, 1)
    shared_t = jnp.transpose(pair)[: 4 * STATE].astype(bf16)
    groups = width // length
    step = 4 * STATE // groups
    for i in range(groups):
        part = shared_t[i * step : (i + 1) * step, :]
        send_ref[0:step, i * length : (i + 1) * length] = part
        keep_ref[0:step, i * length : (i + 1) * length] = part.astype(f32)
    own = tp_size * own_rows
    source = own_source((own, length), 0, ids_ref, tp_size, own_rows)
    pick = jnp.where(source == iota((own, length), 1), 1.0, 0.0).astype(bf16)
    picked = dot(pick, gcat_ref[...]).astype(bf16)
    half = own // 2
    part = dot(picked, wallt_ref[...])
    send_ref[step:, :] = part[:half].astype(bf16)
    keep_ref[step:, :] = part[half:]


def weight_kernel(n_pieces, layout, scaling, *refs):
    ids_ref = refs[0]
    pieces = refs[1 : 1 + n_pieces]
    gcat_ref, gated_ref, _, dwin_ref, dwout_ref, mark_ref = refs[1 + n_pieces : 7 + n_pieces]
    mark_ref[...] = jnp.zeros_like(mark_ref)
    if layout[2] is None:
        h_ref, d_ref = pieces
    else:
        h_ref, d_ref = refs[7 + n_pieces :]
        assemble(ids_ref, pieces, h_ref, d_ref, layout)
    flip = mirror(BLOCK)
    columns = h_ref.shape[1] // BLOCK
    head = dwout_ref.shape[0]
    g_f = gcat_ref[:, 0:LANES]
    g_r = gcat_ref[:, 2 * LANES : 3 * LANES]
    y_f = gated_ref[:, 0:LANES]
    y_r = gated_ref[:, LANES:]
    for i in range(columns):
        cols = slice(i * BLOCK, (i + 1) * BLOCK)
        back = slice((columns - 1 - i) * BLOCK, (columns - i) * BLOCK)
        turned = dot(h_ref[:, back], flip).astype(bf16)
        grad = dot_tn(g_f, h_ref[:, cols]) + dot_tn(g_r, turned)
        dwin_ref[cols, :] = jnp.transpose(grad * scaling)
        turned = dot(d_ref[:, back], flip).astype(bf16)
        grad = dot_tn(y_f, d_ref[:, cols]) + dot_tn(y_r, turned)
        dwout_ref[:, cols] = grad[:head] * scaling


def add_kernel(a_ref, b_ref, _, out_ref):
    rows = slice(0, out_ref.shape[0])
    out_ref[...] = (a_ref[rows, :].astype(f32) + b_ref[rows, :].astype(f32)).astype(bf16)


def stage_kernel(own_rows, keep_ref, got_ref, own_ref, *piece_refs):
    for j, ref in enumerate([own_ref, *piece_refs]):
        rows = slice(j * own_rows, (j + 1) * own_rows)
        value = keep_ref[rows, :] + got_ref[rows, :].astype(f32)
        ref[...] = value.astype(ref.dtype)


def last_kernel(scaling, own_ref, h_ref, shared_ref, other_ref, *refs):
    got_refs, (dhid_ref, dwbct_ref) = refs[:-2], refs[-2:]
    flip = mirror(BLOCK)
    length, width = h_ref.shape
    groups = width // length
    total = own_ref[...]
    for got in got_refs:
        total += got[...].astype(f32)
    dhid_ref[...] = total.astype(bf16)
    shared = (shared_ref[...].astype(f32) + other_ref[...].astype(f32)).astype(bf16)
    shared = jnp.concatenate(
        [shared[:, i * length : (i + 1) * length] for i in range(groups)], axis=0
    )
    fwd = shared[: 2 * STATE]
    rev = turn_columns(shared[2 * STATE :], flip).astype(bf16)
    pairs = dot(jnp.concatenate([fwd, rev], axis=0), h_ref[...])
    turned = exact(split(pairs[2 * STATE :], 2), lambda part: turn_columns(part, flip))
    dwbct_ref[...] = (pairs[: 2 * STATE] + turned) * scaling


def spec(memory=pltpu.VMEM):
    return pl.BlockSpec(memory_space=memory)


def call(kernel, inputs, n_smem, outs, scratch, flops, moved, unread=0, vmem=32):
    return pl.pallas_call(
        kernel,
        out_shape=outs,
        in_specs=[spec(pltpu.SMEM)] * n_smem
        + [spec()] * (len(inputs) - n_smem - unread)
        + [spec(pl.ANY)] * unread,
        out_specs=jax.tree.map(lambda _: spec(), outs),
        scratch_shapes=scratch,
        compiler_params=pltpu.CompilerParams(vmem_limit_bytes=vmem * 1024 * 1024),
        cost_estimate=pl.CostEstimate(flops=flops, bytes_accessed=moved, transcendentals=0),
    )(*inputs)


def shape(dims, dtype):
    return jax.ShapeDtypeStruct(dims, dtype)


def local(ctx_size, tp_size, hidden, w_in, w_bc, w_dt, dt_bias, a_log, d_skip, conv_w, w_out, d_out):
    own_rows, width = hidden.shape
    length = own_rows * tp_size * ctx_size
    head = w_out.shape[0]
    nz = tp_size // 4
    chunks = length // BLOCK
    t = lax.axis_index("tp")
    ids = jnp.stack([t >> 2, (t >> 1) & 1, t & 1, lax.axis_index("ctx")]).astype(jnp.int32)
    params = [dt_bias, a_log, d_skip]
    def across(value, flip_bits):
        return lax.ppermute(value, "tp", [(i, i ^ flip_bits) for i in range(tp_size)])

    def along(value):
        return lax.ppermute(value, "ctx", [(0, 1), (1, 0)])

    def prepare(*begun):
        return call(
            prep_kernel,
            [ids, w_in, w_bc.T, w_dt, w_out, conv_w, *begun],
            1,
            (
                shape((width, 4 * LANES), bf16),
                shape((4 * LANES, width), bf16),
                shape((width, 2 * LANES), bf16),
                shape((CONV, LANES), f32),
            ),
            [],
            6 * width * BLOCK * BLOCK,
            20 * width * LANES,
            len(begun),
        )

    def pack(parts, *first):
        rows = sum(part.shape[0] for part in parts)
        return call(
            functools.partial(pack_kernel, len(parts), own_rows),
            [*parts, *first],
            0,
            shape((rows, width), bf16),
            [],
            0,
            4 * rows * width,
            len(first),
        )

    def after(value, *first):
        return call(
            copy_kernel,
            [value, *first],
            0,
            shape(value.shape, bf16),
            [],
            0,
            4 * value.size,
            len(first),
        )

    if own_rows % TILE_ROWS == 0 and (ctx_size, nz) == (2, 4):
        low = jnp.array(-jnp.inf, bf16)
        own = jnp.maximum(
            lax.pad(hidden, low, [(0, own_rows, 0), (0, 0, 0)]),
            lax.pad(d_out, low, [(own_rows, 0, 0), (0, 0, 0)]),
        )
        z_near, z_far = across(own, 4), across(own, 8)
        chunk_a = pack([own, z_near])
        chunk_b = pack([z_far, across(z_far, 4)])
        direct = [[part, across(part, 2), along(part)] for part in (chunk_a, chunk_b)]
        (_, a_x, a_c), (_, b_x, b_c) = direct
        beside_a = [across(part, 1) for part in direct[0]]
        wall, wallt, gall, taps = prepare(chunk_b)
        a_d = across(after(a_c, a_x, b_x, b_c, *beside_a), 2)
        b_d = along(after(b_x, a_x, a_c, b_c, *beside_a))
        beside = [beside_a, [across(part, 1) for part in direct[1]]]
        early, coords = [], []
        blocks = ((0, 1), (2, 3))
        for g in range(2):
            for place, part, other in zip(((0, 0), (0, 1), (1, 0)), direct[g], beside[g]):
                early += [part, other]
                coords += [(*place, 0, blocks[g]), (*place, 1, blocks[g])]
        coords += [(1, 1, core, blocks[g]) for g in range(2) for core in range(2)]
        layout = (tp_size, own_rows, tuple(coords), len(early))
        late, pieces = None, None
    else:
        pieces = [lax.all_gather(a, ("ctx", "tp"), axis=0, tiled=True) for a in (hidden, d_out)]
        layout = (tp_size, own_rows, None, 0)
        wall, wallt, gall, taps = prepare()
        early, late = [jnp.concatenate(pieces, axis=0)], []
    ordered = layout[2] is None
    vmem = 60 if ordered else 32
    early_rows = sum(piece.shape[0] for piece in early) // 2
    projected = call(
        early_kernel,
        [*early, wall, gall],
        0,
        (shape((early_rows, 4 * LANES), f32), shape((early_rows, 2 * LANES), f32)),
        [],
        2 * early_rows * width * 6 * LANES,
        4 * early_rows * width,
        vmem=vmem,
    )
    if not ordered:
        a_other = across(after(a_d, projected[0]), 1)
        b_other = across(after(b_d, projected[0]), 1)
        late = [a_d, a_other, b_d, b_other]
        pieces = early + late
    extra = 4 * STATE * length // width
    half = tp_size * own_rows // 2
    send, keep, gcat, gated = call(
        functools.partial(core_kernel, len(late), layout),
        [ids, *params, *late, *projected, wall, wallt, gall, taps],
        4,
        (
            shape((extra + half, width), bf16),
            shape((extra + half, width), f32),
            shape((length, 4 * LANES), bf16),
            shape((length, 2 * LANES), bf16),
        ),
        []
        if ordered
        else [pltpu.VMEM((length, 4 * LANES), f32), pltpu.VMEM((length, 2 * LANES), f32)],
        8 * length * width * BLOCK,
        8 * length * width,
        vmem=vmem,
    )
    scaling = 1.0 / math.sqrt(length)
    got = across(send, 1)
    quarter = half // 2
    at = extra + quarter
    given, own_given = got, keep
    send = (keep[extra:at] + got[extra:at].astype(f32)).astype(bf16)
    keep = keep[at:] + got[at:].astype(f32)
    sent = send
    got = across(send, 2)

    def add_shared(a, b, *first):
        return call(
            add_kernel,
            [a, b, *first],
            0,
            shape((extra, width), bf16),
            [],
            extra * width,
            6 * extra * width,
            1,
        )

    outs = (shape((width, LANES), f32), shape((head, width), f32), shape((8, LANES), f32))
    if not ordered:
        outs += (shape((length, width), bf16),)
    d_w_in, d_w_out, mark, *in_order = call(
        functools.partial(weight_kernel, len(pieces), layout, scaling),
        [ids, *pieces, gcat, gated, send],
        1,
        outs,
        [] if ordered else [pltpu.VMEM((length, width), bf16)],
        8 * length * width * BLOCK,
        8 * length * width,
        1,
        vmem=vmem,
    )
    in_order = in_order[0] if in_order else pieces[0]
    own, *send = call(
        functools.partial(stage_kernel, own_rows),
        [keep, got],
        0,
        (shape((own_rows, width), f32),) + (shape((own_rows, width), bf16),) * (nz - 1),
        [],
        4 * quarter * width,
        10 * quarter * width,
    )
    shared = add_shared(own_given, given, sent)
    step = nz // 2
    while step:
        shared = add_shared(shared, across(shared, 4 * step), mark if step > 1 else own)
        step //= 2
    got = [across(piece, 4 * (j + 1)) for j, piece in enumerate(send)]
    d_hidden, d_w_bc = call(
        functools.partial(last_kernel, scaling),
        [own, in_order, shared, across(shared, 2), *got],
        0,
        (shape((own_rows, width), bf16), shape((2 * STATE, width), f32)),
        [],
        2 * length * width * LANES,
        4 * length * width,
    )
    return (d_hidden, d_w_in, d_w_out, d_w_bc.T)


def solution(mesh):
    in_specs = (
        P(("ctx", "tp"), None),
        P(None, "tp"),
        P(),
        P("tp", None),
        P("tp"),
        P("tp"),
        P("tp"),
        P(None, "tp"),
        P("tp", None),
        P(("ctx", "tp"), None),
    )
    out_specs = (P(("ctx", "tp"), None), P(None, "tp"), P("tp", None), P())
    body = functools.partial(local, mesh.shape["ctx"], mesh.shape["tp"])
    return jax.shard_map(body, mesh=mesh, in_specs=in_specs, out_specs=out_specs, check_vma=False)
```
